128 devices in a mesh: dp: 16 (over x, z), seq: 8 (over y, core).
Axes of the slice: x: 4, y: 4, z: 4, core: 2. Of those that a mesh axis runs over, the one named last changes fastest.
Arguments:
- queries: bfloat16 [16, 8, 256, 1536], P('dp', 'seq'), may hold values from -6 to 6
- keys_proj: bfloat16 [16, 8, 256, 1536], P('dp', 'seq'), may hold values from -6 to 6
- values_proj: bfloat16 [16, 8, 256, 1536], P('dp', 'seq'), may hold values from -6 to 6
- gain_query: float32 [64], replicated, may hold values from 0.5 to 6
- gain_key: float32 [64], replicated, may hold values from 0.5 to 6
- frame_counts: int32 [16], P('dp'), may hold values from 4 to 8, as said below
- heights: int32 [16], P('dp'), may hold values from 8 to 16, as said below
- widths: int32 [16], P('dp'), may hold values from 8 to 16, as said below
- out_weight: bfloat16 [1536, 3072], replicated, may hold values from -0.15625 to 0.15625
- cotangent: bfloat16 [16, 8, 256, 3072], P('dp', 'seq'), may hold values from -6 to 6
Outputs:
- block_out: bfloat16 [16, 8, 256, 3072], P('dp', 'seq')
- grad_queries: bfloat16 [16, 8, 256, 1536], P('dp', 'seq')
- grad_keys: bfloat16 [16, 8, 256, 1536], P('dp', 'seq')
- grad_values: bfloat16 [16, 8, 256, 1536], P('dp', 'seq')
- grad_weight: float32 [1536, 3072], P(('dp', 'seq'))
- grad_gain_query: float32 [64], replicated
- grad_gain_key: float32 [64], replicated
The draws below stay inside these ranges and needn't reach their ends.
Inputs may be any that keep to these rules, and one draw needn't show every extreme that they name: `frame_counts`: some clip has exactly 8 frames. `heights`: some clip has exactly 16 patch rows. `widths`: some clip has exactly 16 patch columns.
All inputs are finite; a program needn't handle non-finite values.
Results may differ from the reference program's by a relative error of at most 0.015.
The reference program's roundings to bfloat16 on the way count: a program that leaves them out, or rounds other values in their place, can miss the bound.
Values may be sent and summed in bfloat16 or wider, within the bound.
No kernel may reach another device: no remote copies, remote signals or barrier semaphores. Data moves between devices by JAX's collectives and lax.ppermute only.
A program may use at most 192 MiB of HBM per device.

```python
import jax
import jax.numpy as jnp
from jax import lax

D = 3072
HEADS = 24
HD = 64
INNER = 1536
PH = 16
PW = 16
SPATIAL = 256
FRAMES = 8
CLIPS = 16


def shared_keys(key):
    drawn = jax.random.normal(jax.random.fold_in(key, 77), (CLIPS, FRAMES, SPATIAL, HEADS * HD), jnp.float32)
    return jnp.clip(drawn, -6.0, 6.0)


def draw_keys_proj(key, part):
    shared = shared_keys(key)
    return shared.astype(jnp.bfloat16)


def draw_queries(key, part):
    shared = shared_keys(key)
    key = jax.random.fold_in(key, 1)
    first = jax.random.fold_in(key, 0)
    fresh = jnp.clip(jax.random.normal(first, shared.shape, jnp.float32), -6.0, 6.0)
    return fresh.astype(jnp.bfloat16)


def gain_between(key, lower, upper):
    return jnp.exp(jax.random.uniform(key, (HD,), jnp.float32, jnp.log(lower), jnp.log(upper)))


def draw_gain_query(key, part):
    key = jax.random.fold_in(key, 3)
    return gain_between(key, 0.5, 2.0)


def draw_gain_key(key, part):
    key = jax.random.fold_in(key, 4)
    return gain_between(key, 0.5, 2.0)


def bounded_counts(key, upper):
    first, second = jax.random.split(key)
    lowest = max(upper // 2, 1)
    counts = jax.random.randint(first, (CLIPS,), lowest, upper + 1)
    chosen = jax.random.randint(second, (), 0, CLIPS)
    return counts.at[chosen].set(upper)


def draw_frame_counts(key, part):
    key = jax.random.fold_in(key, 5)
    return bounded_counts(key, FRAMES)


def draw_heights(key, part):
    key = jax.random.fold_in(key, 6)
    return bounded_counts(key, PH)


def draw_widths(key, part):
    key = jax.random.fold_in(key, 7)
    return bounded_counts(key, PW)


def block_levels(own_key, extent, shards, least, largest):
    def one(dim, shards_of):
        draws = jax.random.uniform(jax.random.fold_in(jax.random.fold_in(own_key, 6), dim), (shards_of,), jnp.float32, least / len(shards), largest / len(shards))
        return jnp.repeat(jnp.exp(draws), extent[dim] // shards_of).reshape((-1,) + (1,) * (len(extent) - dim - 1))

    factor_of = one(*shards[0])
    for cut in shards[1:]:
        factor_of = factor_of * one(*cut)
    return factor_of


def gaussian(own_key, shape, spread, limit, cuts=(), held_as=jnp.bfloat16):
    values = jax.random.normal(own_key, shape, jnp.float32) * spread
    if len(cuts) > 0:
        values = block_levels(own_key, shape, cuts, -0.22, 0.18) * values
    return jnp.clip(values, min=-limit, max=limit).astype(held_as)


def setup_inputs(seed: int = 0) -> dict:
    streams_of = jax.random.split(jax.random.key(seed), 11)
    queries = draw_queries(jax.random.fold_in(streams_of[10], 71), 0)
    keys_proj = draw_keys_proj(jax.random.fold_in(streams_of[10], 71), 0)
    values_proj = gaussian(streams_of[2], (CLIPS, FRAMES, SPATIAL, INNER), 1.0, 6.0, ((0, 16), (1, 8)))
    gain_query = draw_gain_query(jax.random.fold_in(streams_of[10], 71), 0)
    gain_key = draw_gain_key(jax.random.fold_in(streams_of[10], 71), 0)
    frame_counts = draw_frame_counts(jax.random.fold_in(streams_of[10], 71), 0)
    heights = draw_heights(jax.random.fold_in(streams_of[10], 71), 0)
    widths = draw_widths(jax.random.fold_in(streams_of[10], 71), 0)
    out_weight = gaussian(streams_of[8], (INNER, D), INNER ** -0.5, 0.15625)
    cotangent = gaussian(streams_of[9], (CLIPS, FRAMES, SPATIAL, D), 1.0, 6.0, ((0, 16), (1, 8)))
    return dict(queries=queries, keys_proj=keys_proj, values_proj=values_proj, gain_query=gain_query, gain_key=gain_key, frame_counts=frame_counts, heights=heights, widths=widths, out_weight=out_weight, cotangent=cotangent)


def product(form, left, right):
    return jnp.einsum(form, left.astype(jnp.float32), right.astype(jnp.float32))

def split_heads(tensor):
    return tensor.reshape(tensor.shape[:-1] + (tensor.shape[-1] // HD, HD))

def layer_norm(tensor, gain):
    rows = split_heads(tensor.astype(jnp.float32))
    centre = rows - lax.optimization_barrier(jnp.mean(rows, -1, keepdims=True))
    inverse = lax.rsqrt(lax.optimization_barrier(jnp.mean(centre * centre, -1, keepdims=True)) + 1e-06)
    normed = centre * inverse
    return ((normed * gain).reshape(tensor.shape).astype(jnp.bfloat16), normed, inverse)

def norm_back(upstream, normed, inverse, gain):
    upstream_heads = upstream.reshape(normed.shape)
    scaled = upstream_heads * gain
    dinput = inverse * (scaled - lax.optimization_barrier(jnp.mean(scaled, -1, keepdims=True)) - normed * lax.optimization_barrier(jnp.mean(scaled * normed, -1, keepdims=True)))
    gain_grad = lax.optimization_barrier(jnp.sum((upstream_heads * normed).reshape(-1, HD), 0))
    return (dinput.reshape(upstream.shape).astype(jnp.bfloat16), gain_grad)

def probabilities(query, key_rows, key_ok):
    scores = product('bqhd,bkhd->bhqk', split_heads(query), split_heads(key_rows)) * HD ** (-0.5)
    scores = jnp.where(key_ok[:, None, None, :] > 0, scores, -1e+30)
    expo = jnp.exp(scores - lax.optimization_barrier(jnp.max(scores, -1, keepdims=True)))
    return expo / lax.optimization_barrier(jnp.sum(expo, -1, keepdims=True))

def attend(query, key_rows, value_rows, key_ok, query_ok):
    weights = probabilities(query, key_rows, key_ok).astype(jnp.bfloat16)
    result = product('bhqk,bkhd->bqhd', weights, split_heads(value_rows)) * query_ok[:, :, None, None]
    return result.reshape(value_rows.shape).astype(jnp.bfloat16)

def attend_back(query, key_rows, value_rows, key_ok, query_ok, upstream):
    chances = probabilities(query, key_rows, key_ok)
    weights = chances.astype(jnp.bfloat16)
    masked = jnp.where(query_ok[:, :, None, None] > 0, split_heads(upstream), 0).astype(upstream.dtype)
    dvalues = product('bhqk,bqhd->bkhd', weights, masked)
    dchances = product('bqhd,bkhd->bhqk', masked, split_heads(value_rows))
    dscores = (chances * (dchances - lax.optimization_barrier(jnp.sum(chances * dchances, -1, keepdims=True))) * HD ** (-0.5)).astype(jnp.bfloat16)
    dquery = product('bhqk,bkhd->bqhd', dscores, split_heads(key_rows))
    dkeys = product('bhqk,bqhd->bkhd', dscores, split_heads(query))
    layout = value_rows.shape
    return (dquery.reshape(layout), dkeys.reshape(layout), dvalues.reshape(layout))

def flip_axes(tensor):
    return jnp.swapaxes(tensor, 0, 1)

def one_clip(queries, keys_proj, values_proj, cotangent, frame_total, height, width_now, gain_query, gain_key, out_weight):
    frame_ids = jnp.arange(queries.shape[0])[:, None]
    cell_ids = jnp.arange(queries.shape[1])[None, :]
    usable = ((frame_ids < frame_total) & (cell_ids // PW < height) & (cell_ids % PW < width_now)).astype(jnp.float32)
    query_norm, query_hat, query_inv = layer_norm(queries, gain_query)
    key_norm, key_hat, key_inv = layer_norm(keys_proj, gain_key)
    spatial = attend(query_norm, key_norm, values_proj, usable, usable)
    mixed = flip_axes(attend(flip_axes(query_norm), flip_axes(key_norm), flip_axes(spatial), usable.T, usable.T))
    mixed_rows = mixed.reshape(-1, mixed.shape[-1])
    grad_rows = cotangent.reshape(-1, cotangent.shape[-1])
    block_out = jnp.dot(mixed_rows, out_weight, preferred_element_type=jnp.float32).astype(jnp.bfloat16).reshape(cotangent.shape)
    grad_mixed = jnp.dot(grad_rows, out_weight.T, preferred_element_type=jnp.float32).astype(jnp.bfloat16).reshape(mixed.shape)
    weight_part = jnp.dot(mixed_rows.T, grad_rows, preferred_element_type=jnp.float32)
    dq_time, dk_time, dspatial = attend_back(flip_axes(query_norm), flip_axes(key_norm), flip_axes(spatial), usable.T, usable.T, flip_axes(grad_mixed))
    dq_time = flip_axes(dq_time).astype(jnp.bfloat16)
    dk_time = flip_axes(dk_time).astype(jnp.bfloat16)
    dspatial = flip_axes(dspatial).astype(jnp.bfloat16)
    dq_space, dk_space, dvalues = attend_back(query_norm, key_norm, values_proj, usable, usable, dspatial)
    grad_queries, gain_q_part = norm_back(dq_space + dq_time.astype(jnp.float32), query_hat, query_inv, gain_query)
    grad_keys, gain_k_part = norm_back(dk_space + dk_time.astype(jnp.float32), key_hat, key_inv, gain_key)
    return (block_out, grad_queries, grad_keys, dvalues.astype(jnp.bfloat16), weight_part, gain_q_part, gain_k_part)

def reference(queries, keys_proj, values_proj, gain_query, gain_key, frame_counts, heights, widths, out_weight, cotangent):

    def step(carry, items):
        outs = one_clip(*items, gain_query, gain_key, out_weight)
        return ((carry[0] + outs[4], carry[1] + outs[5], carry[2] + outs[6]), outs[:4])
    start = (jnp.zeros((INNER, D), jnp.float32), jnp.zeros((HD,), jnp.float32), jnp.zeros((HD,), jnp.float32))
    totals, stacked = lax.scan(step, start, (queries, keys_proj, values_proj, cotangent, frame_counts, heights, widths))
    return (stacked[0], stacked[1], stacked[2], stacked[3], totals[0], totals[1], totals[2])
```

```python
import jax
import jax.numpy as jnp
import numpy as np
from jax import lax
from jax.experimental import pallas as pl
from jax.experimental.pallas import tpu as pltpu
from jax.sharding import Mesh
from jax.sharding import PartitionSpec as P

BF = jnp.bfloat16
F32 = jnp.float32
HD = 64
PW = 16
CELLS = 256
FRAMES = 8
LANES = 128
WIDE = 384
PAIRS = WIDE // LANES
CELLS_HERE = CELLS // FRAMES
BLOCK = 16
NEG = -1e30
SCALE = HD**-0.5
PARAMS = pltpu.CompilerParams(vmem_limit_bytes=56 * 1024 * 1024)


def cost(microseconds):
    return pl.CostEstimate(flops=0, bytes_accessed=int(microseconds * 3.69e6), transcendentals=0)


SMEM = pl.BlockSpec(memory_space=pltpu.SMEM)
VMEM = pl.BlockSpec(memory_space=pltpu.VMEM)


def nn(left, right):
    return jnp.dot(left, right, preferred_element_type=F32)


def nt(left, right):
    return lax.dot_general(left, right, (((1,), (1,)), ((), ())), preferred_element_type=F32)


def tn(left, right):
    return lax.dot_general(left, right, (((0,), (0,)), ((), ())), preferred_element_type=F32)


def low_lanes(shape):
    return lax.broadcasted_iota(jnp.int32, shape, len(shape) - 1) < HD


def stack_heads(pair):
    low = low_lanes((1, LANES)).astype(F32)
    return jnp.concatenate([pair * low.astype(BF), pair * (1.0 - low).astype(BF)], 0)


def pick_heads(stacked):
    half = stacked.shape[0] // 2
    return jnp.where(low_lanes((half, LANES)), stacked[:half], stacked[half:])


def softmax_rows(scores):
    grouped = scores.reshape(2, scores.shape[0] // 2, scores.shape[1])
    expo = jnp.exp(grouped - jnp.max(grouped, 1, keepdims=True))
    return expo * (1.0 / jnp.sum(expo, 1, keepdims=True))


def score_back(chances, dchances):
    grouped = dchances.reshape(chances.shape)
    total = jnp.sum(chances * grouped, 1, keepdims=True)
    return (chances * (grouped - total)).astype(BF).reshape(dchances.shape)


def cell_ok(cells, height, width):
    row = lax.shift_right_logical(cells, 4)
    return (row < height) & ((cells & (PW - 1)) < width)


def head_ones(rows, columns):
    row = lax.broadcasted_iota(jnp.int32, (rows, columns), 0) & (columns - 1)
    column = lax.broadcasted_iota(jnp.int32, (rows, columns), 1)
    same = lax.shift_right_logical(row, 6) == lax.shift_right_logical(column, 6)
    return jnp.where(same, 1.0, 0.0).astype(BF)


def head_mean(tensor, twice):
    high = tensor.astype(BF)
    rest = (tensor - high.astype(F32)).astype(BF)
    return nn(jnp.concatenate([high, rest], 1), twice) * (1.0 / HD)


def hat_of(raw, ones, twice):
    centre = raw.astype(F32) - nn(raw, ones) * (1.0 / HD)
    hats, inverses = [], []
    for left in range(0, raw.shape[1], LANES):
        part = centre[:, left : left + LANES]
        inverse = lax.rsqrt(head_mean(part * part, twice) + 1e-06)
        hats.append(part * inverse)
        inverses.append(inverse)
    return hats, inverses


def pair_slice(number):
    return slice(number * LANES, (number + 1) * LANES)


NORM_WIDE = 512
DUO = 2 * LANES


def both_heads(gain_ref):
    return jnp.concatenate([gain_ref[...], gain_ref[...]], 1)


def norm_kernel(q_ref, k_ref, gain_q_ref, gain_k_ref, out_ref):
    ones, twice = head_ones(DUO, DUO), head_ones(DUO, LANES)
    gains = both_heads(gain_q_ref), both_heads(gain_k_ref)
    for left in range(0, NORM_WIDE, DUO):
        for number, source in enumerate((q_ref, k_ref)):
            hats, _ = hat_of(source[:, left : left + DUO], ones, twice)
            for pair, hat in enumerate(hats):
                normed = (hat * gains[number]).astype(BF)
                if number == 0:
                    normed = normed * jnp.asarray(SCALE, BF)
                at = slice(left + pair * LANES, left + (pair + 1) * LANES)
                out_ref[:, number, :, at] = normed.reshape(FRAMES, CELLS_HERE, LANES)


def norm(queries, keys, gain_query, gain_key):
    inner = queries.shape[1]
    tokens = pl.BlockSpec((CELLS, NORM_WIDE), lambda n: (0, n))
    gain = pl.BlockSpec((1, HD), lambda n: (0, 0))
    return pl.pallas_call(
        norm_kernel,
        grid=(inner // NORM_WIDE,),
        in_specs=[tokens, tokens, gain, gain],
        out_specs=pl.BlockSpec((FRAMES, 2, CELLS_HERE, NORM_WIDE), lambda n: (0, 0, 0, n)),
        out_shape=jax.ShapeDtypeStruct((FRAMES, 2, CELLS_HERE, inner), BF),
        compiler_params=PARAMS,
        cost_estimate=cost(5),
        name="norm",
    )(queries, keys, gain_query, gain_key)


def hats_kernel(q_ref, k_ref, *out_refs):
    ones, twice = head_ones(DUO, DUO), head_ones(DUO, LANES)
    for left in range(0, NORM_WIDE, DUO):
        for number, source in enumerate((q_ref, k_ref)):
            hats, inverses = hat_of(source[:, left : left + DUO], ones, twice)
            at = slice(left, left + DUO)
            out_refs[number][:, at] = jnp.concatenate(hats, 1)
            out_refs[2 + number][:, at] = jnp.concatenate(inverses, 1)


def hats_of(queries, keys):
    inner = queries.shape[1]
    tokens = pl.BlockSpec((CELLS, NORM_WIDE), lambda n: (0, n))
    return pl.pallas_call(
        hats_kernel,
        grid=(inner // NORM_WIDE,),
        in_specs=[tokens, tokens],
        out_specs=[tokens] * 4,
        out_shape=[jax.ShapeDtypeStruct((CELLS, inner), F32)] * 4,
        compiler_params=PARAMS,
        cost_estimate=cost(5.6),
        name="hats",
    )(queries, keys)


def space_kernel(counts_ref, qk_ref, v_ref, gm_ref, out_ref, chances_ref):
    height, width = counts_ref[1], counts_ref[2]
    frame_on = jnp.where(counts_ref[3] < counts_ref[0], 1.0, 0.0)
    key_cell = lax.broadcasted_iota(jnp.int32, (2 * CELLS, CELLS), 0) & (CELLS - 1)
    bias = jnp.where(cell_ok(key_cell, height, width), 0.0, NEG)
    cell = lax.broadcasted_iota(jnp.int32, (CELLS, LANES), 0)
    usable = cell_ok(cell, height, width).astype(F32) * frame_on
    scores = []
    for pair in range(PAIRS):
        query = qk_ref[:, 0, :, pair_slice(pair)].reshape(CELLS, LANES)
        key = qk_ref[:, 1, :, pair_slice(pair)].reshape(CELLS, LANES)
        scores.append(nt(stack_heads(key), query) + bias)
    weights = []
    for pair in range(PAIRS):
        probs = softmax_rows(scores[pair]).reshape(scores[pair].shape)
        chances_ref[pair] = probs
        weights.append(probs.astype(BF))
    for pair in range(PAIRS):
        mixed = tn(weights[pair], stack_heads(v_ref[:, pair_slice(pair)]))
        mixed = (mixed * usable).astype(BF)
        out_ref[:, 0, :, pair_slice(pair)] = mixed.reshape(FRAMES, CELLS_HERE, LANES)
    out_ref[:, 1] = gm_ref[...].reshape(FRAMES, CELLS_HERE, WIDE)


def space_forward(counts, normed, values, grad_mixed):
    inner = values.shape[1]
    tokens = pl.BlockSpec((CELLS, WIDE), lambda n: (0, n))
    return pl.pallas_call(
        space_kernel,
        grid=(inner // WIDE,),
        in_specs=[
            SMEM,
            pl.BlockSpec((FRAMES, 2, CELLS_HERE, WIDE), lambda n: (0, 0, 0, n)),
            tokens,
            tokens,
        ],
        out_specs=[
            pl.BlockSpec((FRAMES, 2, CELLS_HERE, WIDE), lambda n: (0, 0, 0, n)),
            pl.BlockSpec((PAIRS, 2 * CELLS, CELLS), lambda n: (n, 0, 0)),
        ],
        out_shape=[
            jax.ShapeDtypeStruct((FRAMES, 2, CELLS_HERE, inner), BF),
            jax.ShapeDtypeStruct((inner // LANES, 2 * CELLS, CELLS), F32),
        ],
        compiler_params=PARAMS,
        cost_estimate=cost(7),
        name="space_forward",
    )(counts, normed, values, grad_mixed)


def gain_part(grad, normed):
    return jnp.sum(grad * normed.astype(F32), 0, keepdims=True)


def add_gains(sums_ref, of_query, of_key):
    @pl.when(pl.program_id(0) == 0)
    def _():
        sums_ref[...] = jnp.zeros_like(sums_ref)

    sums_ref[0:1] += of_query
    sums_ref[1:2] += of_key


def space_back_kernel(
    hat_q_ref, hat_k_ref, qk_ref, v_ref, up_ref, chances_ref, dq_ref, dk_ref, dv_ref, sums_ref
):
    of_query = jnp.zeros((1, LANES), F32)
    of_key = jnp.zeros((1, LANES), F32)
    slices = [pair_slice(pair) for pair in range(PAIRS)]
    queries = [qk_ref[:, 0, :, at].reshape(CELLS, LANES) for at in slices]
    keys = [stack_heads(qk_ref[:, 1, :, at].reshape(CELLS, LANES)) for at in slices]
    dchances = [nt(stack_heads(v_ref[:, at]), up_ref[:, at]) for at in slices]
    dscores = []
    for pair, at in enumerate(slices):
        probs = chances_ref[pair]
        dv_ref[:, at] = pick_heads(nn(probs.astype(BF), up_ref[:, at])).astype(BF)
        dscores.append(score_back(probs.reshape(2, CELLS, CELLS), dchances[pair]))
    for pair, at in enumerate(slices):
        dk = pick_heads(nn(dscores[pair], queries[pair]))
        dq = tn(dscores[pair], keys[pair]) * SCALE
        dk_ref[:, at] = dk
        dq_ref[:, at] = dq
        of_query += gain_part(dq, hat_q_ref[:, at])
        of_key += gain_part(dk, hat_k_ref[:, at])
    add_gains(sums_ref, of_query, of_key)


def space_back(queries, keys, normed, values, upstream, chances):
    inner = values.shape[1]
    tokens = pl.BlockSpec((CELLS, WIDE), lambda n: (0, n))
    wide = jax.ShapeDtypeStruct((CELLS, inner), F32)
    return pl.pallas_call(
        space_back_kernel,
        grid=(inner // WIDE,),
        in_specs=[
            tokens,
            tokens,
            pl.BlockSpec((FRAMES, 2, CELLS_HERE, WIDE), lambda n: (0, 0, 0, n)),
            tokens,
            tokens,
            pl.BlockSpec((PAIRS, 2 * CELLS, CELLS), lambda n: (n, 0, 0)),
        ],
        out_specs=[tokens, tokens, tokens, pl.BlockSpec((8, LANES), lambda n: (0, 0))],
        out_shape=[
            wide,
            wide,
            jax.ShapeDtypeStruct((CELLS, inner), BF),
            jax.ShapeDtypeStruct((8, LANES), F32),
        ],
        compiler_params=PARAMS,
        cost_estimate=cost(9),
        name="space_back",
    )(queries, keys, normed, values, upstream, chances)


def time_bias(frame_total):
    key = lax.broadcasted_iota(jnp.int32, (2 * LANES, LANES), 0) & (LANES - 1)
    query = lax.broadcasted_iota(jnp.int32, (2 * LANES, LANES), 1)
    same = (key & (BLOCK - 1)) == (query & (BLOCK - 1))
    return jnp.where(same & (lax.shift_right_logical(key, 4) < frame_total), 0.0, NEG)


def time_usable(counts_ref, block):
    row = lax.broadcasted_iota(jnp.int32, (LANES, LANES), 0)
    cell = counts_ref[3] * CELLS_HERE + block * BLOCK + (row & (BLOCK - 1))
    on = cell_ok(cell, counts_ref[1], counts_ref[2])
    return (on & (lax.shift_right_logical(row, 4) < counts_ref[0])).astype(F32)


def time_blocks():
    for block in range(CELLS_HERE // BLOCK):
        for pair in range(PAIRS):
            yield block, slice(block * BLOCK, (block + 1) * BLOCK), pair_slice(pair)


def time_kernel(counts_ref, qk_ref, sg_ref, out_ref):
    bias = time_bias(counts_ref[0])
    usable = [time_usable(counts_ref, block) for block in range(CELLS_HERE // BLOCK)]
    scores = []
    for block, rows, at in time_blocks():
        query = qk_ref[:, 0, rows, at].reshape(LANES, LANES)
        keys = stack_heads(qk_ref[:, 1, rows, at].reshape(LANES, LANES))
        scores.append(nt(keys, query) + bias)
    weights = [softmax_rows(part).astype(BF).reshape(part.shape) for part in scores]
    for number, (block, rows, at) in enumerate(time_blocks()):
        values = stack_heads(sg_ref[:, 0, rows, at].reshape(LANES, LANES))
        mixed = tn(weights[number], values) * usable[block]
        out_ref[:, rows, at] = mixed.astype(BF).reshape(FRAMES, BLOCK, LANES)


def time_back_kernel(counts_ref, qk_ref, sg_ref, dqk_ref, ds_ref, sums_ref):
    bias = time_bias(counts_ref[0])
    of_query = jnp.zeros((1, LANES), F32)
    of_key = jnp.zeros((1, LANES), F32)
    usable = [time_usable(counts_ref, block) for block in range(CELLS_HERE // BLOCK)]
    blocks = list(time_blocks())

    def load(ref, number, rows, at):
        return ref[:, number, rows, at].reshape(LANES, LANES)

    def shaped(tensor):
        return tensor.astype(BF).reshape(FRAMES, BLOCK, LANES)

    queries = [load(qk_ref, 0, rows, at) for _, rows, at in blocks]
    singles = [load(qk_ref, 1, rows, at) for _, rows, at in blocks]
    keys = [stack_heads(key) for key in singles]
    upstreams = [
        (load(sg_ref, 1, rows, at).astype(F32) * usable[block]).astype(BF)
        for block, rows, at in blocks
    ]
    scores = [nt(key, query) + bias for key, query in zip(keys, queries)]
    dchances = [
        nt(stack_heads(load(sg_ref, 0, rows, at)), upstream)
        for (_, rows, at), upstream in zip(blocks, upstreams)
    ]
    chances = [softmax_rows(part) for part in scores]
    dscores = [score_back(probs, part) for probs, part in zip(chances, dchances)]
    for number, (_, rows, at) in enumerate(blocks):
        weights = chances[number].astype(BF).reshape(2 * LANES, LANES)
        ds_ref[:, rows, at] = shaped(pick_heads(nn(weights, upstreams[number])))
        dq = tn(dscores[number], keys[number]) * SCALE
        dk = pick_heads(nn(dscores[number], queries[number]))
        dqk_ref[:, 0, rows, at] = shaped(dq)
        dqk_ref[:, 1, rows, at] = shaped(dk)
        of_query += gain_part(dq, queries[number])
        of_key += gain_part(dk, singles[number])
    add_gains(sums_ref, of_query, of_key)


def time_specs(inner):
    double = pl.BlockSpec((FRAMES, 2, CELLS_HERE, WIDE), lambda n: (0, 0, 0, n))
    single = pl.BlockSpec((FRAMES, CELLS_HERE, WIDE), lambda n: (0, 0, n))
    return (
        double,
        single,
        jax.ShapeDtypeStruct((FRAMES, 2, CELLS_HERE, inner), BF),
        jax.ShapeDtypeStruct((FRAMES, CELLS_HERE, inner), BF),
    )


def time_forward(counts, normed, arrived):
    inner = arrived.shape[3]
    double, single, _, single_shape = time_specs(inner)
    return pl.pallas_call(
        time_kernel,
        grid=(inner // WIDE,),
        in_specs=[SMEM, double, double],
        out_specs=single,
        out_shape=single_shape,
        compiler_params=PARAMS,
        cost_estimate=cost(5),
        name="time_forward",
    )(counts, normed, arrived)


def time_back(counts, normed, arrived):
    inner = arrived.shape[3]
    double, single, double_shape, single_shape = time_specs(inner)
    return pl.pallas_call(
        time_back_kernel,
        grid=(inner // WIDE,),
        in_specs=[SMEM, double, double],
        out_specs=[double, single, pl.BlockSpec((8, LANES), lambda n: (0, 0))],
        out_shape=[double_shape, single_shape, jax.ShapeDtypeStruct((8, LANES), F32)],
        compiler_params=PARAMS,
        cost_estimate=cost(6.5),
        name="time_back",
    )(counts, normed, arrived)


def norm_back_kernel(
    hat_q_ref,
    hat_k_ref,
    inverse_q_ref,
    inverse_k_ref,
    gain_q_ref,
    gain_k_ref,
    dq_ref,
    dk_ref,
    late_ref,
    gq_ref,
    gk_ref,
):
    twice = head_ones(DUO, LANES)
    for left in range(0, NORM_WIDE, LANES):
        at = slice(left, left + LANES)
        for number, (hat_ref, inverse_ref, gain_ref, early, target) in enumerate(
            (
                (hat_q_ref, inverse_q_ref, gain_q_ref, dq_ref, gq_ref),
                (hat_k_ref, inverse_k_ref, gain_k_ref, dk_ref, gk_ref),
            )
        ):
            hat = hat_ref[:, at]
            late = late_ref[:, number, :, at].reshape(CELLS, LANES)
            scaled = (early[:, at] + late.astype(F32)) * both_heads(gain_ref)
            mean = head_mean(scaled, twice)
            dinput = scaled - mean - hat * head_mean(scaled * hat, twice)
            target[:, at] = (inverse_ref[:, at] * dinput).astype(BF)


def norm_back(hats, gain_query, gain_key, dq, dk, late):
    inner = dq.shape[1]
    tokens = pl.BlockSpec((CELLS, NORM_WIDE), lambda n: (0, n))
    gain = pl.BlockSpec((1, HD), lambda n: (0, 0))
    grads = jax.ShapeDtypeStruct((CELLS, inner), BF)
    return pl.pallas_call(
        norm_back_kernel,
        grid=(inner // NORM_WIDE,),
        in_specs=[
            tokens,
            tokens,
            tokens,
            tokens,
            gain,
            gain,
            tokens,
            tokens,
            pl.BlockSpec((FRAMES, 2, CELLS_HERE, NORM_WIDE), lambda n: (0, 0, 0, n)),
        ],
        out_specs=[tokens, tokens],
        out_shape=[grads, grads],
        compiler_params=PARAMS,
        cost_estimate=cost(7),
        name="norm_back",
    )(*hats, gain_query, gain_key, dq, dk, late)


def grad_mixed_kernel(cot_ref, weight_ref, out_ref):
    out_ref[...] = nt(cot_ref[...], weight_ref[...]).astype(BF)


def grad_mixed_of(cotangent, weight):
    inner, width = weight.shape
    return pl.pallas_call(
        grad_mixed_kernel,
        grid=(inner // WIDE,),
        in_specs=[
            pl.BlockSpec((CELLS, width), lambda n: (0, 0)),
            pl.BlockSpec((WIDE, width), lambda n: (n, 0)),
        ],
        out_specs=pl.BlockSpec((CELLS, WIDE), lambda n: (0, n)),
        out_shape=jax.ShapeDtypeStruct((CELLS, inner), BF),
        compiler_params=PARAMS,
        cost_estimate=cost(8.7),
        name="grad_mixed",
    )(cotangent, weight)


def project_kernel(mixed_ref, weight_ref, out_ref):
    out_ref[...] = nn(mixed_ref[...], weight_ref[...]).astype(BF)


def project(mixed, weight):
    inner, width = weight.shape
    block = width // 4
    return pl.pallas_call(
        project_kernel,
        grid=(4,),
        in_specs=[
            pl.BlockSpec((CELLS, inner), lambda n: (0, 0)),
            pl.BlockSpec((inner, block), lambda n: (0, n)),
        ],
        out_specs=pl.BlockSpec((CELLS, block), lambda n: (0, n)),
        out_shape=jax.ShapeDtypeStruct((CELLS, width), BF),
        compiler_params=PARAMS,
        cost_estimate=cost(7),
        name="project",
    )(mixed, weight)


TAIL = 16


def weight_kernel(place_ref, order_ref, mixed_ref, cot_ref, out_ref, turned, product):
    shares, rows, _ = out_ref.shape
    own = (rows - TAIL) // 4

    @pl.when(pl.program_id(0) == 0)
    def _():
        turned[...] = nt(order_ref[0], mixed_ref[...]).astype(BF)

    product[...] = nn(turned[...], cot_ref[...])
    for quarter in range(4):

        @pl.when(pl.program_id(0) == quarter)
        def _():
            for share in range(shares):
                out_ref[share, quarter * own : (quarter + 1) * own] = product[
                    share * own : (share + 1) * own
                ].astype(BF)


def weight_parts(place, order, mixed, cotangents, shares):
    tokens, width = cotangents.shape
    _, features, wide = order.shape
    block = width // 4
    rows = 4 * (features // shares) + TAIL
    return pl.pallas_call(
        weight_kernel,
        grid_spec=pltpu.PrefetchScalarGridSpec(
            num_scalar_prefetch=1,
            grid=(4,),
            in_specs=[
                pl.BlockSpec((1, features, wide), lambda n, place: (place[1], 0, 0)),
                pl.BlockSpec((tokens, wide), lambda n, place: (0, place[0])),
                pl.BlockSpec((tokens, block), lambda n, place: (0, n)),
            ],
            out_specs=pl.BlockSpec((shares, rows, block), lambda n, place: (0, 0, 0)),
            scratch_shapes=[
                pltpu.VMEM((features, tokens), BF),
                pltpu.VMEM((features, block), F32),
            ],
        ),
        out_shape=jax.ShapeDtypeStruct((shares, rows, block), BF),
        compiler_params=PARAMS,
        cost_estimate=cost(9.5),
        name="weight_parts",
    )(place, order, mixed, cotangents)


def tail_kernel(gain_ref, _, out_ref):
    terms = []
    for row in range(2):
        rest = gain_ref[row : row + 1]
        for _ in range(3):
            terms.append(rest.astype(BF).astype(F32))
            rest = rest - terms[-1]
    block = out_ref.shape[2]
    rows = jnp.concatenate(terms + [jnp.zeros((TAIL - 6, LANES), F32)], 0)
    rows = jnp.concatenate([rows, jnp.zeros((TAIL, block - LANES), F32)], 1).astype(BF)
    for share in range(out_ref.shape[0]):
        out_ref[share] = rows


def add_tail(gain_sums, parts):
    shares, rows, block = parts.shape
    return pl.pallas_call(
        tail_kernel,
        grid=(1,),
        in_specs=[
            pl.BlockSpec(gain_sums.shape, lambda n: (0, 0)),
            pl.BlockSpec(memory_space=pl.ANY),
        ],
        out_specs=pl.BlockSpec((shares, TAIL, block), lambda n: (0, rows // TAIL - 1, 0)),
        out_shape=jax.ShapeDtypeStruct(parts.shape, BF),
        input_output_aliases={1: 0},
        compiler_params=PARAMS,
        cost_estimate=cost(1.5),
        name="add_tail",
    )(gain_sums, parts)


def sum_kernel(parts_ref, out_ref, gain_ref):
    shares, rows, block = parts_ref.shape
    own = (rows - TAIL) // 4
    total = parts_ref[0].astype(F32)
    for share in range(1, shares):
        total = total + parts_ref[share].astype(F32)
    for quarter in range(4):
        out_ref[:, quarter * block : (quarter + 1) * block] = total[
            quarter * own : (quarter + 1) * own
        ]
    gain_ref[...] = total[rows - TAIL : rows - TAIL + 8, :LANES]


def sum_parts(parts):
    _, rows, block = parts.shape
    return pl.pallas_call(
        sum_kernel,
        in_specs=[VMEM],
        out_specs=[VMEM, VMEM],
        out_shape=[
            jax.ShapeDtypeStruct(((rows - TAIL) // 4, 4 * block), F32),
            jax.ShapeDtypeStruct((8, LANES), F32),
        ],
        compiler_params=PARAMS,
        cost_estimate=cost(2.2),
        name="sum_parts",
    )(parts)


def feature_order(inner, planes, cores, shares):
    wide = inner // planes
    features = wide // cores
    own = features // shares
    order = np.zeros((cores, features, wide), np.float32)
    for core in range(cores):
        for feature in range(features):
            share, row = divmod(feature, own)
            order[core, feature, own * (cores * share + core) + row] = 1.0
    return jnp.asarray(order, BF)


def local(
    queries,
    keys_proj,
    values_proj,
    gain_query,
    gain_key,
    frame_counts,
    heights,
    widths,
    out_weight,
    cotangent,
):
    seq = ("y", "core")
    group = ("x", "core")
    sums = ("z", "y")
    planes, cores = lax.axis_size("x"), lax.axis_size("core")
    shares = lax.axis_size("z") * lax.axis_size("y")
    inner = out_weight.shape[0]
    rank = lax.axis_index(seq).astype(jnp.int32)
    counts = jnp.stack([frame_counts[0], heights[0], widths[0], rank])
    gains = gain_query.reshape(1, HD), gain_key.reshape(1, HD)
    query_rows, key_rows, value_rows = queries[0, 0], keys_proj[0, 0], values_proj[0, 0]
    cot_rows = cotangent[0, 0]
    by_cells = (FRAMES, CELLS_HERE, inner)

    def exchange(tensor, axes):
        return lax.all_to_all(tensor, axes, split_axis=0, concat_axis=0, tiled=True)

    def after(tensor, earlier):
        return lax.optimization_barrier((tensor, earlier))[0]

    cotangents = lax.all_gather(cot_rows, group, axis=0, tiled=True)
    normed = norm(query_rows, key_rows, *gains)
    normed_cells = exchange(normed, seq)
    grad_mixed = grad_mixed_of(cot_rows, out_weight)
    outgoing, chances = space_forward(counts, normed, value_rows, grad_mixed)
    arrived = exchange(after(outgoing, normed_cells), seq)
    hats = hats_of(*lax.optimization_barrier((query_rows, key_rows, outgoing))[:2])
    arrived, *hats = lax.optimization_barrier((arrived, *hats))
    mixed_cells = time_forward(counts, normed_cells, arrived)
    mixed = exchange(mixed_cells, seq).reshape(CELLS, inner)
    late_cells, dspatial_cells, late_gains = time_back(counts, normed_cells, arrived)
    place = jnp.stack([lax.axis_index("x"), lax.axis_index("core")]).astype(jnp.int32)
    first = (cotangents, dspatial_cells)
    gathered = lax.all_gather(after(mixed, first), group, axis=0, tiled=True)
    dspatial = exchange(after(dspatial_cells, mixed), seq).reshape(CELLS, inner)
    late = exchange(after(late_cells, dspatial), seq)
    block_out = project(mixed, out_weight)
    order = feature_order(inner, planes, cores, shares)
    parts = weight_parts(place, order, gathered, cotangents, shares)
    dq, dk, grad_values, early_gains = space_back(
        hats[0], hats[1], normed, value_rows, dspatial, chances
    )
    late_scale = jnp.stack([gain_query * SCALE, gain_key])
    late_scale = jnp.pad(jnp.tile(late_scale, (1, 2)), ((0, 6), (0, 0)), constant_values=1.0)
    gain_sums = early_gains + late_gains / late_scale
    for axis, extent in (("core", cores), ("x", planes)):
        flip = 1
        while flip < extent:
            pairs = [(i, i ^ flip) for i in range(extent)]
            gain_sums = gain_sums + lax.ppermute(gain_sums, axis, pairs)
            flip *= 2
    grad_queries, grad_keys = norm_back(hats, *gains, dq, dk, late)
    parts = exchange(after(add_tail(gain_sums, parts), late), sums)
    grad_weight, tail = sum_parts(parts)
    gain_sums = jnp.stack([jnp.sum(tail[:3], 0), jnp.sum(tail[3:6], 0)])
    gain_sums = gain_sums[:, :HD] + gain_sums[:, HD:]
    return (
        block_out.reshape(cotangent.shape),
        grad_queries.reshape(queries.shape),
        grad_keys.reshape(queries.shape),
        grad_values.reshape(queries.shape),
        grad_weight,
        gain_sums[0],
        gain_sums[1],
    )


def solution(mesh):
    planes = 4 if mesh.shape["dp"] == 16 else mesh.shape["dp"]
    fine = Mesh(
        mesh.devices.reshape(planes, mesh.shape["dp"] // planes, -1, 2), ("x", "z", "y", "core")
    )
    tokens = P(("x", "z"), ("y", "core"), None, None)
    clips = P(("x", "z"))
    return jax.shard_map(
        local,
        mesh=fine,
        in_specs=(tokens, tokens, tokens, P(), P(), clips, clips, clips, P(), tokens),
        out_specs=(
            tokens,
            tokens,
            tokens,
            tokens,
            P(("x", "z", "y", "core"), None),
            P(),
            P(),
        ),
        check_vma=False,
    )
```

```python
import jax
import jax.numpy as jnp
import numpy as np
from jax import lax
from jax.experimental import pallas as pl
from jax.experimental.pallas import tpu as pltpu
from jax.sharding import Mesh
from jax.sharding import PartitionSpec as P

BF = jnp.bfloat16
F32 = jnp.float32
HD = 64
PW = 16
CELLS = 256
FRAMES = 8
LANES = 128
WIDE = 384
PAIRS = WIDE // LANES
CELLS_HERE = CELLS // FRAMES
BLOCK = 16
NEG = -1e30
SCALE = HD**-0.5
PARAMS = pltpu.CompilerParams(vmem_limit_bytes=60 * 1024 * 1024)


def cost(microseconds):
    return pl.CostEstimate(flops=0, bytes_accessed=int(microseconds * 3.69e6), transcendentals=0)


SMEM = pl.BlockSpec(memory_space=pltpu.SMEM)
VMEM = pl.BlockSpec(memory_space=pltpu.VMEM)


def nn(left, right):
    return jnp.dot(left, right, preferred_element_type=F32)


def nt(left, right):
    return lax.dot_general(left, right, (((1,), (1,)), ((), ())), preferred_element_type=F32)


def tn(left, right):
    return lax.dot_general(left, right, (((0,), (0,)), ((), ())), preferred_element_type=F32)


def low_lanes(shape):
    return lax.broadcasted_iota(jnp.int32, shape, len(shape) - 1) < HD


def stack_heads(pair):
    low = low_lanes((1, LANES)).astype(F32)
    return jnp.concatenate([pair * low.astype(BF), pair * (1.0 - low).astype(BF)], 0)


def pick_heads(stacked):
    half = stacked.shape[0] // 2
    return jnp.where(low_lanes((half, LANES)), stacked[:half], stacked[half:])


def softmax_rows(scores):
    grouped = scores.reshape(2, scores.shape[0] // 2, scores.shape[1])
    expo = jnp.exp(grouped - jnp.max(grouped, 1, keepdims=True))
    return expo * (1.0 / jnp.sum(expo, 1, keepdims=True))


def score_back(chances, dchances):
    grouped = dchances.reshape(chances.shape)
    total = jnp.sum(chances * grouped, 1, keepdims=True)
    return (chances * (grouped - total)).astype(BF).reshape(dchances.shape)


def cell_ok(cells, height, width):
    row = lax.shift_right_logical(cells, 4)
    return (row < height) & ((cells & (PW - 1)) < width)


def head_ones(rows, columns):
    row = lax.broadcasted_iota(jnp.int32, (rows, columns), 0) & (columns - 1)
    column = lax.broadcasted_iota(jnp.int32, (rows, columns), 1)
    same = lax.shift_right_logical(row, 6) == lax.shift_right_logical(column, 6)
    return jnp.where(same, 1.0, 0.0).astype(BF)


def head_mean(tensor, twice):
    high = tensor.astype(BF)
    rest = (tensor - high.astype(F32)).astype(BF)
    return nn(jnp.concatenate([high, rest], 1), twice) * (1.0 / HD)


def hat_of(raw, ones, twice):
    centre = raw.astype(F32) - nn(raw, ones) * (1.0 / HD)
    hats, inverses = [], []
    for left in range(0, raw.shape[1], LANES):
        part = centre[:, left : left + LANES]
        inverse = lax.rsqrt(head_mean(part * part, twice) + 1e-06)
        hats.append(part * inverse)
        inverses.append(inverse)
    return hats, inverses


def both_heads(gain_ref):
    return jnp.concatenate([gain_ref[...], gain_ref[...]], 1)


def pair_slice(number):
    return slice(number * LANES, (number + 1) * LANES)


NORM_WIDE = 512
DUO = 2 * LANES


def norm_kernel(q_ref, k_ref, gain_q_ref, gain_k_ref, out_ref):
    ones, twice = head_ones(DUO, DUO), head_ones(DUO, LANES)
    gains = both_heads(gain_q_ref), both_heads(gain_k_ref)
    for left in range(0, NORM_WIDE, DUO):
        for number, source in enumerate((q_ref, k_ref)):
            hats, _ = hat_of(source[:, left : left + DUO], ones, twice)
            for pair, hat in enumerate(hats):
                normed = (hat * gains[number]).astype(BF)
                if number == 0:
                    normed = normed * jnp.asarray(SCALE, BF)
                at = slice(left + pair * LANES, left + (pair + 1) * LANES)
                out_ref[:, number, :, at] = normed.reshape(FRAMES, CELLS_HERE, LANES)


def norm(queries, keys, gain_query, gain_key):
    inner = queries.shape[1]
    tokens = pl.BlockSpec((CELLS, NORM_WIDE), lambda n: (0, n))
    gain = pl.BlockSpec((1, HD), lambda n: (0, 0))
    return pl.pallas_call(
        norm_kernel,
        grid=(inner // NORM_WIDE,),
        in_specs=[tokens, tokens, gain, gain],
        out_specs=pl.BlockSpec((FRAMES, 2, CELLS_HERE, NORM_WIDE), lambda n: (0, 0, 0, n)),
        out_shape=jax.ShapeDtypeStruct((FRAMES, 2, CELLS_HERE, inner), BF),
        compiler_params=PARAMS,
        cost_estimate=cost(5),
        name="norm",
    )(queries, keys, gain_query, gain_key)


def hats_kernel(q_ref, k_ref, *out_refs):
    ones, twice = head_ones(DUO, DUO), head_ones(DUO, LANES)
    for left in range(0, NORM_WIDE, DUO):
        for number, source in enumerate((q_ref, k_ref)):
            hats, inverses = hat_of(source[:, left : left + DUO], ones, twice)
            at = slice(left, left + DUO)
            out_refs[number][:, at] = jnp.concatenate(hats, 1)
            out_refs[2 + number][:, at] = jnp.concatenate(inverses, 1)


def hats_of(queries, keys):
    inner = queries.shape[1]
    tokens = pl.BlockSpec((CELLS, NORM_WIDE), lambda n: (0, n))
    return pl.pallas_call(
        hats_kernel,
        grid=(inner // NORM_WIDE,),
        in_specs=[tokens, tokens],
        out_specs=[tokens] * 4,
        out_shape=[jax.ShapeDtypeStruct((CELLS, inner), F32)] * 4,
        compiler_params=PARAMS,
        cost_estimate=cost(5.6),
        name="hats",
    )(queries, keys)


def space_kernel(counts_ref, qk_ref, v_ref, gm_ref, out_ref, chances_ref):
    height, width = counts_ref[1], counts_ref[2]
    frame_on = jnp.where(counts_ref[3] < counts_ref[0], 1.0, 0.0)
    key_cell = lax.broadcasted_iota(jnp.int32, (2 * CELLS, CELLS), 0) & (CELLS - 1)
    bias = jnp.where(cell_ok(key_cell, height, width), 0.0, NEG)
    cell = lax.broadcasted_iota(jnp.int32, (CELLS, LANES), 0)
    usable = cell_ok(cell, height, width).astype(F32) * frame_on
    scores = []
    for pair in range(PAIRS):
        query = qk_ref[:, 0, :, pair_slice(pair)].reshape(CELLS, LANES)
        key = qk_ref[:, 1, :, pair_slice(pair)].reshape(CELLS, LANES)
        scores.append(nt(stack_heads(key), query) + bias)
    weights = []
    for pair in range(PAIRS):
        probs = softmax_rows(scores[pair]).reshape(scores[pair].shape)
        chances_ref[pair] = probs
        weights.append(probs.astype(BF))
    for pair in range(PAIRS):
        mixed = tn(weights[pair], stack_heads(v_ref[:, pair_slice(pair)]))
        mixed = (mixed * usable).astype(BF)
        out_ref[:, 0, :, pair_slice(pair)] = mixed.reshape(FRAMES, CELLS_HERE, LANES)
    out_ref[:, 1] = gm_ref[...].reshape(FRAMES, CELLS_HERE, WIDE)


def space_forward(counts, normed, values, grad_mixed):
    inner = values.shape[1]
    tokens = pl.BlockSpec((CELLS, WIDE), lambda n: (0, n))
    return pl.pallas_call(
        space_kernel,
        grid=(inner // WIDE,),
        in_specs=[
            SMEM,
            pl.BlockSpec((FRAMES, 2, CELLS_HERE, WIDE), lambda n: (0, 0, 0, n)),
            tokens,
            tokens,
        ],
        out_specs=[
            pl.BlockSpec((FRAMES, 2, CELLS_HERE, WIDE), lambda n: (0, 0, 0, n)),
            pl.BlockSpec((PAIRS, 2 * CELLS, CELLS), lambda n: (n, 0, 0)),
        ],
        out_shape=[
            jax.ShapeDtypeStruct((FRAMES, 2, CELLS_HERE, inner), BF),
            jax.ShapeDtypeStruct((inner // LANES, 2 * CELLS, CELLS), F32),
        ],
        compiler_params=PARAMS,
        cost_estimate=cost(7),
        name="space_forward",
    )(counts, normed, values, grad_mixed)


def gain_part(grad, normed):
    return jnp.sum(grad * normed.astype(F32), 0, keepdims=True)


def add_gains(sums_ref, of_query, of_key, begin=None):
    @pl.when(pl.program_id(0) == 0)
    def _():
        sums_ref[...] = jnp.zeros_like(sums_ref) if begin is None else begin()

    sums_ref[0:1] += of_query
    sums_ref[1:2] += of_key


def space_back_kernel(
    late_ref,
    gain_q_ref,
    gain_k_ref,
    hat_q_ref,
    hat_k_ref,
    qk_ref,
    v_ref,
    up_ref,
    chances_ref,
    dq_ref,
    dk_ref,
    dv_ref,
    sums_ref,
):
    def late_gains():
        scale = [both_heads(gain_q_ref) * SCALE, both_heads(gain_k_ref)]
        return late_ref[...] / jnp.concatenate(scale + [jnp.ones((6, LANES), F32)], 0)

    of_query = jnp.zeros((1, LANES), F32)
    of_key = jnp.zeros((1, LANES), F32)
    slices = [pair_slice(pair) for pair in range(PAIRS)]
    queries = [qk_ref[:, 0, :, at].reshape(CELLS, LANES) for at in slices]
    keys = [stack_heads(qk_ref[:, 1, :, at].reshape(CELLS, LANES)) for at in slices]
    dchances = [nt(stack_heads(v_ref[:, at]), up_ref[:, at]) for at in slices]
    dscores = []
    for pair, at in enumerate(slices):
        probs = chances_ref[pair]
        dv_ref[:, at] = pick_heads(nn(probs.astype(BF), up_ref[:, at])).astype(BF)
        dscores.append(score_back(probs.reshape(2, CELLS, CELLS), dchances[pair]))
    for pair, at in enumerate(slices):
        dk = pick_heads(nn(dscores[pair], queries[pair]))
        dq = tn(dscores[pair], keys[pair]) * SCALE
        dk_ref[:, at] = dk
        dq_ref[:, at] = dq
        of_query += gain_part(dq, hat_q_ref[:, at])
        of_key += gain_part(dk, hat_k_ref[:, at])
    add_gains(sums_ref, of_query, of_key, late_gains)


def space_back(late_sums, gain_query, gain_key, hats, normed, values, upstream, chances):
    inner = values.shape[1]
    tokens = pl.BlockSpec((CELLS, WIDE), lambda n: (0, n))
    wide = jax.ShapeDtypeStruct((CELLS, inner), F32)
    return pl.pallas_call(
        space_back_kernel,
        grid=(inner // WIDE,),
        in_specs=[
            pl.BlockSpec((8, LANES), lambda n: (0, 0)),
            pl.BlockSpec((1, HD), lambda n: (0, 0)),
            pl.BlockSpec((1, HD), lambda n: (0, 0)),
            tokens,
            tokens,
            pl.BlockSpec((FRAMES, 2, CELLS_HERE, WIDE), lambda n: (0, 0, 0, n)),
            tokens,
            tokens,
            pl.BlockSpec((PAIRS, 2 * CELLS, CELLS), lambda n: (n, 0, 0)),
        ],
        out_specs=[tokens, tokens, tokens, pl.BlockSpec((8, LANES), lambda n: (0, 0))],
        out_shape=[
            wide,
            wide,
            jax.ShapeDtypeStruct((CELLS, inner), BF),
            jax.ShapeDtypeStruct((8, LANES), F32),
        ],
        compiler_params=PARAMS,
        cost_estimate=cost(9),
        name="space_back",
    )(late_sums, gain_query, gain_key, *hats, normed, values, upstream, chances)


def time_bias(frame_total):
    key = lax.broadcasted_iota(jnp.int32, (2 * LANES, LANES), 0) & (LANES - 1)
    query = lax.broadcasted_iota(jnp.int32, (2 * LANES, LANES), 1)
    same = (key & (BLOCK - 1)) == (query & (BLOCK - 1))
    return jnp.where(same & (lax.shift_right_logical(key, 4) < frame_total), 0.0, NEG)


def time_usable(counts_ref, block):
    row = lax.broadcasted_iota(jnp.int32, (LANES, LANES), 0)
    cell = counts_ref[3] * CELLS_HERE + block * BLOCK + (row & (BLOCK - 1))
    on = cell_ok(cell, counts_ref[1], counts_ref[2])
    return (on & (lax.shift_right_logical(row, 4) < counts_ref[0])).astype(F32)


def time_blocks():
    for block in range(CELLS_HERE // BLOCK):
        for pair in range(PAIRS):
            yield block, slice(block * BLOCK, (block + 1) * BLOCK), pair_slice(pair)


def time_kernel(counts_ref, qk_ref, sg_ref, out_ref):
    bias = time_bias(counts_ref[0])
    usable = [time_usable(counts_ref, block) for block in range(CELLS_HERE // BLOCK)]
    scores = []
    for block, rows, at in time_blocks():
        query = qk_ref[:, 0, rows, at].reshape(LANES, LANES)
        keys = stack_heads(qk_ref[:, 1, rows, at].reshape(LANES, LANES))
        scores.append(nt(keys, query) + bias)
    weights = [softmax_rows(part).astype(BF).reshape(part.shape) for part in scores]
    for number, (block, rows, at) in enumerate(time_blocks()):
        values = stack_heads(sg_ref[:, 0, rows, at].reshape(LANES, LANES))
        mixed = tn(weights[number], values) * usable[block]
        out_ref[:, rows, at] = mixed.astype(BF).reshape(FRAMES, BLOCK, LANES)


def time_back_kernel(counts_ref, qk_ref, sg_ref, dqk_ref, ds_ref, sums_ref):
    bias = time_bias(counts_ref[0])
    of_query = jnp.zeros((1, LANES), F32)
    of_key = jnp.zeros((1, LANES), F32)
    usable = [time_usable(counts_ref, block) for block in range(CELLS_HERE // BLOCK)]
    blocks = list(time_blocks())

    def load(ref, number, rows, at):
        return ref[:, number, rows, at].reshape(LANES, LANES)

    def shaped(tensor):
        return tensor.astype(BF).reshape(FRAMES, BLOCK, LANES)

    queries = [load(qk_ref, 0, rows, at) for _, rows, at in blocks]
    singles = [load(qk_ref, 1, rows, at) for _, rows, at in blocks]
    keys = [stack_heads(key) for key in singles]
    upstreams = [
        (load(sg_ref, 1, rows, at).astype(F32) * usable[block]).astype(BF)
        for block, rows, at in blocks
    ]
    scores = [nt(key, query) + bias for key, query in zip(keys, queries)]
    dchances = [
        nt(stack_heads(load(sg_ref, 0, rows, at)), upstream)
        for (_, rows, at), upstream in zip(blocks, upstreams)
    ]
    chances = [softmax_rows(part) for part in scores]
    dscores = [score_back(probs, part) for probs, part in zip(chances, dchances)]
    for number, (_, rows, at) in enumerate(blocks):
        weights = chances[number].astype(BF).reshape(2 * LANES, LANES)
        ds_ref[:, rows, at] = shaped(pick_heads(nn(weights, upstreams[number])))
        dq = tn(dscores[number], keys[number]) * SCALE
        dk = pick_heads(nn(dscores[number], queries[number]))
        dqk_ref[:, 0, rows, at] = shaped(dq)
        dqk_ref[:, 1, rows, at] = shaped(dk)
        of_query += gain_part(dq, queries[number])
        of_key += gain_part(dk, singles[number])
    add_gains(sums_ref, of_query, of_key)


def time_specs(inner):
    double = pl.BlockSpec((FRAMES, 2, CELLS_HERE, WIDE), lambda n: (0, 0, 0, n))
    single = pl.BlockSpec((FRAMES, CELLS_HERE, WIDE), lambda n: (0, 0, n))
    return (
        double,
        single,
        jax.ShapeDtypeStruct((FRAMES, 2, CELLS_HERE, inner), BF),
        jax.ShapeDtypeStruct((FRAMES, CELLS_HERE, inner), BF),
    )


def time_forward(counts, normed, arrived):
    inner = arrived.shape[3]
    double, single, _, single_shape = time_specs(inner)
    return pl.pallas_call(
        time_kernel,
        grid=(inner // WIDE,),
        in_specs=[SMEM, double, double],
        out_specs=single,
        out_shape=single_shape,
        compiler_params=PARAMS,
        cost_estimate=cost(5),
        name="time_forward",
    )(counts, normed, arrived)


def time_back(counts, normed, arrived):
    inner = arrived.shape[3]
    double, single, double_shape, single_shape = time_specs(inner)
    return pl.pallas_call(
        time_back_kernel,
        grid=(inner // WIDE,),
        in_specs=[SMEM, double, double],
        out_specs=[double, single, pl.BlockSpec((8, LANES), lambda n: (0, 0))],
        out_shape=[double_shape, single_shape, jax.ShapeDtypeStruct((8, LANES), F32)],
        compiler_params=PARAMS,
        cost_estimate=cost(6.5),
        name="time_back",
    )(counts, normed, arrived)


def norm_back_kernel(
    hat_q_ref,
    hat_k_ref,
    inverse_q_ref,
    inverse_k_ref,
    gain_q_ref,
    gain_k_ref,
    dq_ref,
    dk_ref,
    late_ref,
    gq_ref,
    gk_ref,
):
    twice = head_ones(DUO, LANES)
    for left in range(0, NORM_WIDE, LANES):
        at = slice(left, left + LANES)
        for number, (hat_ref, inverse_ref, gain_ref, early, target) in enumerate(
            (
                (hat_q_ref, inverse_q_ref, gain_q_ref, dq_ref, gq_ref),
                (hat_k_ref, inverse_k_ref, gain_k_ref, dk_ref, gk_ref),
            )
        ):
            hat = hat_ref[:, at]
            late = late_ref[:, number, :, at].reshape(CELLS, LANES)
            scaled = (early[:, at] + late.astype(F32)) * both_heads(gain_ref)
            mean = head_mean(scaled, twice)
            dinput = scaled - mean - hat * head_mean(scaled * hat, twice)
            target[:, at] = (inverse_ref[:, at] * dinput).astype(BF)


def norm_back(hats, gain_query, gain_key, dq, dk, late):
    inner = dq.shape[1]
    tokens = pl.BlockSpec((CELLS, NORM_WIDE), lambda n: (0, n))
    gain = pl.BlockSpec((1, HD), lambda n: (0, 0))
    grads = jax.ShapeDtypeStruct((CELLS, inner), BF)
    return pl.pallas_call(
        norm_back_kernel,
        grid=(inner // NORM_WIDE,),
        in_specs=[
            tokens,
            tokens,
            tokens,
            tokens,
            gain,
            gain,
            tokens,
            tokens,
            pl.BlockSpec((FRAMES, 2, CELLS_HERE, NORM_WIDE), lambda n: (0, 0, 0, n)),
        ],
        out_specs=[tokens, tokens],
        out_shape=[grads, grads],
        compiler_params=PARAMS,
        cost_estimate=cost(7),
        name="norm_back",
    )(*hats, gain_query, gain_key, dq, dk, late)


def grad_mixed_kernel(cot_ref, weight_ref, out_ref):
    out_ref[...] = nt(cot_ref[...], weight_ref[...]).astype(BF)


def grad_mixed_of(cotangent, weight):
    inner, width = weight.shape
    return pl.pallas_call(
        grad_mixed_kernel,
        grid=(inner // WIDE,),
        in_specs=[
            pl.BlockSpec((CELLS, width), lambda n: (0, 0)),
            pl.BlockSpec((WIDE, width), lambda n: (n, 0)),
        ],
        out_specs=pl.BlockSpec((CELLS, WIDE), lambda n: (0, n)),
        out_shape=jax.ShapeDtypeStruct((CELLS, inner), BF),
        compiler_params=PARAMS,
        cost_estimate=cost(8.7),
        name="grad_mixed",
    )(cotangent, weight)


def project_kernel(mixed_ref, weight_ref, out_ref):
    out_ref[...] = nn(mixed_ref[...], weight_ref[...]).astype(BF)


def project(mixed, weight):
    inner, width = weight.shape
    block = width // 4
    return pl.pallas_call(
        project_kernel,
        grid=(4,),
        in_specs=[
            pl.BlockSpec((CELLS, inner), lambda n: (0, 0)),
            pl.BlockSpec((inner, block), lambda n: (0, n)),
        ],
        out_specs=pl.BlockSpec((CELLS, block), lambda n: (0, n)),
        out_shape=jax.ShapeDtypeStruct((CELLS, width), BF),
        compiler_params=PARAMS,
        cost_estimate=cost(7),
        name="project",
    )(mixed, weight)


PIECES = 6
TAIL = 8


def weight_kernel(place_ref, order_ref, mixed_ref, cot_ref, out_ref, turned, product):
    shares = out_ref.shape[0]
    own = product.shape[0] // shares

    @pl.when(pl.program_id(0) == 0)
    def _():
        turned[...] = nt(order_ref[0], mixed_ref[...]).astype(BF)

    product[...] = nn(turned[...], cot_ref[...])
    for piece in range(PIECES):

        @pl.when(pl.program_id(0) == piece)
        def _():
            for share in range(shares):
                out_ref[share, piece * own : (piece + 1) * own] = product[
                    share * own : (share + 1) * own
                ].astype(BF)


def weight_parts(place, order, mixed, cotangents, shares):
    tokens, width = cotangents.shape
    _, features, wide = order.shape
    block = width // PIECES
    rows = -(-(PIECES * (features // shares) + TAIL) // 16) * 16
    return pl.pallas_call(
        weight_kernel,
        grid_spec=pltpu.PrefetchScalarGridSpec(
            num_scalar_prefetch=1,
            grid=(PIECES,),
            in_specs=[
                pl.BlockSpec((1, features, wide), lambda n, place: (place[1], 0, 0)),
                pl.BlockSpec((tokens, wide), lambda n, place: (0, place[0])),
                pl.BlockSpec((tokens, block), lambda n, place: (0, n)),
            ],
            out_specs=pl.BlockSpec((shares, rows, block), lambda n, place: (0, 0, 0)),
            scratch_shapes=[
                pltpu.VMEM((features, tokens), BF),
                pltpu.VMEM((features, block), F32),
            ],
        ),
        out_shape=jax.ShapeDtypeStruct((shares, rows, block), BF),
        compiler_params=PARAMS,
        cost_estimate=cost(9.5),
        name="weight_parts",
    )(place, order, mixed, cotangents)


def tail_kernel(*refs):
    *gain_refs, parts_ref, out_ref = refs
    total = gain_refs[0][...]
    for gain_ref in gain_refs[1:]:
        total = total + gain_ref[...]
    terms = []
    for row in range(2):
        rest = total[row : row + 1]
        for _ in range(3):
            terms.append(rest.astype(BF).astype(F32))
            rest = rest - terms[-1]
    block = out_ref.shape[2]
    rows = jnp.concatenate(terms + [jnp.zeros((TAIL - 6, LANES), F32)], 0)
    rows = jnp.concatenate([rows, jnp.zeros((TAIL, block - LANES), F32)], 1)
    for share in range(out_ref.shape[0]):
        kept = parts_ref[share].astype(F32)[:TAIL]
        out_ref[share] = jnp.concatenate([kept, rows], 0).astype(BF)


def add_tail(gain_sums, parts):
    shares, rows, block = parts.shape
    last = pl.BlockSpec((shares, 2 * TAIL, block), lambda n: (0, rows // (2 * TAIL) - 1, 0))
    gain = pl.BlockSpec((8, LANES), lambda n: (0, 0))
    return pl.pallas_call(
        tail_kernel,
        grid=(1,),
        in_specs=[gain] * len(gain_sums) + [last],
        out_specs=last,
        out_shape=jax.ShapeDtypeStruct(parts.shape, BF),
        input_output_aliases={len(gain_sums): 0},
        compiler_params=PARAMS,
        cost_estimate=cost(1.5),
        name="add_tail",
    )(*gain_sums, parts)


def sum_kernel(parts_ref, out_ref, gain_q_ref, gain_k_ref):
    shares, rows, block = parts_ref.shape
    own = out_ref.shape[0]
    total = parts_ref[0].astype(F32)
    for share in range(1, shares):
        total = total + parts_ref[share].astype(F32)
    for piece in range(PIECES):
        out_ref[:, piece * block : (piece + 1) * block] = total[piece * own : (piece + 1) * own]
    tail = total[rows - TAIL :, :LANES]
    for number, gain_ref in enumerate((gain_q_ref, gain_k_ref)):
        gain = jnp.sum(tail[3 * number : 3 * number + 3], 0, keepdims=True)
        gain_ref[...] = gain[:, :HD] + gain[:, HD:]


def sum_parts(parts, own):
    block = parts.shape[2]
    gain = jax.ShapeDtypeStruct((1, HD), F32)
    return pl.pallas_call(
        sum_kernel,
        in_specs=[VMEM],
        out_specs=[VMEM] * 3,
        out_shape=[jax.ShapeDtypeStruct((own, PIECES * block), F32), gain, gain],
        compiler_params=PARAMS,
        cost_estimate=cost(2.2),
        name="sum_parts",
    )(parts)


def feature_order(inner, planes, cores, shares):
    wide = inner // planes
    features = wide // cores
    own = features // shares
    order = np.zeros((cores, features, wide), np.float32)
    for core in range(cores):
        for feature in range(features):
            share, row = divmod(feature, own)
            order[core, feature, own * (cores * share + core) + row] = 1.0
    return jnp.asarray(order, BF)


def local(
    queries,
    keys_proj,
    values_proj,
    gain_query,
    gain_key,
    frame_counts,
    heights,
    widths,
    out_weight,
    cotangent,
):
    seq = ("y", "core")
    group = ("x", "core")
    sums = ("z", "y")
    planes, cores = lax.axis_size("x"), lax.axis_size("core")
    shares = lax.axis_size("z") * lax.axis_size("y")
    inner = out_weight.shape[0]
    rank = lax.axis_index(seq).astype(jnp.int32)
    counts = jnp.stack([frame_counts[0], heights[0], widths[0], rank])
    gains = gain_query.reshape(1, HD), gain_key.reshape(1, HD)
    query_rows, key_rows, value_rows = queries[0, 0], keys_proj[0, 0], values_proj[0, 0]
    cot_rows = cotangent[0, 0]
    by_cells = (FRAMES, CELLS_HERE, inner)

    def exchange(tensor, axes):
        return lax.all_to_all(tensor, axes, split_axis=0, concat_axis=0, tiled=True)

    def after(tensor, earlier):
        return lax.optimization_barrier((tensor, earlier))[0]

    cotangents = lax.all_gather(cot_rows, group, axis=0, tiled=True)
    normed = norm(query_rows, key_rows, *gains)
    normed_cells = exchange(normed, seq)
    grad_mixed = grad_mixed_of(cot_rows, out_weight)
    outgoing, chances = space_forward(counts, normed, value_rows, grad_mixed)
    arrived = exchange(after(outgoing, normed_cells), seq)
    hats = hats_of(*lax.optimization_barrier((query_rows, key_rows, outgoing))[:2])
    arrived, *hats = lax.optimization_barrier((arrived, *hats))
    mixed_cells = time_forward(counts, normed_cells, arrived)
    mixed = exchange(mixed_cells, seq).reshape(CELLS, inner)
    late_cells, dspatial_cells, late_gains = time_back(counts, normed_cells, arrived)
    place = jnp.stack([lax.axis_index("x"), lax.axis_index("core")]).astype(jnp.int32)
    first = (cotangents, dspatial_cells)
    gathered = lax.all_gather(after(mixed, first), group, axis=0, tiled=True)
    dspatial = exchange(after(dspatial_cells, mixed), seq).reshape(CELLS, inner)
    late = exchange(after(late_cells, dspatial), seq)
    block_out = project(mixed, out_weight)
    order = feature_order(inner, planes, cores, shares)
    parts = weight_parts(place, order, gathered, cotangents, shares)
    dq, dk, grad_values, gain_sums = space_back(
        late_gains, *gains, hats[:2], normed, value_rows, dspatial, chances
    )
    for flip in range(1, cores):
        pairs = [(i, (i + flip) % cores) for i in range(cores)]
        gain_sums = gain_sums + lax.ppermute(gain_sums, "core", pairs)
    gain_sums = [gain_sums] + [
        lax.ppermute(gain_sums, "x", [(i, (i + step) % planes) for i in range(planes)])
        for step in range(1, planes)
    ]
    grad_queries, grad_keys = norm_back(hats, *gains, dq, dk, late)
    parts = exchange(after(add_tail(gain_sums, parts), late), sums)
    own = order.shape[1] // shares
    grad_weight, grad_gain_query, grad_gain_key = sum_parts(parts, own)
    return (
        block_out.reshape(cotangent.shape),
        grad_queries.reshape(queries.shape),
        grad_keys.reshape(queries.shape),
        grad_values.reshape(queries.shape),
        grad_weight,
        grad_gain_query.reshape(HD),
        grad_gain_key.reshape(HD),
    )


def solution(mesh):
    planes = 4 if mesh.shape["dp"] == 16 else mesh.shape["dp"]
    fine = Mesh(
        mesh.devices.reshape(planes, mesh.shape["dp"] // planes, -1, 2), ("x", "z", "y", "core")
    )
    tokens = P(("x", "z"), ("y", "core"), None, None)
    clips = P(("x", "z"))
    return jax.shard_map(
        local,
        mesh=fine,
        in_specs=(tokens, tokens, tokens, P(), P(), clips, clips, clips, P(), tokens),
        out_specs=(
            tokens,
            tokens,
            tokens,
            tokens,
            P(("x", "z", "y", "core"), None),
            P(),
            P(),
        ),
        check_vma=False,
    )
```

```python
import jax
import jax.numpy as jnp
import numpy as np
from jax import lax
from jax.experimental import pallas as pl
from jax.experimental.pallas import tpu as pltpu
from jax.sharding import Mesh
from jax.sharding import PartitionSpec as P

BF = jnp.bfloat16
F32 = jnp.float32
HD = 64
PW = 16
CELLS = 256
FRAMES = 8
LANES = 128
WIDE = 384
PAIRS = WIDE // LANES
CELLS_HERE = CELLS // FRAMES
BLOCK = 16
NEG = -1e30
SCALE = HD**-0.5
PARAMS = pltpu.CompilerParams(vmem_limit_bytes=24 * 1024 * 1024)


def cost(microseconds):
    return pl.CostEstimate(flops=0, bytes_accessed=int(microseconds * 3.69e6), transcendentals=0)


SMEM = pl.BlockSpec(memory_space=pltpu.SMEM)
VMEM = pl.BlockSpec(memory_space=pltpu.VMEM)


def nn(left, right):
    return jnp.dot(left, right, preferred_element_type=F32)


def nt(left, right):
    return lax.dot_general(left, right, (((1,), (1,)), ((), ())), preferred_element_type=F32)


def tn(left, right):
    return lax.dot_general(left, right, (((0,), (0,)), ((), ())), preferred_element_type=F32)


def low_lanes(shape):
    return lax.broadcasted_iota(jnp.int32, shape, len(shape) - 1) < HD


def stack_heads(pair):
    low = low_lanes((1, LANES)).astype(F32)
    return jnp.concatenate([pair * low.astype(BF), pair * (1.0 - low).astype(BF)], 0)


def pick_heads(stacked):
    half = stacked.shape[0] // 2
    return jnp.where(low_lanes((half, LANES)), stacked[:half], stacked[half:])


def softmax_rows(scores):
    grouped = scores.reshape(2, scores.shape[0] // 2, scores.shape[1])
    expo = jnp.exp(grouped - jnp.max(grouped, 1, keepdims=True))
    return expo * (1.0 / jnp.sum(expo, 1, keepdims=True))


def score_back(chances, dchances):
    grouped = dchances.reshape(chances.shape)
    total = jnp.sum(chances * grouped, 1, keepdims=True)
    return (chances * (grouped - total)).astype(BF).reshape(dchances.shape)


def cell_ok(cells, height, width):
    row = lax.shift_right_logical(cells, 4)
    return (row < height) & ((cells & (PW - 1)) < width)


def head_ones(rows, columns):
    row = lax.broadcasted_iota(jnp.int32, (rows, columns), 0) & (columns - 1)
    column = lax.broadcasted_iota(jnp.int32, (rows, columns), 1)
    same = lax.shift_right_logical(row, 6) == lax.shift_right_logical(column, 6)
    return jnp.where(same, 1.0, 0.0).astype(BF)


def head_mean(tensor, twice):
    high = tensor.astype(BF)
    rest = (tensor - high.astype(F32)).astype(BF)
    return nn(jnp.concatenate([high, rest], 1), twice) * (1.0 / HD)


def hat_of(raw, ones, twice):
    centre = raw.astype(F32) - nn(raw, ones) * (1.0 / HD)
    hats, inverses = [], []
    for left in range(0, raw.shape[1], LANES):
        part = centre[:, left : left + LANES]
        inverse = lax.rsqrt(head_mean(part * part, twice) + 1e-06)
        hats.append(part * inverse)
        inverses.append(inverse)
    return hats, inverses


def both_heads(gain_ref):
    return jnp.concatenate([gain_ref[...], gain_ref[...]], 1)


def pair_slice(number):
    return slice(number * LANES, (number + 1) * LANES)


NORM_WIDE = 512
DUO = 2 * LANES


def norm_kernel(q_ref, k_ref, gain_q_ref, gain_k_ref, out_ref):
    ones, twice = head_ones(DUO, DUO), head_ones(DUO, LANES)
    gains = both_heads(gain_q_ref), both_heads(gain_k_ref)
    for left in range(0, NORM_WIDE, DUO):
        for number, source in enumerate((q_ref, k_ref)):
            hats, _ = hat_of(source[:, left : left + DUO], ones, twice)
            for pair, hat in enumerate(hats):
                normed = (hat * gains[number]).astype(BF)
                if number == 0:
                    normed = normed * jnp.asarray(SCALE, BF)
                at = slice(left + pair * LANES, left + (pair + 1) * LANES)
                out_ref[:, number, :, at] = normed.reshape(FRAMES, CELLS_HERE, LANES)


def norm(queries, keys, gain_query, gain_key):
    inner = queries.shape[1]
    tokens = pl.BlockSpec((CELLS, NORM_WIDE), lambda n: (0, n))
    gain = pl.BlockSpec((1, HD), lambda n: (0, 0))
    return pl.pallas_call(
        norm_kernel,
        grid=(inner // NORM_WIDE,),
        in_specs=[tokens, tokens, gain, gain],
        out_specs=pl.BlockSpec((FRAMES, 2, CELLS_HERE, NORM_WIDE), lambda n: (0, 0, 0, n)),
        out_shape=jax.ShapeDtypeStruct((FRAMES, 2, CELLS_HERE, inner), BF),
        compiler_params=PARAMS,
        cost_estimate=cost(5),
        name="norm",
    )(queries, keys, gain_query, gain_key)


def hats_kernel(q_ref, k_ref, *out_refs):
    ones, twice = head_ones(DUO, DUO), head_ones(DUO, LANES)
    for left in range(0, NORM_WIDE, DUO):
        for number, source in enumerate((q_ref, k_ref)):
            hats, inverses = hat_of(source[:, left : left + DUO], ones, twice)
            at = slice(left, left + DUO)
            out_refs[number][:, at] = jnp.concatenate(hats, 1)
            out_refs[2 + number][:, at] = jnp.concatenate(inverses, 1)


def hats_of(queries, keys):
    inner = queries.shape[1]
    tokens = pl.BlockSpec((CELLS, NORM_WIDE), lambda n: (0, n))
    return pl.pallas_call(
        hats_kernel,
        grid=(inner // NORM_WIDE,),
        in_specs=[tokens, tokens],
        out_specs=[tokens] * 4,
        out_shape=[jax.ShapeDtypeStruct((CELLS, inner), F32)] * 4,
        compiler_params=PARAMS,
        cost_estimate=cost(5.6),
        name="hats",
    )(queries, keys)


def space_kernel(counts_ref, qk_ref, v_ref, gm_ref, out_ref, chances_ref):
    height, width = counts_ref[1], counts_ref[2]
    frame_on = jnp.where(counts_ref[3] < counts_ref[0], 1.0, 0.0)
    key_cell = lax.broadcasted_iota(jnp.int32, (2 * CELLS, CELLS), 0) & (CELLS - 1)
    bias = jnp.where(cell_ok(key_cell, height, width), 0.0, NEG)
    cell = lax.broadcasted_iota(jnp.int32, (CELLS, LANES), 0)
    usable = cell_ok(cell, height, width).astype(F32) * frame_on
    scores = []
    for pair in range(PAIRS):
        query = qk_ref[:, 0, :, pair_slice(pair)].reshape(CELLS, LANES)
        key = qk_ref[:, 1, :, pair_slice(pair)].reshape(CELLS, LANES)
        scores.append(nt(stack_heads(key), query) + bias)
    weights = []
    for pair in range(PAIRS):
        probs = softmax_rows(scores[pair]).reshape(scores[pair].shape)
        chances_ref[pair] = probs
        weights.append(probs.astype(BF))
    for pair in range(PAIRS):
        mixed = tn(weights[pair], stack_heads(v_ref[:, pair_slice(pair)]))
        mixed = (mixed * usable).astype(BF)
        out_ref[:, 0, :, pair_slice(pair)] = mixed.reshape(FRAMES, CELLS_HERE, LANES)
    out_ref[:, 1] = gm_ref[...].reshape(FRAMES, CELLS_HERE, WIDE)


def space_forward(counts, normed, values, grad_mixed):
    inner = values.shape[1]
    tokens = pl.BlockSpec((CELLS, WIDE), lambda n: (0, n))
    return pl.pallas_call(
        space_kernel,
        grid=(inner // WIDE,),
        in_specs=[
            SMEM,
            pl.BlockSpec((FRAMES, 2, CELLS_HERE, WIDE), lambda n: (0, 0, 0, n)),
            tokens,
            tokens,
        ],
        out_specs=[
            pl.BlockSpec((FRAMES, 2, CELLS_HERE, WIDE), lambda n: (0, 0, 0, n)),
            pl.BlockSpec((PAIRS, 2 * CELLS, CELLS), lambda n: (n, 0, 0)),
        ],
        out_shape=[
            jax.ShapeDtypeStruct((FRAMES, 2, CELLS_HERE, inner), BF),
            jax.ShapeDtypeStruct((inner // LANES, 2 * CELLS, CELLS), F32),
        ],
        compiler_params=PARAMS,
        cost_estimate=cost(7),
        name="space_forward",
    )(counts, normed, values, grad_mixed)


def gain_part(grad, normed):
    return jnp.sum(grad * normed.astype(F32), 0, keepdims=True)


def add_gains(sums_ref, of_query, of_key, begin=None):
    @pl.when(pl.program_id(0) == 0)
    def _():
        sums_ref[...] = jnp.zeros_like(sums_ref) if begin is None else begin()

    sums_ref[0:1] += of_query
    sums_ref[1:2] += of_key


def space_back_kernel(
    late_ref,
    gain_q_ref,
    gain_k_ref,
    hat_q_ref,
    hat_k_ref,
    qk_ref,
    v_ref,
    up_ref,
    chances_ref,
    dq_ref,
    dk_ref,
    dv_ref,
    sums_ref,
):
    def late_gains():
        scale = [both_heads(gain_q_ref) * SCALE, both_heads(gain_k_ref)]
        return late_ref[...] / jnp.concatenate(scale + [jnp.ones((6, LANES), F32)], 0)

    of_query = jnp.zeros((1, LANES), F32)
    of_key = jnp.zeros((1, LANES), F32)
    slices = [pair_slice(pair) for pair in range(PAIRS)]
    queries = [qk_ref[:, 0, :, at].reshape(CELLS, LANES) for at in slices]
    keys = [stack_heads(qk_ref[:, 1, :, at].reshape(CELLS, LANES)) for at in slices]
    dchances = [nt(stack_heads(v_ref[:, at]), up_ref[:, at]) for at in slices]
    dscores = []
    for pair, at in enumerate(slices):
        probs = chances_ref[pair]
        dv_ref[:, at] = pick_heads(nn(probs.astype(BF), up_ref[:, at])).astype(BF)
        dscores.append(score_back(probs.reshape(2, CELLS, CELLS), dchances[pair]))
    for pair, at in enumerate(slices):
        dk = pick_heads(nn(dscores[pair], queries[pair]))
        dq = tn(dscores[pair], keys[pair]) * SCALE
        dk_ref[:, at] = dk
        dq_ref[:, at] = dq
        of_query += gain_part(dq, hat_q_ref[:, at])
        of_key += gain_part(dk, hat_k_ref[:, at])
    add_gains(sums_ref, of_query, of_key, late_gains)


def space_back(late_sums, gain_query, gain_key, hats, normed, values, upstream, chances):
    inner = values.shape[1]
    tokens = pl.BlockSpec((CELLS, WIDE), lambda n: (0, n))
    wide = jax.ShapeDtypeStruct((CELLS, inner), F32)
    return pl.pallas_call(
        space_back_kernel,
        grid=(inner // WIDE,),
        in_specs=[
            pl.BlockSpec((8, LANES), lambda n: (0, 0)),
            pl.BlockSpec((1, HD), lambda n: (0, 0)),
            pl.BlockSpec((1, HD), lambda n: (0, 0)),
            tokens,
            tokens,
            pl.BlockSpec((FRAMES, 2, CELLS_HERE, WIDE), lambda n: (0, 0, 0, n)),
            tokens,
            tokens,
            pl.BlockSpec((PAIRS, 2 * CELLS, CELLS), lambda n: (n, 0, 0)),
        ],
        out_specs=[tokens, tokens, tokens, pl.BlockSpec((8, LANES), lambda n: (0, 0))],
        out_shape=[
            wide,
            wide,
            jax.ShapeDtypeStruct((CELLS, inner), BF),
            jax.ShapeDtypeStruct((8, LANES), F32),
        ],
        compiler_params=PARAMS,
        cost_estimate=cost(9),
        name="space_back",
    )(late_sums, gain_query, gain_key, *hats, normed, values, upstream, chances)


def time_bias(frame_total):
    key = lax.broadcasted_iota(jnp.int32, (2 * LANES, LANES), 0) & (LANES - 1)
    query = lax.broadcasted_iota(jnp.int32, (2 * LANES, LANES), 1)
    same = (key & (BLOCK - 1)) == (query & (BLOCK - 1))
    return jnp.where(same & (lax.shift_right_logical(key, 4) < frame_total), 0.0, NEG)


def time_usable(counts_ref, block):
    row = lax.broadcasted_iota(jnp.int32, (LANES, LANES), 0)
    cell = counts_ref[3] * CELLS_HERE + block * BLOCK + (row & (BLOCK - 1))
    on = cell_ok(cell, counts_ref[1], counts_ref[2])
    return (on & (lax.shift_right_logical(row, 4) < counts_ref[0])).astype(F32)


def time_blocks():
    for block in range(CELLS_HERE // BLOCK):
        for pair in range(PAIRS):
            yield block, slice(block * BLOCK, (block + 1) * BLOCK), pair_slice(pair)


def time_kernel(counts_ref, qk_ref, sg_ref, out_ref):
    bias = time_bias(counts_ref[0])
    usable = [time_usable(counts_ref, block) for block in range(CELLS_HERE // BLOCK)]
    scores = []
    for block, rows, at in time_blocks():
        query = qk_ref[:, 0, rows, at].reshape(LANES, LANES)
        keys = stack_heads(qk_ref[:, 1, rows, at].reshape(LANES, LANES))
        scores.append(nt(keys, query) + bias)
    weights = [softmax_rows(part).astype(BF).reshape(part.shape) for part in scores]
    for number, (block, rows, at) in enumerate(time_blocks()):
        values = stack_heads(sg_ref[:, 0, rows, at].reshape(LANES, LANES))
        mixed = tn(weights[number], values) * usable[block]
        out_ref[:, rows, at] = mixed.astype(BF).reshape(FRAMES, BLOCK, LANES)


def time_back_kernel(counts_ref, qk_ref, sg_ref, dqk_ref, ds_ref, sums_ref):
    bias = time_bias(counts_ref[0])
    of_query = jnp.zeros((1, LANES), F32)
    of_key = jnp.zeros((1, LANES), F32)
    usable = [time_usable(counts_ref, block) for block in range(CELLS_HERE // BLOCK)]
    blocks = list(time_blocks())

    def load(ref, number, rows, at):
        return ref[:, number, rows, at].reshape(LANES, LANES)

    def shaped(tensor):
        return tensor.astype(BF).reshape(FRAMES, BLOCK, LANES)

    queries = [load(qk_ref, 0, rows, at) for _, rows, at in blocks]
    singles = [load(qk_ref, 1, rows, at) for _, rows, at in blocks]
    keys = [stack_heads(key) for key in singles]
    upstreams = [
        (load(sg_ref, 1, rows, at).astype(F32) * usable[block]).astype(BF)
        for block, rows, at in blocks
    ]
    scores = [nt(key, query) + bias for key, query in zip(keys, queries)]
    dchances = [
        nt(stack_heads(load(sg_ref, 0, rows, at)), upstream)
        for (_, rows, at), upstream in zip(blocks, upstreams)
    ]
    chances = [softmax_rows(part) for part in scores]
    dscores = [score_back(probs, part) for probs, part in zip(chances, dchances)]
    for number, (_, rows, at) in enumerate(blocks):
        weights = chances[number].astype(BF).reshape(2 * LANES, LANES)
        ds_ref[:, rows, at] = shaped(pick_heads(nn(weights, upstreams[number])))
        dq = tn(dscores[number], keys[number]) * SCALE
        dk = pick_heads(nn(dscores[number], queries[number]))
        dqk_ref[:, 0, rows, at] = shaped(dq)
        dqk_ref[:, 1, rows, at] = shaped(dk)
        of_query += gain_part(dq, queries[number])
        of_key += gain_part(dk, singles[number])
    add_gains(sums_ref, of_query, of_key)


def time_specs(inner):
    double = pl.BlockSpec((FRAMES, 2, CELLS_HERE, WIDE), lambda n: (0, 0, 0, n))
    single = pl.BlockSpec((FRAMES, CELLS_HERE, WIDE), lambda n: (0, 0, n))
    return (
        double,
        single,
        jax.ShapeDtypeStruct((FRAMES, 2, CELLS_HERE, inner), BF),
        jax.ShapeDtypeStruct((FRAMES, CELLS_HERE, inner), BF),
    )


def time_forward(counts, normed, arrived):
    inner = arrived.shape[3]
    double, single, _, single_shape = time_specs(inner)
    return pl.pallas_call(
        time_kernel,
        grid=(inner // WIDE,),
        in_specs=[SMEM, double, double],
        out_specs=single,
        out_shape=single_shape,
        compiler_params=PARAMS,
        cost_estimate=cost(5),
        name="time_forward",
    )(counts, normed, arrived)


def time_back(counts, normed, arrived):
    inner = arrived.shape[3]
    double, single, double_shape, single_shape = time_specs(inner)
    return pl.pallas_call(
        time_back_kernel,
        grid=(inner // WIDE,),
        in_specs=[SMEM, double, double],
        out_specs=[double, single, pl.BlockSpec((8, LANES), lambda n: (0, 0))],
        out_shape=[double_shape, single_shape, jax.ShapeDtypeStruct((8, LANES), F32)],
        compiler_params=PARAMS,
        cost_estimate=cost(6.5),
        name="time_back",
    )(counts, normed, arrived)


def norm_back_kernel(
    hat_q_ref,
    hat_k_ref,
    inverse_q_ref,
    inverse_k_ref,
    gain_q_ref,
    gain_k_ref,
    dq_ref,
    dk_ref,
    late_ref,
    gq_ref,
    gk_ref,
):
    twice = head_ones(DUO, LANES)
    for left in range(0, NORM_WIDE, LANES):
        at = slice(left, left + LANES)
        for number, (hat_ref, inverse_ref, gain_ref, early, target) in enumerate(
            (
                (hat_q_ref, inverse_q_ref, gain_q_ref, dq_ref, gq_ref),
                (hat_k_ref, inverse_k_ref, gain_k_ref, dk_ref, gk_ref),
            )
        ):
            hat = hat_ref[:, at]
            late = late_ref[:, number, :, at].reshape(CELLS, LANES)
            scaled = (early[:, at] + late.astype(F32)) * both_heads(gain_ref)
            mean = head_mean(scaled, twice)
            dinput = scaled - mean - hat * head_mean(scaled * hat, twice)
            target[:, at] = (inverse_ref[:, at] * dinput).astype(BF)


def norm_back(hats, gain_query, gain_key, dq, dk, late):
    inner = dq.shape[1]
    tokens = pl.BlockSpec((CELLS, NORM_WIDE), lambda n: (0, n))
    gain = pl.BlockSpec((1, HD), lambda n: (0, 0))
    grads = jax.ShapeDtypeStruct((CELLS, inner), BF)
    return pl.pallas_call(
        norm_back_kernel,
        grid=(inner // NORM_WIDE,),
        in_specs=[
            tokens,
            tokens,
            tokens,
            tokens,
            gain,
            gain,
            tokens,
            tokens,
            pl.BlockSpec((FRAMES, 2, CELLS_HERE, NORM_WIDE), lambda n: (0, 0, 0, n)),
        ],
        out_specs=[tokens, tokens],
        out_shape=[grads, grads],
        compiler_params=PARAMS,
        cost_estimate=cost(7),
        name="norm_back",
    )(*hats, gain_query, gain_key, dq, dk, late)


def grad_mixed_kernel(cot_ref, weight_ref, out_ref):
    out_ref[...] = nt(cot_ref[...], weight_ref[...]).astype(BF)


def grad_mixed_of(cotangent, weight):
    inner, width = weight.shape
    return pl.pallas_call(
        grad_mixed_kernel,
        grid=(inner // WIDE,),
        in_specs=[
            pl.BlockSpec((CELLS, width), lambda n: (0, 0)),
            pl.BlockSpec((WIDE, width), lambda n: (n, 0)),
        ],
        out_specs=pl.BlockSpec((CELLS, WIDE), lambda n: (0, n)),
        out_shape=jax.ShapeDtypeStruct((CELLS, inner), BF),
        compiler_params=PARAMS,
        cost_estimate=cost(8.7),
        name="grad_mixed",
    )(cotangent, weight)


def project_kernel(mixed_ref, weight_ref, out_ref):
    out_ref[...] = nn(mixed_ref[...], weight_ref[...]).astype(BF)


def project(mixed, weight):
    inner, width = weight.shape
    block = width // 4
    return pl.pallas_call(
        project_kernel,
        grid=(4,),
        in_specs=[
            pl.BlockSpec((CELLS, inner), lambda n: (0, 0)),
            pl.BlockSpec((inner, block), lambda n: (0, n)),
        ],
        out_specs=pl.BlockSpec((CELLS, block), lambda n: (0, n)),
        out_shape=jax.ShapeDtypeStruct((CELLS, width), BF),
        compiler_params=PARAMS,
        cost_estimate=cost(7),
        name="project",
    )(mixed, weight)


PIECES = 6
STEPS = 3
TAIL = 8


def gain_rows(gain_refs, block):
    total = gain_refs[0][...]
    for gain_ref in gain_refs[1:]:
        total = total + gain_ref[...]
    terms = []
    for row in range(2):
        rest = total[row : row + 1]
        for _ in range(3):
            terms.append(rest.astype(BF).astype(F32))
            rest = rest - terms[-1]
    rows = jnp.concatenate(terms + [jnp.zeros((TAIL - 6, LANES), F32)], 0)
    return jnp.concatenate([rows, jnp.zeros((TAIL, block - LANES), F32)], 1).astype(BF)


def weight_kernel(place_ref, order_ref, mixed_ref, cot_ref, *refs):
    *gain_refs, out_ref, turned, product = refs
    shares, rows, block = out_ref.shape
    own = product.shape[0] // shares

    @pl.when(pl.program_id(0) == 0)
    def _():
        turned[...] = nt(order_ref[0], mixed_ref[...]).astype(BF)
        tail = gain_rows(gain_refs, block)
        for share in range(shares):
            out_ref[share, rows - TAIL :] = tail

    product[...] = nn(turned[...], cot_ref[...])
    for step in range(STEPS):

        @pl.when(pl.program_id(0) == step)
        def _():
            for share in range(shares):
                for half in range(PIECES // STEPS):
                    top = (step * (PIECES // STEPS) + half) * own
                    out_ref[share, top : top + own] = product[
                        share * own : (share + 1) * own, half * block : (half + 1) * block
                    ].astype(BF)


def weight_parts(place, order, mixed, cotangents, gain_sums, shares):
    tokens, width = cotangents.shape
    _, features, wide = order.shape
    block = width // PIECES
    columns = width // STEPS
    rows = -(-(PIECES * (features // shares) + TAIL) // 16) * 16
    gain = pl.BlockSpec((8, LANES), lambda n, place: (0, 0))
    return pl.pallas_call(
        weight_kernel,
        grid_spec=pltpu.PrefetchScalarGridSpec(
            num_scalar_prefetch=1,
            grid=(STEPS,),
            in_specs=[
                pl.BlockSpec((1, features, wide), lambda n, place: (place[1], 0, 0)),
                pl.BlockSpec((tokens, wide), lambda n, place: (0, place[0])),
                pl.BlockSpec((tokens, columns), lambda n, place: (0, n)),
            ]
            + [gain] * len(gain_sums),
            out_specs=pl.BlockSpec((shares, rows, block), lambda n, place: (0, 0, 0)),
            scratch_shapes=[
                pltpu.VMEM((features, tokens), BF),
                pltpu.VMEM((features, columns), F32),
            ],
        ),
        out_shape=jax.ShapeDtypeStruct((shares, rows, block), BF),
        compiler_params=PARAMS,
        cost_estimate=cost(9.5),
        name="weight_parts",
    )(place, order, mixed, cotangents, *gain_sums)


def sum_kernel(parts_ref, out_ref, gain_q_ref, gain_k_ref):
    shares, rows, block = parts_ref.shape
    own = out_ref.shape[0]
    total = parts_ref[0].astype(F32)
    for share in range(1, shares):
        total = total + parts_ref[share].astype(F32)
    for piece in range(PIECES):
        out_ref[:, piece * block : (piece + 1) * block] = total[piece * own : (piece + 1) * own]
    tail = total[rows - TAIL :, :LANES]
    for number, gain_ref in enumerate((gain_q_ref, gain_k_ref)):
        gain = jnp.sum(tail[3 * number : 3 * number + 3], 0, keepdims=True)
        gain_ref[...] = gain[:, :HD] + gain[:, HD:]


def sum_parts(parts, own):
    block = parts.shape[2]
    gain = jax.ShapeDtypeStruct((1, HD), F32)
    return pl.pallas_call(
        sum_kernel,
        in_specs=[VMEM],
        out_specs=[VMEM] * 3,
        out_shape=[jax.ShapeDtypeStruct((own, PIECES * block), F32), gain, gain],
        compiler_params=PARAMS,
        cost_estimate=cost(2.2),
        name="sum_parts",
    )(parts)


def feature_order(inner, planes, cores, shares):
    wide = inner // planes
    features = wide // cores
    own = features // shares
    order = np.zeros((cores, features, wide), np.float32)
    for core in range(cores):
        for feature in range(features):
            share, row = divmod(feature, own)
            order[core, feature, own * (cores * share + core) + row] = 1.0
    return jnp.asarray(order, BF)


def local(
    queries,
    keys_proj,
    values_proj,
    gain_query,
    gain_key,
    frame_counts,
    heights,
    widths,
    out_weight,
    cotangent,
):
    seq = ("y", "core")
    group = ("x", "core")
    sums = ("z", "y")
    planes, cores = lax.axis_size("x"), lax.axis_size("core")
    shares = lax.axis_size("z") * lax.axis_size("y")
    inner = out_weight.shape[0]
    rank = lax.axis_index(seq).astype(jnp.int32)
    counts = jnp.stack([frame_counts[0], heights[0], widths[0], rank])
    gains = gain_query.reshape(1, HD), gain_key.reshape(1, HD)
    query_rows, key_rows, value_rows = queries[0, 0], keys_proj[0, 0], values_proj[0, 0]
    cot_rows = cotangent[0, 0]
    by_cells = (FRAMES, CELLS_HERE, inner)

    def exchange(tensor, axes):
        return lax.all_to_all(tensor, axes, split_axis=0, concat_axis=0, tiled=True)

    def after(tensor, earlier):
        return lax.optimization_barrier((tensor, earlier))[0]

    cotangents = lax.all_gather(cot_rows, group, axis=0, tiled=True)
    normed = norm(query_rows, key_rows, *gains)
    normed_cells = exchange(normed, seq)
    grad_mixed = grad_mixed_of(cot_rows, out_weight)
    outgoing, chances = space_forward(counts, normed, value_rows, grad_mixed)
    arrived = exchange(after(outgoing, normed_cells), seq)
    hats = hats_of(*lax.optimization_barrier((query_rows, key_rows, outgoing))[:2])
    arrived, *hats = lax.optimization_barrier((arrived, *hats))
    mixed_cells = time_forward(counts, normed_cells, arrived)
    mixed = exchange(mixed_cells, seq).reshape(CELLS, inner)
    late_cells, dspatial_cells, late_gains = time_back(counts, normed_cells, arrived)
    place = jnp.stack([lax.axis_index("x"), lax.axis_index("core")]).astype(jnp.int32)
    first = (cotangents, dspatial_cells)
    gathered = lax.all_gather(after(mixed, first), group, axis=0, tiled=True)
    dspatial = exchange(after(dspatial_cells, mixed), seq).reshape(CELLS, inner)
    late = exchange(after(late_cells, dspatial), seq)
    block_out = project(mixed, out_weight)
    dq, dk, grad_values, gain_sums = space_back(
        late_gains, *gains, hats[:2], normed, value_rows, dspatial, chances
    )
    for flip in range(1, cores):
        pairs = [(i, (i + flip) % cores) for i in range(cores)]
        gain_sums = gain_sums + lax.ppermute(gain_sums, "core", pairs)
    gain_sums = [gain_sums] + [
        lax.ppermute(gain_sums, "x", [(i, (i + step) % planes) for i in range(planes)])
        for step in range(1, planes)
    ]
    grad_queries, grad_keys = norm_back(hats, *gains, dq, dk, late)
    order = feature_order(inner, planes, cores, shares)
    parts = weight_parts(place, order, gathered, cotangents, gain_sums, shares)
    parts = exchange(after(parts, late), sums)
    own = order.shape[1] // shares
    grad_weight, grad_gain_query, grad_gain_key = sum_parts(parts, own)
    return (
        block_out.reshape(cotangent.shape),
        grad_queries.reshape(queries.shape),
        grad_keys.reshape(queries.shape),
        grad_values.reshape(queries.shape),
        grad_weight,
        grad_gain_query.reshape(HD),
        grad_gain_key.reshape(HD),
    )


def solution(mesh):
    planes = 4 if mesh.shape["dp"] == 16 else mesh.shape["dp"]
    fine = Mesh(
        mesh.devices.reshape(planes, mesh.shape["dp"] // planes, -1, 2), ("x", "z", "y", "core")
    )
    tokens = P(("x", "z"), ("y", "core"), None, None)
    clips = P(("x", "z"))
    return jax.shard_map(
        local,
        mesh=fine,
        in_specs=(tokens, tokens, tokens, P(), P(), clips, clips, clips, P(), tokens),
        out_specs=(
            tokens,
            tokens,
            tokens,
            tokens,
            P(("x", "z", "y", "core"), None),
            P(),
            P(),
        ),
        check_vma=False,
    )
```

```python
import jax
import jax.numpy as jnp
import numpy as np
from jax import lax
from jax.experimental import pallas as pl
from jax.experimental.pallas import tpu as pltpu
from jax.sharding import Mesh
from jax.sharding import PartitionSpec as P

BF = jnp.bfloat16
F32 = jnp.float32
HD = 64
PW = 16
CELLS = 256
FRAMES = 8
LANES = 128
WIDE = 384
PAIRS = WIDE // LANES
CELLS_HERE = CELLS // FRAMES
BLOCK = 16
NEG = -1e30
SCALE = HD**-0.5
PARAMS = pltpu.CompilerParams(vmem_limit_bytes=56 * 1024 * 1024)
SMALL = pltpu.CompilerParams(vmem_limit_bytes=16 * 1024 * 1024)


def cost(microseconds):
    return pl.CostEstimate(flops=0, bytes_accessed=int(microseconds * 3.69e6), transcendentals=0)


SMEM = pl.BlockSpec(memory_space=pltpu.SMEM)
VMEM = pl.BlockSpec(memory_space=pltpu.VMEM)


def nn(left, right):
    return jnp.dot(left, right, preferred_element_type=F32)


def nt(left, right):
    return lax.dot_general(left, right, (((1,), (1,)), ((), ())), preferred_element_type=F32)


def tn(left, right):
    return lax.dot_general(left, right, (((0,), (0,)), ((), ())), preferred_element_type=F32)


def low_lanes(shape):
    return lax.broadcasted_iota(jnp.int32, shape, len(shape) - 1) < HD


def stack_heads(pair):
    low = low_lanes((1, LANES)).astype(F32)
    return jnp.concatenate([pair * low.astype(BF), pair * (1.0 - low).astype(BF)], 0)


def pick_heads(stacked):
    half = stacked.shape[0] // 2
    return jnp.where(low_lanes((half, LANES)), stacked[:half], stacked[half:])


def softmax_rows(scores):
    grouped = scores.reshape(2, scores.shape[0] // 2, scores.shape[1])
    expo = jnp.exp(grouped - jnp.max(grouped, 1, keepdims=True))
    return expo * (1.0 / jnp.sum(expo, 1, keepdims=True))


def score_back(chances, dchances):
    grouped = dchances.reshape(chances.shape)
    total = jnp.sum(chances * grouped, 1, keepdims=True)
    return (chances * (grouped - total)).astype(BF).reshape(dchances.shape)


def cell_ok(cells, height, width):
    row = lax.shift_right_logical(cells, 4)
    return (row < height) & ((cells & (PW - 1)) < width)


def head_ones(rows, columns):
    row = lax.broadcasted_iota(jnp.int32, (rows, columns), 0) & (columns - 1)
    column = lax.broadcasted_iota(jnp.int32, (rows, columns), 1)
    same = lax.shift_right_logical(row, 6) == lax.shift_right_logical(column, 6)
    return jnp.where(same, 1.0, 0.0).astype(BF)


def head_mean(tensor, twice):
    high = tensor.astype(BF)
    rest = (tensor - high.astype(F32)).astype(BF)
    return nn(jnp.concatenate([high, rest], 1), twice) * (1.0 / HD)


def hat_of(raw, ones, twice):
    centre = raw.astype(F32) - nn(raw, ones) * (1.0 / HD)
    hats, inverses = [], []
    for left in range(0, raw.shape[1], LANES):
        part = centre[:, left : left + LANES]
        inverse = lax.rsqrt(head_mean(part * part, twice) + 1e-06)
        hats.append(part * inverse)
        inverses.append(inverse)
    return hats, inverses


def both_heads(gain_ref):
    return jnp.concatenate([gain_ref[...], gain_ref[...]], 1)


def pair_slice(number):
    return slice(number * LANES, (number + 1) * LANES)


NORM_WIDE = 512
DUO = 2 * LANES


def norm_kernel(q_ref, k_ref, gain_q_ref, gain_k_ref, out_ref):
    ones, twice = head_ones(DUO, DUO), head_ones(DUO, LANES)
    gains = both_heads(gain_q_ref), both_heads(gain_k_ref)
    for left in range(0, NORM_WIDE, DUO):
        for number, source in enumerate((q_ref, k_ref)):
            hats, _ = hat_of(source[:, left : left + DUO], ones, twice)
            for pair, hat in enumerate(hats):
                normed = (hat * gains[number]).astype(BF)
                if number == 0:
                    normed = normed * jnp.asarray(SCALE, BF)
                at = slice(left + pair * LANES, left + (pair + 1) * LANES)
                out_ref[:, number, :, at] = normed.reshape(FRAMES, CELLS_HERE, LANES)


def norm(queries, keys, gain_query, gain_key):
    inner = queries.shape[1]
    tokens = pl.BlockSpec((CELLS, NORM_WIDE), lambda n: (0, n))
    gain = pl.BlockSpec((1, HD), lambda n: (0, 0))
    return pl.pallas_call(
        norm_kernel,
        grid=(inner // NORM_WIDE,),
        in_specs=[tokens, tokens, gain, gain],
        out_specs=pl.BlockSpec((FRAMES, 2, CELLS_HERE, NORM_WIDE), lambda n: (0, 0, 0, n)),
        out_shape=jax.ShapeDtypeStruct((FRAMES, 2, CELLS_HERE, inner), BF),
        compiler_params=PARAMS,
        cost_estimate=cost(5),
        name="norm",
    )(queries, keys, gain_query, gain_key)


def hats_kernel(q_ref, k_ref, *out_refs):
    ones, twice = head_ones(DUO, DUO), head_ones(DUO, LANES)
    for left in range(0, NORM_WIDE, DUO):
        for number, source in enumerate((q_ref, k_ref)):
            hats, inverses = hat_of(source[:, left : left + DUO], ones, twice)
            at = slice(left, left + DUO)
            out_refs[number][:, at] = jnp.concatenate(hats, 1)
            out_refs[2 + number][:, at] = jnp.concatenate(inverses, 1)


def hats_of(queries, keys):
    inner = queries.shape[1]
    tokens = pl.BlockSpec((CELLS, NORM_WIDE), lambda n: (0, n))
    return pl.pallas_call(
        hats_kernel,
        grid=(inner // NORM_WIDE,),
        in_specs=[tokens, tokens],
        out_specs=[tokens] * 4,
        out_shape=[jax.ShapeDtypeStruct((CELLS, inner), F32)] * 4,
        compiler_params=PARAMS,
        cost_estimate=cost(5.6),
        name="hats",
    )(queries, keys)


def space_kernel(counts_ref, qk_ref, v_ref, gm_ref, out_ref, chances_ref):
    height, width = counts_ref[1], counts_ref[2]
    frame_on = jnp.where(counts_ref[3] < counts_ref[0], 1.0, 0.0)
    key_cell = lax.broadcasted_iota(jnp.int32, (2 * CELLS, CELLS), 0) & (CELLS - 1)
    bias = jnp.where(cell_ok(key_cell, height, width), 0.0, NEG)
    cell = lax.broadcasted_iota(jnp.int32, (CELLS, LANES), 0)
    usable = cell_ok(cell, height, width).astype(F32) * frame_on
    scores = []
    for pair in range(PAIRS):
        query = qk_ref[:, 0, :, pair_slice(pair)].reshape(CELLS, LANES)
        key = qk_ref[:, 1, :, pair_slice(pair)].reshape(CELLS, LANES)
        scores.append(nt(stack_heads(key), query) + bias)
    weights = []
    for pair in range(PAIRS):
        probs = softmax_rows(scores[pair]).reshape(scores[pair].shape)
        chances_ref[pair] = probs
        weights.append(probs.astype(BF))
    for pair in range(PAIRS):
        mixed = tn(weights[pair], stack_heads(v_ref[:, pair_slice(pair)]))
        mixed = (mixed * usable).astype(BF)
        out_ref[:, 0, :, pair_slice(pair)] = mixed.reshape(FRAMES, CELLS_HERE, LANES)
    out_ref[:, 1] = gm_ref[...].reshape(FRAMES, CELLS_HERE, WIDE)


def space_forward(counts, normed, values, grad_mixed):
    inner = values.shape[1]
    tokens = pl.BlockSpec((CELLS, WIDE), lambda n: (0, n))
    return pl.pallas_call(
        space_kernel,
        grid=(inner // WIDE,),
        in_specs=[
            SMEM,
            pl.BlockSpec((FRAMES, 2, CELLS_HERE, WIDE), lambda n: (0, 0, 0, n)),
            tokens,
            tokens,
        ],
        out_specs=[
            pl.BlockSpec((FRAMES, 2, CELLS_HERE, WIDE), lambda n: (0, 0, 0, n)),
            pl.BlockSpec((PAIRS, 2 * CELLS, CELLS), lambda n: (n, 0, 0)),
        ],
        out_shape=[
            jax.ShapeDtypeStruct((FRAMES, 2, CELLS_HERE, inner), BF),
            jax.ShapeDtypeStruct((inner // LANES, 2 * CELLS, CELLS), F32),
        ],
        compiler_params=PARAMS,
        cost_estimate=cost(7),
        name="space_forward",
    )(counts, normed, values, grad_mixed)


def gain_part(grad, normed):
    return jnp.sum(grad * normed.astype(F32), 0, keepdims=True)


def add_gains(sums_ref, of_query, of_key, begin=None):
    @pl.when(pl.program_id(0) == 0)
    def _():
        sums_ref[...] = jnp.zeros_like(sums_ref) if begin is None else begin()

    sums_ref[0:1] += of_query
    sums_ref[1:2] += of_key


def space_back_kernel(
    late_ref,
    gain_q_ref,
    gain_k_ref,
    hat_q_ref,
    hat_k_ref,
    qk_ref,
    v_ref,
    up_ref,
    chances_ref,
    dq_ref,
    dk_ref,
    dv_ref,
    sums_ref,
):
    def late_gains():
        scale = [both_heads(gain_q_ref) * SCALE, both_heads(gain_k_ref)]
        return late_ref[...] / jnp.concatenate(scale + [jnp.ones((6, LANES), F32)], 0)

    of_query = jnp.zeros((1, LANES), F32)
    of_key = jnp.zeros((1, LANES), F32)
    slices = [pair_slice(pair) for pair in range(PAIRS)]
    queries = [qk_ref[:, 0, :, at].reshape(CELLS, LANES) for at in slices]
    keys = [stack_heads(qk_ref[:, 1, :, at].reshape(CELLS, LANES)) for at in slices]
    dchances = [nt(stack_heads(v_ref[:, at]), up_ref[:, at]) for at in slices]
    dscores = []
    for pair, at in enumerate(slices):
        probs = chances_ref[pair]
        dv_ref[:, at] = pick_heads(nn(probs.astype(BF), up_ref[:, at])).astype(BF)
        dscores.append(score_back(probs.reshape(2, CELLS, CELLS), dchances[pair]))
    for pair, at in enumerate(slices):
        dk = pick_heads(nn(dscores[pair], queries[pair]))
        dq = tn(dscores[pair], keys[pair]) * SCALE
        dk_ref[:, at] = dk
        dq_ref[:, at] = dq
        of_query += gain_part(dq, hat_q_ref[:, at])
        of_key += gain_part(dk, hat_k_ref[:, at])
    add_gains(sums_ref, of_query, of_key, late_gains)


def space_back(late_sums, gain_query, gain_key, hats, normed, values, upstream, chances):
    inner = values.shape[1]
    tokens = pl.BlockSpec((CELLS, WIDE), lambda n: (0, n))
    wide = jax.ShapeDtypeStruct((CELLS, inner), F32)
    return pl.pallas_call(
        space_back_kernel,
        grid=(inner // WIDE,),
        in_specs=[
            pl.BlockSpec((8, LANES), lambda n: (0, 0)),
            pl.BlockSpec((1, HD), lambda n: (0, 0)),
            pl.BlockSpec((1, HD), lambda n: (0, 0)),
            tokens,
            tokens,
            pl.BlockSpec((FRAMES, 2, CELLS_HERE, WIDE), lambda n: (0, 0, 0, n)),
            tokens,
            tokens,
            pl.BlockSpec((PAIRS, 2 * CELLS, CELLS), lambda n: (n, 0, 0)),
        ],
        out_specs=[tokens, tokens, tokens, pl.BlockSpec((8, LANES), lambda n: (0, 0))],
        out_shape=[
            wide,
            wide,
            jax.ShapeDtypeStruct((CELLS, inner), BF),
            jax.ShapeDtypeStruct((8, LANES), F32),
        ],
        compiler_params=PARAMS,
        cost_estimate=cost(9),
        name="space_back",
    )(late_sums, gain_query, gain_key, *hats, normed, values, upstream, chances)


def time_bias(frame_total):
    key = lax.broadcasted_iota(jnp.int32, (2 * LANES, LANES), 0) & (LANES - 1)
    query = lax.broadcasted_iota(jnp.int32, (2 * LANES, LANES), 1)
    same = (key & (BLOCK - 1)) == (query & (BLOCK - 1))
    return jnp.where(same & (lax.shift_right_logical(key, 4) < frame_total), 0.0, NEG)


def time_usable(counts_ref, block):
    row = lax.broadcasted_iota(jnp.int32, (LANES, LANES), 0)
    cell = counts_ref[3] * CELLS_HERE + block * BLOCK + (row & (BLOCK - 1))
    on = cell_ok(cell, counts_ref[1], counts_ref[2])
    return (on & (lax.shift_right_logical(row, 4) < counts_ref[0])).astype(F32)


def time_blocks():
    for block in range(CELLS_HERE // BLOCK):
        for pair in range(PAIRS):
            yield block, slice(block * BLOCK, (block + 1) * BLOCK), pair_slice(pair)


def time_kernel(counts_ref, qk_ref, sg_ref, out_ref):
    bias = time_bias(counts_ref[0])
    usable = [time_usable(counts_ref, block) for block in range(CELLS_HERE // BLOCK)]
    scores = []
    for block, rows, at in time_blocks():
        query = qk_ref[:, 0, rows, at].reshape(LANES, LANES)
        keys = stack_heads(qk_ref[:, 1, rows, at].reshape(LANES, LANES))
        scores.append(nt(keys, query) + bias)
    weights = [softmax_rows(part).astype(BF).reshape(part.shape) for part in scores]
    for number, (block, rows, at) in enumerate(time_blocks()):
        values = stack_heads(sg_ref[:, 0, rows, at].reshape(LANES, LANES))
        mixed = tn(weights[number], values) * usable[block]
        out_ref[:, rows, at] = mixed.astype(BF).reshape(FRAMES, BLOCK, LANES)


def time_back_kernel(counts_ref, qk_ref, sg_ref, dqk_ref, ds_ref, sums_ref):
    bias = time_bias(counts_ref[0])
    of_query = jnp.zeros((1, LANES), F32)
    of_key = jnp.zeros((1, LANES), F32)
    usable = [time_usable(counts_ref, block) for block in range(CELLS_HERE // BLOCK)]
    blocks = list(time_blocks())

    def load(ref, number, rows, at):
        return ref[:, number, rows, at].reshape(LANES, LANES)

    def shaped(tensor):
        return tensor.astype(BF).reshape(FRAMES, BLOCK, LANES)

    queries = [load(qk_ref, 0, rows, at) for _, rows, at in blocks]
    singles = [load(qk_ref, 1, rows, at) for _, rows, at in blocks]
    keys = [stack_heads(key) for key in singles]
    upstreams = [
        (load(sg_ref, 1, rows, at).astype(F32) * usable[block]).astype(BF)
        for block, rows, at in blocks
    ]
    scores = [nt(key, query) + bias for key, query in zip(keys, queries)]
    dchances = [
        nt(stack_heads(load(sg_ref, 0, rows, at)), upstream)
        for (_, rows, at), upstream in zip(blocks, upstreams)
    ]
    chances = [softmax_rows(part) for part in scores]
    dscores = [score_back(probs, part) for probs, part in zip(chances, dchances)]
    for number, (_, rows, at) in enumerate(blocks):
        weights = chances[number].astype(BF).reshape(2 * LANES, LANES)
        ds_ref[:, rows, at] = shaped(pick_heads(nn(weights, upstreams[number])))
        dq = tn(dscores[number], keys[number]) * SCALE
        dk = pick_heads(nn(dscores[number], queries[number]))
        dqk_ref[:, 0, rows, at] = shaped(dq)
        dqk_ref[:, 1, rows, at] = shaped(dk)
        of_query += gain_part(dq, queries[number])
        of_key += gain_part(dk, singles[number])
    add_gains(sums_ref, of_query, of_key)


def time_specs(inner):
    double = pl.BlockSpec((FRAMES, 2, CELLS_HERE, WIDE), lambda n: (0, 0, 0, n))
    single = pl.BlockSpec((FRAMES, CELLS_HERE, WIDE), lambda n: (0, 0, n))
    return (
        double,
        single,
        jax.ShapeDtypeStruct((FRAMES, 2, CELLS_HERE, inner), BF),
        jax.ShapeDtypeStruct((FRAMES, CELLS_HERE, inner), BF),
    )


def time_forward(counts, normed, arrived):
    inner = arrived.shape[3]
    double, single, _, single_shape = time_specs(inner)
    return pl.pallas_call(
        time_kernel,
        grid=(inner // WIDE,),
        in_specs=[SMEM, double, double],
        out_specs=single,
        out_shape=single_shape,
        compiler_params=SMALL,
        cost_estimate=cost(5),
        name="time_forward",
    )(counts, normed, arrived)


def time_back(counts, normed, arrived):
    inner = arrived.shape[3]
    double, single, double_shape, single_shape = time_specs(inner)
    return pl.pallas_call(
        time_back_kernel,
        grid=(inner // WIDE,),
        in_specs=[SMEM, double, double],
        out_specs=[double, single, pl.BlockSpec((8, LANES), lambda n: (0, 0))],
        out_shape=[double_shape, single_shape, jax.ShapeDtypeStruct((8, LANES), F32)],
        compiler_params=SMALL,
        cost_estimate=cost(6.5),
        name="time_back",
    )(counts, normed, arrived)


def norm_back_kernel(
    hat_q_ref,
    hat_k_ref,
    inverse_q_ref,
    inverse_k_ref,
    gain_q_ref,
    gain_k_ref,
    dq_ref,
    dk_ref,
    late_ref,
    gq_ref,
    gk_ref,
):
    twice = head_ones(DUO, LANES)
    for left in range(0, NORM_WIDE, LANES):
        at = slice(left, left + LANES)
        for number, (hat_ref, inverse_ref, gain_ref, early, target) in enumerate(
            (
                (hat_q_ref, inverse_q_ref, gain_q_ref, dq_ref, gq_ref),
                (hat_k_ref, inverse_k_ref, gain_k_ref, dk_ref, gk_ref),
            )
        ):
            hat = hat_ref[:, at]
            late = late_ref[:, number, :, at].reshape(CELLS, LANES)
            scaled = (early[:, at] + late.astype(F32)) * both_heads(gain_ref)
            mean = head_mean(scaled, twice)
            dinput = scaled - mean - hat * head_mean(scaled * hat, twice)
            target[:, at] = (inverse_ref[:, at] * dinput).astype(BF)


def norm_back(hats, gain_query, gain_key, dq, dk, late):
    inner = dq.shape[1]
    tokens = pl.BlockSpec((CELLS, NORM_WIDE), lambda n: (0, n))
    gain = pl.BlockSpec((1, HD), lambda n: (0, 0))
    grads = jax.ShapeDtypeStruct((CELLS, inner), BF)
    return pl.pallas_call(
        norm_back_kernel,
        grid=(inner // NORM_WIDE,),
        in_specs=[
            tokens,
            tokens,
            tokens,
            tokens,
            gain,
            gain,
            tokens,
            tokens,
            pl.BlockSpec((FRAMES, 2, CELLS_HERE, NORM_WIDE), lambda n: (0, 0, 0, n)),
        ],
        out_specs=[tokens, tokens],
        out_shape=[grads, grads],
        compiler_params=PARAMS,
        cost_estimate=cost(7),
        name="norm_back",
    )(*hats, gain_query, gain_key, dq, dk, late)


def grad_mixed_kernel(cot_ref, weight_ref, out_ref):
    out_ref[...] = nt(cot_ref[...], weight_ref[...]).astype(BF)


def grad_mixed_of(cotangent, weight):
    inner, width = weight.shape
    return pl.pallas_call(
        grad_mixed_kernel,
        grid=(inner // WIDE,),
        in_specs=[
            pl.BlockSpec((CELLS, width), lambda n: (0, 0)),
            pl.BlockSpec((WIDE, width), lambda n: (n, 0)),
        ],
        out_specs=pl.BlockSpec((CELLS, WIDE), lambda n: (0, n)),
        out_shape=jax.ShapeDtypeStruct((CELLS, inner), BF),
        compiler_params=PARAMS,
        cost_estimate=cost(8.7),
        name="grad_mixed",
    )(cotangent, weight)


def project_kernel(mixed_ref, weight_ref, out_ref):
    out_ref[...] = nn(mixed_ref[...], weight_ref[...]).astype(BF)


def project(mixed, weight):
    inner, width = weight.shape
    block = width // 4
    return pl.pallas_call(
        project_kernel,
        grid=(4,),
        in_specs=[
            pl.BlockSpec((CELLS, inner), lambda n: (0, 0)),
            pl.BlockSpec((inner, block), lambda n: (0, n)),
        ],
        out_specs=pl.BlockSpec((CELLS, block), lambda n: (0, n)),
        out_shape=jax.ShapeDtypeStruct((CELLS, width), BF),
        compiler_params=PARAMS,
        cost_estimate=cost(7),
        name="project",
    )(mixed, weight)


PIECES = 6
STEPS = 3
TAIL = 8


def gain_rows(gain_refs, block):
    total = gain_refs[0][...]
    for gain_ref in gain_refs[1:]:
        total = total + gain_ref[...]
    terms = []
    for row in range(2):
        rest = total[row : row + 1]
        for _ in range(3):
            terms.append(rest.astype(BF).astype(F32))
            rest = rest - terms[-1]
    rows = jnp.concatenate(terms + [jnp.zeros((TAIL - 6, LANES), F32)], 0)
    return jnp.concatenate([rows, jnp.zeros((TAIL, block - LANES), F32)], 1).astype(BF)


def weight_kernel(place_ref, order_ref, mixed_ref, cot_ref, *refs):
    *gain_refs, out_ref, turned, product = refs
    shares, rows, block = out_ref.shape
    own = product.shape[0] // shares

    @pl.when(pl.program_id(0) == 0)
    def _():
        turned[...] = nt(order_ref[0], mixed_ref[...]).astype(BF)
        tail = gain_rows(gain_refs, block)
        for share in range(shares):
            out_ref[share, rows - TAIL :] = tail

    product[...] = nn(turned[...], cot_ref[...])
    for step in range(STEPS):

        @pl.when(pl.program_id(0) == step)
        def _():
            for share in range(shares):
                for half in range(PIECES // STEPS):
                    top = (step * (PIECES // STEPS) + half) * own
                    out_ref[share, top : top + own] = product[
                        share * own : (share + 1) * own, half * block : (half + 1) * block
                    ].astype(BF)


def weight_parts(place, order, mixed, cotangents, gain_sums, shares):
    tokens, width = cotangents.shape
    _, features, wide = order.shape
    block = width // PIECES
    columns = width // STEPS
    rows = -(-(PIECES * (features // shares) + TAIL) // 16) * 16
    gain = pl.BlockSpec((8, LANES), lambda n, place: (0, 0))
    return pl.pallas_call(
        weight_kernel,
        grid_spec=pltpu.PrefetchScalarGridSpec(
            num_scalar_prefetch=1,
            grid=(STEPS,),
            in_specs=[
                pl.BlockSpec((1, features, wide), lambda n, place: (place[1], 0, 0)),
                pl.BlockSpec((tokens, wide), lambda n, place: (0, place[0])),
                pl.BlockSpec((tokens, columns), lambda n, place: (0, n)),
            ]
            + [gain] * len(gain_sums),
            out_specs=pl.BlockSpec((shares, rows, block), lambda n, place: (0, 0, 0)),
            scratch_shapes=[
                pltpu.VMEM((features, tokens), BF),
                pltpu.VMEM((features, columns), F32),
            ],
        ),
        out_shape=jax.ShapeDtypeStruct((shares, rows, block), BF),
        compiler_params=PARAMS,
        cost_estimate=cost(9.5),
        name="weight_parts",
    )(place, order, mixed, cotangents, *gain_sums)


def sum_kernel(parts_ref, out_ref, gain_q_ref, gain_k_ref):
    shares, rows, block = parts_ref.shape
    own = out_ref.shape[0]
    total = parts_ref[0].astype(F32)
    for share in range(1, shares):
        total = total + parts_ref[share].astype(F32)
    for piece in range(PIECES):
        out_ref[:, piece * block : (piece + 1) * block] = total[piece * own : (piece + 1) * own]
    tail = total[rows - TAIL :, :LANES]
    for number, gain_ref in enumerate((gain_q_ref, gain_k_ref)):
        gain = jnp.sum(tail[3 * number : 3 * number + 3], 0, keepdims=True)
        gain_ref[...] = gain[:, :HD] + gain[:, HD:]


def sum_parts(parts, own):
    block = parts.shape[2]
    gain = jax.ShapeDtypeStruct((1, HD), F32)
    return pl.pallas_call(
        sum_kernel,
        in_specs=[VMEM],
        out_specs=[VMEM] * 3,
        out_shape=[jax.ShapeDtypeStruct((own, PIECES * block), F32), gain, gain],
        compiler_params=SMALL,
        cost_estimate=cost(2.2),
        name="sum_parts",
    )(parts)


def feature_order(inner, planes, cores, shares):
    wide = inner // planes
    features = wide // cores
    own = features // shares
    order = np.zeros((cores, features, wide), np.float32)
    for core in range(cores):
        for feature in range(features):
            share, row = divmod(feature, own)
            order[core, feature, own * (cores * share + core) + row] = 1.0
    return jnp.asarray(order, BF)


def local(
    queries,
    keys_proj,
    values_proj,
    gain_query,
    gain_key,
    frame_counts,
    heights,
    widths,
    out_weight,
    cotangent,
):
    seq = ("y", "core")
    group = ("x", "core")
    sums = ("z", "y")
    planes, cores = lax.axis_size("x"), lax.axis_size("core")
    shares = lax.axis_size("z") * lax.axis_size("y")
    inner = out_weight.shape[0]
    rank = lax.axis_index(seq).astype(jnp.int32)
    counts = jnp.stack([frame_counts[0], heights[0], widths[0], rank])
    gains = gain_query.reshape(1, HD), gain_key.reshape(1, HD)
    query_rows, key_rows, value_rows = queries[0, 0], keys_proj[0, 0], values_proj[0, 0]
    cot_rows = cotangent[0, 0]
    by_cells = (FRAMES, CELLS_HERE, inner)

    def exchange(tensor, axes):
        return lax.all_to_all(tensor, axes, split_axis=0, concat_axis=0, tiled=True)

    def after(tensor, earlier):
        return lax.optimization_barrier((tensor, earlier))[0]

    cotangents = lax.all_gather(cot_rows, group, axis=0, tiled=True)
    normed = norm(query_rows, key_rows, *gains)
    normed_cells = exchange(normed, seq)
    grad_mixed = grad_mixed_of(cot_rows, out_weight)
    outgoing, chances = space_forward(counts, normed, value_rows, grad_mixed)
    arrived = exchange(after(outgoing, normed_cells), seq)
    hats = hats_of(*lax.optimization_barrier((query_rows, key_rows, outgoing))[:2])
    arrived, *hats = lax.optimization_barrier((arrived, *hats))
    mixed_cells = time_forward(counts, normed_cells, arrived)
    mixed = exchange(mixed_cells, seq).reshape(CELLS, inner)
    late_cells, dspatial_cells, late_gains = time_back(counts, normed_cells, arrived)
    place = jnp.stack([lax.axis_index("x"), lax.axis_index("core")]).astype(jnp.int32)
    first = (cotangents, dspatial_cells)
    gathered = lax.all_gather(after(mixed, first), group, axis=0, tiled=True)
    dspatial = exchange(after(dspatial_cells, mixed), seq).reshape(CELLS, inner)
    late = exchange(after(late_cells, dspatial), seq)
    block_out = project(mixed, out_weight)
    dq, dk, grad_values, gain_sums = space_back(
        late_gains, *gains, hats[:2], normed, value_rows, dspatial, chances
    )
    for flip in range(1, cores):
        pairs = [(i, (i + flip) % cores) for i in range(cores)]
        gain_sums = gain_sums + lax.ppermute(gain_sums, "core", pairs)
    gain_sums = [gain_sums] + [
        lax.ppermute(gain_sums, "x", [(i, (i + step) % planes) for i in range(planes)])
        for step in range(1, planes)
    ]
    grad_queries, grad_keys = norm_back(hats, *gains, dq, dk, late)
    order = feature_order(inner, planes, cores, shares)
    parts = weight_parts(place, order, gathered, cotangents, gain_sums, shares)
    parts = exchange(after(parts, late), sums)
    own = order.shape[1] // shares
    grad_weight, grad_gain_query, grad_gain_key = sum_parts(parts, own)
    return (
        block_out.reshape(cotangent.shape),
        grad_queries.reshape(queries.shape),
        grad_keys.reshape(queries.shape),
        grad_values.reshape(queries.shape),
        grad_weight,
        grad_gain_query.reshape(HD),
        grad_gain_key.reshape(HD),
    )


def solution(mesh):
    planes = 4 if mesh.shape["dp"] == 16 else mesh.shape["dp"]
    fine = Mesh(
        mesh.devices.reshape(planes, mesh.shape["dp"] // planes, -1, 2), ("x", "z", "y", "core")
    )
    tokens = P(("x", "z"), ("y", "core"), None, None)
    clips = P(("x", "z"))
    return jax.shard_map(
        local,
        mesh=fine,
        in_specs=(tokens, tokens, tokens, P(), P(), clips, clips, clips, P(), tokens),
        out_specs=(
            tokens,
            tokens,
            tokens,
            tokens,
            P(("x", "z", "y", "core"), None),
            P(),
            P(),
        ),
        check_vma=False,
    )
```

```python
import jax
import jax.numpy as jnp
import numpy as np
from jax import lax
from jax.experimental import pallas as pl
from jax.experimental.pallas import tpu as pltpu
from jax.sharding import Mesh
from jax.sharding import PartitionSpec as P

BF = jnp.bfloat16
F32 = jnp.float32
HD = 64
PW = 16
CELLS = 256
FRAMES = 8
LANES = 128
WIDE = 384
PAIRS = WIDE // LANES
CELLS_HERE = CELLS // FRAMES
BLOCK = 16
NEG = -1e30
SCALE = HD**-0.5
PARAMS = pltpu.CompilerParams(vmem_limit_bytes=56 * 1024 * 1024)
SMALL = pltpu.CompilerParams(vmem_limit_bytes=16 * 1024 * 1024)


def cost(microseconds):
    return pl.CostEstimate(flops=0, bytes_accessed=int(microseconds * 3.69e6), transcendentals=0)


SMEM = pl.BlockSpec(memory_space=pltpu.SMEM)
VMEM = pl.BlockSpec(memory_space=pltpu.VMEM)


def nn(left, right):
    return jnp.dot(left, right, preferred_element_type=F32)


def nt(left, right):
    return lax.dot_general(left, right, (((1,), (1,)), ((), ())), preferred_element_type=F32)


def tn(left, right):
    return lax.dot_general(left, right, (((0,), (0,)), ((), ())), preferred_element_type=F32)


def low_lanes(shape):
    return lax.broadcasted_iota(jnp.int32, shape, len(shape) - 1) < HD


def stack_heads(pair):
    low = low_lanes((1, LANES)).astype(F32)
    return jnp.concatenate([pair * low.astype(BF), pair * (1.0 - low).astype(BF)], 0)


def pick_heads(stacked):
    half = stacked.shape[0] // 2
    return jnp.where(low_lanes((half, LANES)), stacked[:half], stacked[half:])


def softmax_rows(scores):
    grouped = scores.reshape(2, scores.shape[0] // 2, scores.shape[1])
    expo = jnp.exp(grouped - jnp.max(grouped, 1, keepdims=True))
    return expo * (1.0 / jnp.sum(expo, 1, keepdims=True))


def score_back(chances, dchances):
    grouped = dchances.reshape(chances.shape)
    total = jnp.sum(chances * grouped, 1, keepdims=True)
    return (chances * (grouped - total)).astype(BF).reshape(dchances.shape)


def cell_ok(cells, height, width):
    row = lax.shift_right_logical(cells, 4)
    return (row < height) & ((cells & (PW - 1)) < width)


def head_ones(rows, columns):
    row = lax.broadcasted_iota(jnp.int32, (rows, columns), 0) & (columns - 1)
    column = lax.broadcasted_iota(jnp.int32, (rows, columns), 1)
    same = lax.shift_right_logical(row, 6) == lax.shift_right_logical(column, 6)
    return jnp.where(same, 1.0, 0.0).astype(BF)


def head_mean(tensor, twice):
    high = tensor.astype(BF)
    rest = (tensor - high.astype(F32)).astype(BF)
    return nn(jnp.concatenate([high, rest], 1), twice) * (1.0 / HD)


def hat_of(raw, ones, twice):
    centre = raw.astype(F32) - nn(raw, ones) * (1.0 / HD)
    hats, inverses = [], []
    for left in range(0, raw.shape[1], LANES):
        part = centre[:, left : left + LANES]
        inverse = lax.rsqrt(head_mean(part * part, twice) + 1e-06)
        hats.append(part * inverse)
        inverses.append(inverse)
    return hats, inverses


def both_heads(gain_ref):
    return jnp.concatenate([gain_ref[...], gain_ref[...]], 1)


def pair_slice(number):
    return slice(number * LANES, (number + 1) * LANES)


NORM_WIDE = 512
DUO = 2 * LANES


def norm_kernel(q_ref, k_ref, gain_q_ref, gain_k_ref, out_ref):
    ones, twice = head_ones(DUO, DUO), head_ones(DUO, LANES)
    gains = both_heads(gain_q_ref), both_heads(gain_k_ref)
    for left in range(0, NORM_WIDE, DUO):
        for number, source in enumerate((q_ref, k_ref)):
            hats, _ = hat_of(source[:, left : left + DUO], ones, twice)
            for pair, hat in enumerate(hats):
                normed = (hat * gains[number]).astype(BF)
                if number == 0:
                    normed = normed * jnp.asarray(SCALE, BF)
                at = slice(left + pair * LANES, left + (pair + 1) * LANES)
                out_ref[:, number, :, at] = normed.reshape(FRAMES, CELLS_HERE, LANES)


def norm(queries, keys, gain_query, gain_key):
    inner = queries.shape[1]
    tokens = pl.BlockSpec((CELLS, NORM_WIDE), lambda n: (0, n))
    gain = pl.BlockSpec((1, HD), lambda n: (0, 0))
    return pl.pallas_call(
        norm_kernel,
        grid=(inner // NORM_WIDE,),
        in_specs=[tokens, tokens, gain, gain],
        out_specs=pl.BlockSpec((FRAMES, 2, CELLS_HERE, NORM_WIDE), lambda n: (0, 0, 0, n)),
        out_shape=jax.ShapeDtypeStruct((FRAMES, 2, CELLS_HERE, inner), BF),
        compiler_params=PARAMS,
        cost_estimate=cost(5),
        name="norm",
    )(queries, keys, gain_query, gain_key)


def hats_kernel(q_ref, k_ref, *out_refs):
    ones, twice = head_ones(DUO, DUO), head_ones(DUO, LANES)
    for left in range(0, NORM_WIDE, DUO):
        for number, source in enumerate((q_ref, k_ref)):
            hats, inverses = hat_of(source[:, left : left + DUO], ones, twice)
            at = slice(left, left + DUO)
            out_refs[number][:, at] = jnp.concatenate(hats, 1)
            out_refs[2 + number][:, at] = jnp.concatenate(inverses, 1)


def hats_of(queries, keys):
    inner = queries.shape[1]
    tokens = pl.BlockSpec((CELLS, NORM_WIDE), lambda n: (0, n))
    return pl.pallas_call(
        hats_kernel,
        grid=(inner // NORM_WIDE,),
        in_specs=[tokens, tokens],
        out_specs=[tokens] * 4,
        out_shape=[jax.ShapeDtypeStruct((CELLS, inner), F32)] * 4,
        compiler_params=PARAMS,
        cost_estimate=cost(5.6),
        name="hats",
    )(queries, keys)


def space_kernel(counts_ref, qk_ref, v_ref, gm_ref, out_ref, chances_ref):
    height, width = counts_ref[1], counts_ref[2]
    frame_on = jnp.where(counts_ref[3] < counts_ref[0], 1.0, 0.0)
    key_cell = lax.broadcasted_iota(jnp.int32, (2 * CELLS, CELLS), 0) & (CELLS - 1)
    bias = jnp.where(cell_ok(key_cell, height, width), 0.0, NEG)
    cell = lax.broadcasted_iota(jnp.int32, (CELLS, LANES), 0)
    usable = cell_ok(cell, height, width).astype(F32) * frame_on
    scores = []
    for pair in range(PAIRS):
        query = qk_ref[:, 0, :, pair_slice(pair)].reshape(CELLS, LANES)
        key = qk_ref[:, 1, :, pair_slice(pair)].reshape(CELLS, LANES)
        scores.append(nt(stack_heads(key), query) + bias)
    weights = []
    for pair in range(PAIRS):
        probs = softmax_rows(scores[pair]).reshape(scores[pair].shape)
        chances_ref[pair] = probs
        weights.append(probs.astype(BF))
    for pair in range(PAIRS):
        mixed = tn(weights[pair], stack_heads(v_ref[:, pair_slice(pair)]))
        mixed = (mixed * usable).astype(BF)
        out_ref[:, 0, :, pair_slice(pair)] = mixed.reshape(FRAMES, CELLS_HERE, LANES)
    out_ref[:, 1] = gm_ref[...].reshape(FRAMES, CELLS_HERE, WIDE)


def space_forward(counts, normed, values, grad_mixed):
    inner = values.shape[1]
    tokens = pl.BlockSpec((CELLS, WIDE), lambda n: (0, n))
    return pl.pallas_call(
        space_kernel,
        grid=(inner // WIDE,),
        in_specs=[
            SMEM,
            pl.BlockSpec((FRAMES, 2, CELLS_HERE, WIDE), lambda n: (0, 0, 0, n)),
            tokens,
            tokens,
        ],
        out_specs=[
            pl.BlockSpec((FRAMES, 2, CELLS_HERE, WIDE), lambda n: (0, 0, 0, n)),
            pl.BlockSpec((PAIRS, 2 * CELLS, CELLS), lambda n: (n, 0, 0)),
        ],
        out_shape=[
            jax.ShapeDtypeStruct((FRAMES, 2, CELLS_HERE, inner), BF),
            jax.ShapeDtypeStruct((inner // LANES, 2 * CELLS, CELLS), F32),
        ],
        compiler_params=PARAMS,
        cost_estimate=cost(7),
        name="space_forward",
    )(counts, normed, values, grad_mixed)


def gain_part(grad, normed):
    return jnp.sum(grad * normed.astype(F32), 0, keepdims=True)


def add_gains(sums_ref, of_query, of_key, begin=None):
    @pl.when(pl.program_id(0) == 0)
    def _():
        sums_ref[...] = jnp.zeros_like(sums_ref) if begin is None else begin()

    sums_ref[0:1] += of_query
    sums_ref[1:2] += of_key


def space_back_kernel(
    late_ref,
    gain_q_ref,
    gain_k_ref,
    hat_q_ref,
    hat_k_ref,
    qk_ref,
    v_ref,
    up_ref,
    chances_ref,
    dq_ref,
    dk_ref,
    dv_ref,
    sums_ref,
):
    def late_gains():
        scale = [both_heads(gain_q_ref) * SCALE, both_heads(gain_k_ref)]
        return late_ref[...] / jnp.concatenate(scale + [jnp.ones((6, LANES), F32)], 0)

    of_query = jnp.zeros((1, LANES), F32)
    of_key = jnp.zeros((1, LANES), F32)
    slices = [pair_slice(pair) for pair in range(PAIRS)]
    queries = [qk_ref[:, 0, :, at].reshape(CELLS, LANES) for at in slices]
    keys = [stack_heads(qk_ref[:, 1, :, at].reshape(CELLS, LANES)) for at in slices]
    dchances = [nt(stack_heads(v_ref[:, at]), up_ref[:, at]) for at in slices]
    dscores = []
    for pair, at in enumerate(slices):
        probs = chances_ref[pair]
        dv_ref[:, at] = pick_heads(nn(probs.astype(BF), up_ref[:, at])).astype(BF)
        dscores.append(score_back(probs.reshape(2, CELLS, CELLS), dchances[pair]))
    for pair, at in enumerate(slices):
        dk = pick_heads(nn(dscores[pair], queries[pair]))
        dq = tn(dscores[pair], keys[pair]) * SCALE
        dk_ref[:, at] = dk
        dq_ref[:, at] = dq
        of_query += gain_part(dq, hat_q_ref[:, at])
        of_key += gain_part(dk, hat_k_ref[:, at])
    add_gains(sums_ref, of_query, of_key, late_gains)


def space_back(late_sums, gain_query, gain_key, hats, normed, values, upstream, chances):
    inner = values.shape[1]
    tokens = pl.BlockSpec((CELLS, WIDE), lambda n: (0, n))
    wide = jax.ShapeDtypeStruct((CELLS, inner), F32)
    return pl.pallas_call(
        space_back_kernel,
        grid=(inner // WIDE,),
        in_specs=[
            pl.BlockSpec((8, LANES), lambda n: (0, 0)),
            pl.BlockSpec((1, HD), lambda n: (0, 0)),
            pl.BlockSpec((1, HD), lambda n: (0, 0)),
            tokens,
            tokens,
            pl.BlockSpec((FRAMES, 2, CELLS_HERE, WIDE), lambda n: (0, 0, 0, n)),
            tokens,
            tokens,
            pl.BlockSpec((PAIRS, 2 * CELLS, CELLS), lambda n: (n, 0, 0)),
        ],
        out_specs=[tokens, tokens, tokens, pl.BlockSpec((8, LANES), lambda n: (0, 0))],
        out_shape=[
            wide,
            wide,
            jax.ShapeDtypeStruct((CELLS, inner), BF),
            jax.ShapeDtypeStruct((8, LANES), F32),
        ],
        compiler_params=PARAMS,
        cost_estimate=cost(9),
        name="space_back",
    )(late_sums, gain_query, gain_key, *hats, normed, values, upstream, chances)


def time_bias(frame_total):
    key = lax.broadcasted_iota(jnp.int32, (2 * LANES, LANES), 0) & (LANES - 1)
    query = lax.broadcasted_iota(jnp.int32, (2 * LANES, LANES), 1)
    same = (key & (BLOCK - 1)) == (query & (BLOCK - 1))
    return jnp.where(same & (lax.shift_right_logical(key, 4) < frame_total), 0.0, NEG)


def time_usable(counts_ref, block):
    row = lax.broadcasted_iota(jnp.int32, (LANES, LANES), 0)
    cell = counts_ref[3] * CELLS_HERE + block * BLOCK + (row & (BLOCK - 1))
    on = cell_ok(cell, counts_ref[1], counts_ref[2])
    return (on & (lax.shift_right_logical(row, 4) < counts_ref[0])).astype(F32)


def time_blocks():
    for block in range(CELLS_HERE // BLOCK):
        for pair in range(PAIRS):
            yield block, slice(block * BLOCK, (block + 1) * BLOCK), pair_slice(pair)


def time_kernel(counts_ref, qk_ref, sg_ref, out_ref):
    bias = time_bias(counts_ref[0])
    usable = [time_usable(counts_ref, block) for block in range(CELLS_HERE // BLOCK)]
    scores = []
    for block, rows, at in time_blocks():
        query = qk_ref[:, 0, rows, at].reshape(LANES, LANES)
        keys = stack_heads(qk_ref[:, 1, rows, at].reshape(LANES, LANES))
        scores.append(nt(keys, query) + bias)
    weights = [softmax_rows(part).astype(BF).reshape(part.shape) for part in scores]
    for number, (block, rows, at) in enumerate(time_blocks()):
        values = stack_heads(sg_ref[:, 0, rows, at].reshape(LANES, LANES))
        mixed = tn(weights[number], values) * usable[block]
        out_ref[:, rows, at] = mixed.astype(BF).reshape(FRAMES, BLOCK, LANES)


def time_back_kernel(counts_ref, qk_ref, sg_ref, dqk_ref, ds_ref, sums_ref):
    bias = time_bias(counts_ref[0])
    of_query = jnp.zeros((1, LANES), F32)
    of_key = jnp.zeros((1, LANES), F32)
    usable = [time_usable(counts_ref, block) for block in range(CELLS_HERE // BLOCK)]
    blocks = list(time_blocks())

    def load(ref, number, rows, at):
        return ref[:, number, rows, at].reshape(LANES, LANES)

    def shaped(tensor):
        return tensor.astype(BF).reshape(FRAMES, BLOCK, LANES)

    queries = [load(qk_ref, 0, rows, at) for _, rows, at in blocks]
    singles = [load(qk_ref, 1, rows, at) for _, rows, at in blocks]
    keys = [stack_heads(key) for key in singles]
    upstreams = [
        (load(sg_ref, 1, rows, at).astype(F32) * usable[block]).astype(BF)
        for block, rows, at in blocks
    ]
    scores = [nt(key, query) + bias for key, query in zip(keys, queries)]
    dchances = [
        nt(stack_heads(load(sg_ref, 0, rows, at)), upstream)
        for (_, rows, at), upstream in zip(blocks, upstreams)
    ]
    chances = [softmax_rows(part) for part in scores]
    dscores = [score_back(probs, part) for probs, part in zip(chances, dchances)]
    for number, (_, rows, at) in enumerate(blocks):
        weights = chances[number].astype(BF).reshape(2 * LANES, LANES)
        ds_ref[:, rows, at] = shaped(pick_heads(nn(weights, upstreams[number])))
        dq = tn(dscores[number], keys[number]) * SCALE
        dk = pick_heads(nn(dscores[number], queries[number]))
        dqk_ref[:, 0, rows, at] = shaped(dq)
        dqk_ref[:, 1, rows, at] = shaped(dk)
        of_query += gain_part(dq, queries[number])
        of_key += gain_part(dk, singles[number])
    add_gains(sums_ref, of_query, of_key)


def time_specs(inner):
    double = pl.BlockSpec((FRAMES, 2, CELLS_HERE, WIDE), lambda n: (0, 0, 0, n))
    single = pl.BlockSpec((FRAMES, CELLS_HERE, WIDE), lambda n: (0, 0, n))
    return (
        double,
        single,
        jax.ShapeDtypeStruct((FRAMES, 2, CELLS_HERE, inner), BF),
        jax.ShapeDtypeStruct((FRAMES, CELLS_HERE, inner), BF),
    )


def time_forward(counts, normed, arrived):
    inner = arrived.shape[3]
    double, single, _, single_shape = time_specs(inner)
    return pl.pallas_call(
        time_kernel,
        grid=(inner // WIDE,),
        in_specs=[SMEM, double, double],
        out_specs=single,
        out_shape=single_shape,
        compiler_params=SMALL,
        cost_estimate=cost(5),
        name="time_forward",
    )(counts, normed, arrived)


def time_back(counts, normed, arrived):
    inner = arrived.shape[3]
    double, single, double_shape, single_shape = time_specs(inner)
    return pl.pallas_call(
        time_back_kernel,
        grid=(inner // WIDE,),
        in_specs=[SMEM, double, double],
        out_specs=[double, single, pl.BlockSpec((8, LANES), lambda n: (0, 0))],
        out_shape=[double_shape, single_shape, jax.ShapeDtypeStruct((8, LANES), F32)],
        compiler_params=SMALL,
        cost_estimate=cost(6.5),
        name="time_back",
    )(counts, normed, arrived)


def norm_back_kernel(
    hat_q_ref,
    hat_k_ref,
    inverse_q_ref,
    inverse_k_ref,
    gain_q_ref,
    gain_k_ref,
    dq_ref,
    dk_ref,
    late_ref,
    gq_ref,
    gk_ref,
):
    twice = head_ones(DUO, LANES)
    for left in range(0, NORM_WIDE, LANES):
        at = slice(left, left + LANES)
        for number, (hat_ref, inverse_ref, gain_ref, early, target) in enumerate(
            (
                (hat_q_ref, inverse_q_ref, gain_q_ref, dq_ref, gq_ref),
                (hat_k_ref, inverse_k_ref, gain_k_ref, dk_ref, gk_ref),
            )
        ):
            hat = hat_ref[:, at]
            late = late_ref[:, number, :, at].reshape(CELLS, LANES)
            scaled = (early[:, at] + late.astype(F32)) * both_heads(gain_ref)
            mean = head_mean(scaled, twice)
            dinput = scaled - mean - hat * head_mean(scaled * hat, twice)
            target[:, at] = (inverse_ref[:, at] * dinput).astype(BF)


def norm_back(hats, gain_query, gain_key, dq, dk, late):
    inner = dq.shape[1]
    tokens = pl.BlockSpec((CELLS, NORM_WIDE), lambda n: (0, n))
    gain = pl.BlockSpec((1, HD), lambda n: (0, 0))
    grads = jax.ShapeDtypeStruct((CELLS, inner), BF)
    return pl.pallas_call(
        norm_back_kernel,
        grid=(inner // NORM_WIDE,),
        in_specs=[
            tokens,
            tokens,
            tokens,
            tokens,
            gain,
            gain,
            tokens,
            tokens,
            pl.BlockSpec((FRAMES, 2, CELLS_HERE, NORM_WIDE), lambda n: (0, 0, 0, n)),
        ],
        out_specs=[tokens, tokens],
        out_shape=[grads, grads],
        compiler_params=PARAMS,
        cost_estimate=cost(7),
        name="norm_back",
    )(*hats, gain_query, gain_key, dq, dk, late)


def grad_mixed_kernel(cot_ref, weight_ref, out_ref):
    out_ref[...] = nt(cot_ref[...], weight_ref[...]).astype(BF)


def grad_mixed_of(cotangent, weight):
    inner, width = weight.shape
    return pl.pallas_call(
        grad_mixed_kernel,
        grid=(inner // WIDE,),
        in_specs=[
            pl.BlockSpec((CELLS, width), lambda n: (0, 0)),
            pl.BlockSpec((WIDE, width), lambda n: (n, 0)),
        ],
        out_specs=pl.BlockSpec((CELLS, WIDE), lambda n: (0, n)),
        out_shape=jax.ShapeDtypeStruct((CELLS, inner), BF),
        compiler_params=PARAMS,
        cost_estimate=cost(8.7),
        name="grad_mixed",
    )(cotangent, weight)


def project_kernel(mixed_ref, weight_ref, out_ref):
    out_ref[...] = nn(mixed_ref[...], weight_ref[...]).astype(BF)


def project(mixed, weight):
    inner, width = weight.shape
    block = width // 4
    return pl.pallas_call(
        project_kernel,
        grid=(4,),
        in_specs=[
            pl.BlockSpec((CELLS, inner), lambda n: (0, 0)),
            pl.BlockSpec((inner, block), lambda n: (0, n)),
        ],
        out_specs=pl.BlockSpec((CELLS, block), lambda n: (0, n)),
        out_shape=jax.ShapeDtypeStruct((CELLS, width), BF),
        compiler_params=PARAMS,
        cost_estimate=cost(7),
        name="project",
    )(mixed, weight)


PIECES = 6
TAIL = 8


def gain_rows(gain_refs, block):
    total = gain_refs[0][...]
    for gain_ref in gain_refs[1:]:
        total = total + gain_ref[...]
    terms = []
    for row in range(2):
        rest = total[row : row + 1]
        for _ in range(3):
            terms.append(rest.astype(BF).astype(F32))
            rest = rest - terms[-1]
    rows = jnp.concatenate(terms + [jnp.zeros((TAIL - 6, LANES), F32)], 0)
    return jnp.concatenate([rows, jnp.zeros((TAIL, block - LANES), F32)], 1).astype(BF)


def weight_kernel(counts_ref, order_ref, mixed_hbm, cot_hbm, *refs):
    *gain_refs, out_ref, mixed_ref, cot_ref, turned, product, mixed_sem, cot_sems = refs
    shares, rows, block = out_ref.shape
    wide = mixed_ref.shape[1]
    own = turned.shape[0] // shares
    left = pl.multiple_of(counts_ref[4] * wide, LANES)
    mixed_copy = pltpu.make_async_copy(mixed_hbm.at[:, pl.ds(left, wide)], mixed_ref, mixed_sem)
    mixed_copy.start()
    copies = [
        pltpu.make_async_copy(
            cot_hbm.at[:, piece * block : (piece + 1) * block],
            cot_ref.at[piece],
            cot_sems.at[piece],
        )
        for piece in range(PIECES)
    ]
    for copy in copies:
        copy.start()
    tail = gain_rows(gain_refs, block)
    for share in range(shares):
        out_ref[share, rows - TAIL :] = tail
    mixed_copy.wait()
    turned[...] = nt(order_ref[counts_ref[5]], mixed_ref[...]).astype(BF)
    for piece, copy in enumerate(copies):
        copy.wait()
        slot = piece % 2
        product[slot] = nn(turned[...], cot_ref[piece])
        for share in range(shares):
            out_ref[share, piece * own : (piece + 1) * own] = product[
                slot, share * own : (share + 1) * own
            ].astype(BF)


def weight_parts(counts, order, mixed, cotangents, gain_sums, shares):
    tokens, width = cotangents.shape
    _, features, wide = order.shape
    block = width // PIECES
    rows = -(-(PIECES * (features // shares) + TAIL) // 16) * 16
    anywhere = pl.BlockSpec(memory_space=pl.ANY)
    return pl.pallas_call(
        weight_kernel,
        in_specs=[SMEM, VMEM, anywhere, anywhere] + [VMEM] * len(gain_sums),
        out_specs=VMEM,
        out_shape=jax.ShapeDtypeStruct((shares, rows, block), BF),
        scratch_shapes=[
            pltpu.VMEM((tokens, wide), BF),
            pltpu.VMEM((PIECES, tokens, block), BF),
            pltpu.VMEM((features, tokens), BF),
            pltpu.VMEM((2, features, block), F32),
            pltpu.SemaphoreType.DMA,
            pltpu.SemaphoreType.DMA((PIECES,)),
        ],
        compiler_params=PARAMS,
        cost_estimate=cost(7.5),
        name="weight_parts",
    )(counts, order, mixed, cotangents, *gain_sums)


def sum_kernel(parts_ref, out_ref, gain_q_ref, gain_k_ref):
    shares, rows, block = parts_ref.shape
    own = out_ref.shape[0]
    total = parts_ref[0].astype(F32)
    for share in range(1, shares):
        total = total + parts_ref[share].astype(F32)
    for piece in range(PIECES):
        out_ref[:, piece * block : (piece + 1) * block] = total[piece * own : (piece + 1) * own]
    tail = total[rows - TAIL :, :LANES]
    for number, gain_ref in enumerate((gain_q_ref, gain_k_ref)):
        gain = jnp.sum(tail[3 * number : 3 * number + 3], 0, keepdims=True)
        gain_ref[...] = gain[:, :HD] + gain[:, HD:]


def sum_parts(parts, own):
    block = parts.shape[2]
    gain = jax.ShapeDtypeStruct((1, HD), F32)
    return pl.pallas_call(
        sum_kernel,
        in_specs=[VMEM],
        out_specs=[VMEM] * 3,
        out_shape=[jax.ShapeDtypeStruct((own, PIECES * block), F32), gain, gain],
        compiler_params=SMALL,
        cost_estimate=cost(2.2),
        name="sum_parts",
    )(parts)


def feature_order(inner, planes, cores, shares):
    wide = inner // planes
    features = wide // cores
    own = features // shares
    order = np.zeros((cores, features, wide), np.float32)
    for core in range(cores):
        for feature in range(features):
            share, row = divmod(feature, own)
            order[core, feature, own * (cores * share + core) + row] = 1.0
    return jnp.asarray(order, BF)


def local(
    queries,
    keys_proj,
    values_proj,
    gain_query,
    gain_key,
    frame_counts,
    heights,
    widths,
    out_weight,
    cotangent,
):
    seq = ("y", "core")
    group = ("x", "core")
    sums = ("z", "y")
    planes, cores = lax.axis_size("x"), lax.axis_size("core")
    shares = lax.axis_size("z") * lax.axis_size("y")
    inner = out_weight.shape[0]
    rank = lax.axis_index(seq).astype(jnp.int32)
    counts = [frame_counts[0], heights[0], widths[0], rank]
    counts += [lax.axis_index("x").astype(jnp.int32), lax.axis_index("core").astype(jnp.int32)]
    counts = jnp.stack(counts)
    gains = gain_query.reshape(1, HD), gain_key.reshape(1, HD)
    query_rows, key_rows, value_rows = queries[0, 0], keys_proj[0, 0], values_proj[0, 0]
    cot_rows = cotangent[0, 0]
    by_cells = (FRAMES, CELLS_HERE, inner)

    def exchange(tensor, axes):
        return lax.all_to_all(tensor, axes, split_axis=0, concat_axis=0, tiled=True)

    def after(tensor, earlier):
        return lax.optimization_barrier((tensor, earlier))[0]

    cotangents = lax.all_gather(cot_rows, group, axis=0, tiled=True)
    normed = norm(query_rows, key_rows, *gains)
    normed_cells = exchange(normed, seq)
    grad_mixed = grad_mixed_of(cot_rows, out_weight)
    outgoing, chances = space_forward(counts, normed, value_rows, grad_mixed)
    arrived = exchange(after(outgoing, normed_cells), seq)
    hats = hats_of(*lax.optimization_barrier((query_rows, key_rows, outgoing))[:2])
    arrived, *hats = lax.optimization_barrier((arrived, *hats))
    mixed_cells = time_forward(counts, normed_cells, arrived)
    mixed = exchange(mixed_cells, seq).reshape(CELLS, inner)
    late_cells, dspatial_cells, late_gains = time_back(counts, normed_cells, arrived)
    first = (cotangents, dspatial_cells)
    gathered = lax.all_gather(after(mixed, first), group, axis=0, tiled=True)
    dspatial = exchange(after(dspatial_cells, mixed), seq).reshape(CELLS, inner)
    late = exchange(after(late_cells, dspatial), seq)
    block_out = project(mixed, out_weight)
    dq, dk, grad_values, gain_sums = space_back(
        late_gains, *gains, hats[:2], normed, value_rows, dspatial, chances
    )
    for flip in range(1, cores):
        pairs = [(i, (i + flip) % cores) for i in range(cores)]
        gain_sums = gain_sums + lax.ppermute(gain_sums, "core", pairs)
    gain_sums = [gain_sums] + [
        lax.ppermute(gain_sums, "x", [(i, (i + step) % planes) for i in range(planes)])
        for step in range(1, planes)
    ]
    grad_queries, grad_keys = norm_back(hats, *gains, dq, dk, late)
    order = feature_order(inner, planes, cores, shares)
    parts = weight_parts(counts, order, gathered, cotangents, gain_sums, shares)
    parts = exchange(after(parts, late), sums)
    own = order.shape[1] // shares
    grad_weight, grad_gain_query, grad_gain_key = sum_parts(parts, own)
    return (
        block_out.reshape(cotangent.shape),
        grad_queries.reshape(queries.shape),
        grad_keys.reshape(queries.shape),
        grad_values.reshape(queries.shape),
        grad_weight,
        grad_gain_query.reshape(HD),
        grad_gain_key.reshape(HD),
    )


def solution(mesh):
    planes = 4 if mesh.shape["dp"] == 16 else mesh.shape["dp"]
    fine = Mesh(
        mesh.devices.reshape(planes, mesh.shape["dp"] // planes, -1, 2), ("x", "z", "y", "core")
    )
    tokens = P(("x", "z"), ("y", "core"), None, None)
    clips = P(("x", "z"))
    return jax.shard_map(
        local,
        mesh=fine,
        in_specs=(tokens, tokens, tokens, P(), P(), clips, clips, clips, P(), tokens),
        out_specs=(
            tokens,
            tokens,
            tokens,
            tokens,
            P(("x", "z", "y", "core"), None),
            P(),
            P(),
        ),
        check_vma=False,
    )
```

```python
import jax
import jax.numpy as jnp
import numpy as np
from jax import lax
from jax.experimental import pallas as pl
from jax.experimental.pallas import tpu as pltpu
from jax.sharding import Mesh
from jax.sharding import PartitionSpec as P

BF = jnp.bfloat16
F32 = jnp.float32
HD = 64
PW = 16
CELLS = 256
FRAMES = 8
LANES = 128
WIDE = 384
PAIRS = WIDE // LANES
CELLS_HERE = CELLS // FRAMES
BLOCK = 16
NEG = -1e30
SCALE = HD**-0.5
PARAMS = pltpu.CompilerParams(vmem_limit_bytes=56 * 1024 * 1024)
SMALL = pltpu.CompilerParams(vmem_limit_bytes=16 * 1024 * 1024)
MEDIUM = pltpu.CompilerParams(vmem_limit_bytes=24 * 1024 * 1024)
LARGE = pltpu.CompilerParams(vmem_limit_bytes=46 * 1024 * 1024)


def cost(microseconds):
    return pl.CostEstimate(flops=0, bytes_accessed=int(microseconds * 3.69e6), transcendentals=0)


SMEM = pl.BlockSpec(memory_space=pltpu.SMEM)
VMEM = pl.BlockSpec(memory_space=pltpu.VMEM)


def nn(left, right):
    return jnp.dot(left, right, preferred_element_type=F32)


def nt(left, right):
    return lax.dot_general(left, right, (((1,), (1,)), ((), ())), preferred_element_type=F32)


def tn(left, right):
    return lax.dot_general(left, right, (((0,), (0,)), ((), ())), preferred_element_type=F32)


def low_lanes(shape):
    return lax.broadcasted_iota(jnp.int32, shape, len(shape) - 1) < HD


def stack_heads(pair):
    low = low_lanes((1, LANES)).astype(F32)
    return jnp.concatenate([pair * low.astype(BF), pair * (1.0 - low).astype(BF)], 0)


def pick_heads(stacked):
    half = stacked.shape[0] // 2
    return jnp.where(low_lanes((half, LANES)), stacked[:half], stacked[half:])


def softmax_rows(scores):
    grouped = scores.reshape(2, scores.shape[0] // 2, scores.shape[1])
    expo = jnp.exp(grouped - jnp.max(grouped, 1, keepdims=True))
    return expo * (1.0 / jnp.sum(expo, 1, keepdims=True))


def score_back(chances, dchances):
    grouped = dchances.reshape(chances.shape)
    total = jnp.sum(chances * grouped, 1, keepdims=True)
    return (chances * (grouped - total)).astype(BF).reshape(dchances.shape)


def cell_ok(cells, height, width):
    row = lax.shift_right_logical(cells, 4)
    return (row < height) & ((cells & (PW - 1)) < width)


def head_ones(rows, columns):
    row = lax.broadcasted_iota(jnp.int32, (rows, columns), 0) & (columns - 1)
    column = lax.broadcasted_iota(jnp.int32, (rows, columns), 1)
    same = lax.shift_right_logical(row, 6) == lax.shift_right_logical(column, 6)
    return jnp.where(same, 1.0, 0.0).astype(BF)


def head_mean(tensor, twice):
    high = tensor.astype(BF)
    rest = (tensor - high.astype(F32)).astype(BF)
    return nn(jnp.concatenate([high, rest], 1), twice) * (1.0 / HD)


def hat_of(raw, ones, twice):
    centre = raw.astype(F32) - nn(raw, ones) * (1.0 / HD)
    hats, inverses = [], []
    for left in range(0, raw.shape[1], LANES):
        part = centre[:, left : left + LANES]
        inverse = lax.rsqrt(head_mean(part * part, twice) + 1e-06)
        hats.append(part * inverse)
        inverses.append(inverse)
    return hats, inverses


def both_heads(gain_ref):
    return jnp.concatenate([gain_ref[...], gain_ref[...]], 1)


def pair_slice(number):
    return slice(number * LANES, (number + 1) * LANES)


NORM_WIDE = 512
DUO = 2 * LANES


def norm_kernel(q_ref, k_ref, gain_q_ref, gain_k_ref, out_ref):
    ones, twice = head_ones(DUO, DUO), head_ones(DUO, LANES)
    gains = both_heads(gain_q_ref), both_heads(gain_k_ref)
    for left in range(0, NORM_WIDE, DUO):
        for number, source in enumerate((q_ref, k_ref)):
            hats, _ = hat_of(source[:, left : left + DUO], ones, twice)
            for pair, hat in enumerate(hats):
                normed = (hat * gains[number]).astype(BF)
                if number == 0:
                    normed = normed * jnp.asarray(SCALE, BF)
                at = slice(left + pair * LANES, left + (pair + 1) * LANES)
                out_ref[:, number, :, at] = normed.reshape(FRAMES, CELLS_HERE, LANES)


def norm(queries, keys, gain_query, gain_key):
    inner = queries.shape[1]
    tokens = pl.BlockSpec((CELLS, NORM_WIDE), lambda n: (0, n))
    gain = pl.BlockSpec((1, HD), lambda n: (0, 0))
    return pl.pallas_call(
        norm_kernel,
        grid=(inner // NORM_WIDE,),
        in_specs=[tokens, tokens, gain, gain],
        out_specs=pl.BlockSpec((FRAMES, 2, CELLS_HERE, NORM_WIDE), lambda n: (0, 0, 0, n)),
        out_shape=jax.ShapeDtypeStruct((FRAMES, 2, CELLS_HERE, inner), BF),
        compiler_params=PARAMS,
        cost_estimate=cost(5),
        name="norm",
    )(queries, keys, gain_query, gain_key)


def hats_kernel(q_ref, k_ref, *out_refs):
    ones, twice = head_ones(DUO, DUO), head_ones(DUO, LANES)
    for left in range(0, NORM_WIDE, DUO):
        for number, source in enumerate((q_ref, k_ref)):
            hats, inverses = hat_of(source[:, left : left + DUO], ones, twice)
            at = slice(left, left + DUO)
            out_refs[number][:, at] = jnp.concatenate(hats, 1)
            out_refs[2 + number][:, at] = jnp.concatenate(inverses, 1)


def hats_of(queries, keys):
    inner = queries.shape[1]
    tokens = pl.BlockSpec((CELLS, NORM_WIDE), lambda n: (0, n))
    return pl.pallas_call(
        hats_kernel,
        grid=(inner // NORM_WIDE,),
        in_specs=[tokens, tokens],
        out_specs=[tokens] * 4,
        out_shape=[jax.ShapeDtypeStruct((CELLS, inner), F32)] * 4,
        compiler_params=PARAMS,
        cost_estimate=cost(5.6),
        name="hats",
    )(queries, keys)


def space_kernel(counts_ref, qk_ref, v_ref, gm_ref, out_ref, chances_ref):
    height, width = counts_ref[1], counts_ref[2]
    frame_on = jnp.where(counts_ref[3] < counts_ref[0], 1.0, 0.0)
    key_cell = lax.broadcasted_iota(jnp.int32, (2 * CELLS, CELLS), 0) & (CELLS - 1)
    bias = jnp.where(cell_ok(key_cell, height, width), 0.0, NEG)
    cell = lax.broadcasted_iota(jnp.int32, (CELLS, LANES), 0)
    usable = cell_ok(cell, height, width).astype(F32) * frame_on
    scores = []
    for pair in range(PAIRS):
        query = qk_ref[:, 0, :, pair_slice(pair)].reshape(CELLS, LANES)
        key = qk_ref[:, 1, :, pair_slice(pair)].reshape(CELLS, LANES)
        scores.append(nt(stack_heads(key), query) + bias)
    weights = []
    for pair in range(PAIRS):
        probs = softmax_rows(scores[pair]).reshape(scores[pair].shape)
        chances_ref[pair] = probs
        weights.append(probs.astype(BF))
    for pair in range(PAIRS):
        mixed = tn(weights[pair], stack_heads(v_ref[:, pair_slice(pair)]))
        mixed = (mixed * usable).astype(BF)
        out_ref[:, 0, :, pair_slice(pair)] = mixed.reshape(FRAMES, CELLS_HERE, LANES)
    out_ref[:, 1] = gm_ref[...].reshape(FRAMES, CELLS_HERE, WIDE)


def space_forward(counts, normed, values, grad_mixed):
    inner = values.shape[1]
    tokens = pl.BlockSpec((CELLS, WIDE), lambda n: (0, n))
    return pl.pallas_call(
        space_kernel,
        grid=(inner // WIDE,),
        in_specs=[
            SMEM,
            pl.BlockSpec((FRAMES, 2, CELLS_HERE, WIDE), lambda n: (0, 0, 0, n)),
            tokens,
            tokens,
        ],
        out_specs=[
            pl.BlockSpec((FRAMES, 2, CELLS_HERE, WIDE), lambda n: (0, 0, 0, n)),
            pl.BlockSpec((PAIRS, 2 * CELLS, CELLS), lambda n: (n, 0, 0)),
        ],
        out_shape=[
            jax.ShapeDtypeStruct((FRAMES, 2, CELLS_HERE, inner), BF),
            jax.ShapeDtypeStruct((inner // LANES, 2 * CELLS, CELLS), F32),
        ],
        compiler_params=PARAMS,
        cost_estimate=cost(7),
        name="space_forward",
    )(counts, normed, values, grad_mixed)


def gain_part(grad, normed):
    return jnp.sum(grad * normed.astype(F32), 0, keepdims=True)


def add_gains(sums_ref, of_query, of_key, begin=None):
    @pl.when(pl.program_id(0) == 0)
    def _():
        sums_ref[...] = jnp.zeros_like(sums_ref) if begin is None else begin()

    sums_ref[0:1] += of_query
    sums_ref[1:2] += of_key


def space_back_kernel(
    late_ref,
    gain_q_ref,
    gain_k_ref,
    hat_q_ref,
    hat_k_ref,
    qk_ref,
    v_ref,
    up_ref,
    chances_ref,
    dq_ref,
    dk_ref,
    dv_ref,
    sums_ref,
):
    def late_gains():
        scale = [both_heads(gain_q_ref) * SCALE, both_heads(gain_k_ref)]
        return late_ref[...] / jnp.concatenate(scale + [jnp.ones((6, LANES), F32)], 0)

    of_query = jnp.zeros((1, LANES), F32)
    of_key = jnp.zeros((1, LANES), F32)
    slices = [pair_slice(pair) for pair in range(PAIRS)]
    queries = [qk_ref[:, 0, :, at].reshape(CELLS, LANES) for at in slices]
    keys = [stack_heads(qk_ref[:, 1, :, at].reshape(CELLS, LANES)) for at in slices]
    dchances = [nt(stack_heads(v_ref[:, at]), up_ref[:, at]) for at in slices]
    dscores = []
    for pair, at in enumerate(slices):
        probs = chances_ref[pair]
        dv_ref[:, at] = pick_heads(nn(probs.astype(BF), up_ref[:, at])).astype(BF)
        dscores.append(score_back(probs.reshape(2, CELLS, CELLS), dchances[pair]))
    for pair, at in enumerate(slices):
        dk = pick_heads(nn(dscores[pair], queries[pair]))
        dq = tn(dscores[pair], keys[pair]) * SCALE
        dk_ref[:, at] = dk
        dq_ref[:, at] = dq
        of_query += gain_part(dq, hat_q_ref[:, at])
        of_key += gain_part(dk, hat_k_ref[:, at])
    add_gains(sums_ref, of_query, of_key, late_gains)


def space_back(late_sums, gain_query, gain_key, hats, normed, values, upstream, chances):
    inner = values.shape[1]
    tokens = pl.BlockSpec((CELLS, WIDE), lambda n: (0, n))
    wide = jax.ShapeDtypeStruct((CELLS, inner), F32)
    return pl.pallas_call(
        space_back_kernel,
        grid=(inner // WIDE,),
        in_specs=[
            pl.BlockSpec((8, LANES), lambda n: (0, 0)),
            pl.BlockSpec((1, HD), lambda n: (0, 0)),
            pl.BlockSpec((1, HD), lambda n: (0, 0)),
            tokens,
            tokens,
            pl.BlockSpec((FRAMES, 2, CELLS_HERE, WIDE), lambda n: (0, 0, 0, n)),
            tokens,
            tokens,
            pl.BlockSpec((PAIRS, 2 * CELLS, CELLS), lambda n: (n, 0, 0)),
        ],
        out_specs=[tokens, tokens, tokens, pl.BlockSpec((8, LANES), lambda n: (0, 0))],
        out_shape=[
            wide,
            wide,
            jax.ShapeDtypeStruct((CELLS, inner), BF),
            jax.ShapeDtypeStruct((8, LANES), F32),
        ],
        compiler_params=LARGE,
        cost_estimate=cost(9),
        name="space_back",
    )(late_sums, gain_query, gain_key, *hats, normed, values, upstream, chances)


def time_bias(frame_total):
    key = lax.broadcasted_iota(jnp.int32, (2 * LANES, LANES), 0) & (LANES - 1)
    query = lax.broadcasted_iota(jnp.int32, (2 * LANES, LANES), 1)
    same = (key & (BLOCK - 1)) == (query & (BLOCK - 1))
    return jnp.where(same & (lax.shift_right_logical(key, 4) < frame_total), 0.0, NEG)


def time_usable(counts_ref, block):
    row = lax.broadcasted_iota(jnp.int32, (LANES, LANES), 0)
    cell = counts_ref[3] * CELLS_HERE + block * BLOCK + (row & (BLOCK - 1))
    on = cell_ok(cell, counts_ref[1], counts_ref[2])
    return (on & (lax.shift_right_logical(row, 4) < counts_ref[0])).astype(F32)


def time_blocks():
    for block in range(CELLS_HERE // BLOCK):
        for pair in range(PAIRS):
            yield block, slice(block * BLOCK, (block + 1) * BLOCK), pair_slice(pair)


def time_kernel(counts_ref, qk_ref, sg_ref, out_ref):
    bias = time_bias(counts_ref[0])
    usable = [time_usable(counts_ref, block) for block in range(CELLS_HERE // BLOCK)]
    scores = []
    for block, rows, at in time_blocks():
        query = qk_ref[:, 0, rows, at].reshape(LANES, LANES)
        keys = stack_heads(qk_ref[:, 1, rows, at].reshape(LANES, LANES))
        scores.append(nt(keys, query) + bias)
    weights = [softmax_rows(part).astype(BF).reshape(part.shape) for part in scores]
    for number, (block, rows, at) in enumerate(time_blocks()):
        values = stack_heads(sg_ref[:, 0, rows, at].reshape(LANES, LANES))
        mixed = tn(weights[number], values) * usable[block]
        out_ref[:, rows, at] = mixed.astype(BF).reshape(FRAMES, BLOCK, LANES)


def time_back_kernel(counts_ref, qk_ref, sg_ref, dqk_ref, ds_ref, sums_ref):
    bias = time_bias(counts_ref[0])
    of_query = jnp.zeros((1, LANES), F32)
    of_key = jnp.zeros((1, LANES), F32)
    usable = [time_usable(counts_ref, block) for block in range(CELLS_HERE // BLOCK)]
    blocks = list(time_blocks())

    def load(ref, number, rows, at):
        return ref[:, number, rows, at].reshape(LANES, LANES)

    def shaped(tensor):
        return tensor.astype(BF).reshape(FRAMES, BLOCK, LANES)

    queries = [load(qk_ref, 0, rows, at) for _, rows, at in blocks]
    singles = [load(qk_ref, 1, rows, at) for _, rows, at in blocks]
    keys = [stack_heads(key) for key in singles]
    upstreams = [
        (load(sg_ref, 1, rows, at).astype(F32) * usable[block]).astype(BF)
        for block, rows, at in blocks
    ]
    scores = [nt(key, query) + bias for key, query in zip(keys, queries)]
    dchances = [
        nt(stack_heads(load(sg_ref, 0, rows, at)), upstream)
        for (_, rows, at), upstream in zip(blocks, upstreams)
    ]
    chances = [softmax_rows(part) for part in scores]
    dscores = [score_back(probs, part) for probs, part in zip(chances, dchances)]
    for number, (_, rows, at) in enumerate(blocks):
        weights = chances[number].astype(BF).reshape(2 * LANES, LANES)
        ds_ref[:, rows, at] = shaped(pick_heads(nn(weights, upstreams[number])))
        dq = tn(dscores[number], keys[number]) * SCALE
        dk = pick_heads(nn(dscores[number], queries[number]))
        dqk_ref[:, 0, rows, at] = shaped(dq)
        dqk_ref[:, 1, rows, at] = shaped(dk)
        of_query += gain_part(dq, queries[number])
        of_key += gain_part(dk, singles[number])
    add_gains(sums_ref, of_query, of_key)


def time_specs(inner):
    double = pl.BlockSpec((FRAMES, 2, CELLS_HERE, WIDE), lambda n: (0, 0, 0, n))
    single = pl.BlockSpec((FRAMES, CELLS_HERE, WIDE), lambda n: (0, 0, n))
    return (
        double,
        single,
        jax.ShapeDtypeStruct((FRAMES, 2, CELLS_HERE, inner), BF),
        jax.ShapeDtypeStruct((FRAMES, CELLS_HERE, inner), BF),
    )


def time_forward(counts, normed, arrived):
    inner = arrived.shape[3]
    double, single, _, single_shape = time_specs(inner)
    return pl.pallas_call(
        time_kernel,
        grid=(inner // WIDE,),
        in_specs=[SMEM, double, double],
        out_specs=single,
        out_shape=single_shape,
        compiler_params=SMALL,
        cost_estimate=cost(5),
        name="time_forward",
    )(counts, normed, arrived)


def time_back(counts, normed, arrived):
    inner = arrived.shape[3]
    double, single, double_shape, single_shape = time_specs(inner)
    return pl.pallas_call(
        time_back_kernel,
        grid=(inner // WIDE,),
        in_specs=[SMEM, double, double],
        out_specs=[double, single, pl.BlockSpec((8, LANES), lambda n: (0, 0))],
        out_shape=[double_shape, single_shape, jax.ShapeDtypeStruct((8, LANES), F32)],
        compiler_params=SMALL,
        cost_estimate=cost(6.5),
        name="time_back",
    )(counts, normed, arrived)


def norm_back_kernel(
    hat_q_ref,
    hat_k_ref,
    inverse_q_ref,
    inverse_k_ref,
    gain_q_ref,
    gain_k_ref,
    dq_ref,
    dk_ref,
    late_ref,
    gq_ref,
    gk_ref,
):
    twice = head_ones(DUO, LANES)
    for left in range(0, NORM_WIDE, LANES):
        at = slice(left, left + LANES)
        for number, (hat_ref, inverse_ref, gain_ref, early, target) in enumerate(
            (
                (hat_q_ref, inverse_q_ref, gain_q_ref, dq_ref, gq_ref),
                (hat_k_ref, inverse_k_ref, gain_k_ref, dk_ref, gk_ref),
            )
        ):
            hat = hat_ref[:, at]
            late = late_ref[:, number, :, at].reshape(CELLS, LANES)
            scaled = (early[:, at] + late.astype(F32)) * both_heads(gain_ref)
            mean = head_mean(scaled, twice)
            dinput = scaled - mean - hat * head_mean(scaled * hat, twice)
            target[:, at] = (inverse_ref[:, at] * dinput).astype(BF)


def norm_back(hats, gain_query, gain_key, dq, dk, late):
    inner = dq.shape[1]
    tokens = pl.BlockSpec((CELLS, NORM_WIDE), lambda n: (0, n))
    gain = pl.BlockSpec((1, HD), lambda n: (0, 0))
    grads = jax.ShapeDtypeStruct((CELLS, inner), BF)
    return pl.pallas_call(
        norm_back_kernel,
        grid=(inner // NORM_WIDE,),
        in_specs=[
            tokens,
            tokens,
            tokens,
            tokens,
            gain,
            gain,
            tokens,
            tokens,
            pl.BlockSpec((FRAMES, 2, CELLS_HERE, NORM_WIDE), lambda n: (0, 0, 0, n)),
        ],
        out_specs=[tokens, tokens],
        out_shape=[grads, grads],
        compiler_params=PARAMS,
        cost_estimate=cost(7),
        name="norm_back",
    )(*hats, gain_query, gain_key, dq, dk, late)


def grad_mixed_kernel(cot_ref, weight_ref, out_ref):
    out_ref[...] = nt(cot_ref[...], weight_ref[...]).astype(BF)


def grad_mixed_of(cotangent, weight):
    inner, width = weight.shape
    return pl.pallas_call(
        grad_mixed_kernel,
        grid=(inner // WIDE,),
        in_specs=[
            pl.BlockSpec((CELLS, width), lambda n: (0, 0)),
            pl.BlockSpec((WIDE, width), lambda n: (n, 0)),
        ],
        out_specs=pl.BlockSpec((CELLS, WIDE), lambda n: (0, n)),
        out_shape=jax.ShapeDtypeStruct((CELLS, inner), BF),
        compiler_params=PARAMS,
        cost_estimate=cost(8.7),
        name="grad_mixed",
    )(cotangent, weight)


def project_kernel(mixed_ref, weight_ref, out_ref):
    out_ref[...] = nn(mixed_ref[...], weight_ref[...]).astype(BF)


def project(mixed, weight):
    inner, width = weight.shape
    block = width // 4
    return pl.pallas_call(
        project_kernel,
        grid=(4,),
        in_specs=[
            pl.BlockSpec((CELLS, inner), lambda n: (0, 0)),
            pl.BlockSpec((inner, block), lambda n: (0, n)),
        ],
        out_specs=pl.BlockSpec((CELLS, block), lambda n: (0, n)),
        out_shape=jax.ShapeDtypeStruct((CELLS, width), BF),
        compiler_params=PARAMS,
        cost_estimate=cost(7),
        name="project",
    )(mixed, weight)


PIECES = 6
STEPS = 3
TAIL = 8


def gain_rows(gain_refs, block):
    total = gain_refs[0][...]
    for gain_ref in gain_refs[1:]:
        total = total + gain_ref[...]
    terms = []
    for row in range(2):
        rest = total[row : row + 1]
        for _ in range(3):
            terms.append(rest.astype(BF).astype(F32))
            rest = rest - terms[-1]
    rows = jnp.concatenate(terms + [jnp.zeros((TAIL - 6, LANES), F32)], 0)
    return jnp.concatenate([rows, jnp.zeros((TAIL, block - LANES), F32)], 1).astype(BF)


def weight_kernel(place_ref, order_ref, mixed_ref, cot_ref, *refs):
    *gain_refs, out_ref, turned, product = refs
    shares, rows, block = out_ref.shape
    own = product.shape[0] // shares

    @pl.when(pl.program_id(0) == 0)
    def _():
        turned[...] = nt(order_ref[0], mixed_ref[...]).astype(BF)
        tail = gain_rows(gain_refs, block)
        for share in range(shares):
            out_ref[share, rows - TAIL :] = tail

    product[...] = nn(turned[...], cot_ref[...])
    for step in range(STEPS):

        @pl.when(pl.program_id(0) == step)
        def _():
            for share in range(shares):
                for half in range(PIECES // STEPS):
                    top = (step * (PIECES // STEPS) + half) * own
                    out_ref[share, top : top + own] = product[
                        share * own : (share + 1) * own, half * block : (half + 1) * block
                    ].astype(BF)


def weight_parts(counts, order, mixed, cotangents, gain_sums, shares):
    tokens, width = cotangents.shape
    _, features, wide = order.shape
    block = width // PIECES
    columns = width // STEPS
    rows = -(-(PIECES * (features // shares) + TAIL) // 16) * 16
    gain = pl.BlockSpec((8, LANES), lambda n, place: (0, 0))
    return pl.pallas_call(
        weight_kernel,
        grid_spec=pltpu.PrefetchScalarGridSpec(
            num_scalar_prefetch=1,
            grid=(STEPS,),
            in_specs=[
                pl.BlockSpec((1, features, wide), lambda n, place: (place[5], 0, 0)),
                pl.BlockSpec((tokens, wide), lambda n, place: (0, place[4])),
                pl.BlockSpec((tokens, columns), lambda n, place: (0, n)),
            ]
            + [gain] * len(gain_sums),
            out_specs=pl.BlockSpec((shares, rows, block), lambda n, place: (0, 0, 0)),
            scratch_shapes=[
                pltpu.VMEM((features, tokens), BF),
                pltpu.VMEM((features, columns), F32),
            ],
        ),
        out_shape=jax.ShapeDtypeStruct((shares, rows, block), BF),
        compiler_params=MEDIUM,
        cost_estimate=cost(9.5),
        name="weight_parts",
    )(counts, order, mixed, cotangents, *gain_sums)


def sum_kernel(parts_ref, out_ref, gain_q_ref, gain_k_ref):
    shares, rows, block = parts_ref.shape
    own = out_ref.shape[0]
    total = parts_ref[0].astype(F32)
    for share in range(1, shares):
        total = total + parts_ref[share].astype(F32)
    for piece in range(PIECES):
        out_ref[:, piece * block : (piece + 1) * block] = total[piece * own : (piece + 1) * own]
    tail = total[rows - TAIL :, :LANES]
    for number, gain_ref in enumerate((gain_q_ref, gain_k_ref)):
        gain = jnp.sum(tail[3 * number : 3 * number + 3], 0, keepdims=True)
        gain_ref[...] = gain[:, :HD] + gain[:, HD:]


def sum_parts(parts, own):
    block = parts.shape[2]
    gain = jax.ShapeDtypeStruct((1, HD), F32)
    return pl.pallas_call(
        sum_kernel,
        in_specs=[VMEM],
        out_specs=[VMEM] * 3,
        out_shape=[jax.ShapeDtypeStruct((own, PIECES * block), F32), gain, gain],
        compiler_params=SMALL,
        cost_estimate=cost(2.2),
        name="sum_parts",
    )(parts)


def feature_order(inner, planes, cores, shares):
    wide = inner // planes
    features = wide // cores
    own = features // shares
    order = np.zeros((cores, features, wide), np.float32)
    for core in range(cores):
        for feature in range(features):
            share, row = divmod(feature, own)
            order[core, feature, own * (cores * share + core) + row] = 1.0
    return jnp.asarray(order, BF)


def local(
    queries,
    keys_proj,
    values_proj,
    gain_query,
    gain_key,
    frame_counts,
    heights,
    widths,
    out_weight,
    cotangent,
):
    seq = ("y", "core")
    group = ("x", "core")
    sums = ("z", "y")
    planes, cores = lax.axis_size("x"), lax.axis_size("core")
    shares = lax.axis_size("z") * lax.axis_size("y")
    inner = out_weight.shape[0]
    rank = lax.axis_index(seq).astype(jnp.int32)
    place = [lax.axis_index("x").astype(jnp.int32), lax.axis_index("core").astype(jnp.int32)]
    counts = jnp.stack([frame_counts[0], heights[0], widths[0], rank, *place])
    gains = gain_query.reshape(1, HD), gain_key.reshape(1, HD)
    query_rows, key_rows, value_rows = queries[0, 0], keys_proj[0, 0], values_proj[0, 0]
    cot_rows = cotangent[0, 0]
    by_cells = (FRAMES, CELLS_HERE, inner)

    def exchange(tensor, axes):
        return lax.all_to_all(tensor, axes, split_axis=0, concat_axis=0, tiled=True)

    def after(tensor, earlier):
        return lax.optimization_barrier((tensor, earlier))[0]

    cotangents = lax.all_gather(cot_rows, group, axis=0, tiled=True)
    normed = norm(query_rows, key_rows, *gains)
    normed_cells = exchange(normed, seq)
    grad_mixed = grad_mixed_of(cot_rows, out_weight)
    outgoing, chances = space_forward(counts, normed, value_rows, grad_mixed)
    arrived = exchange(after(outgoing, normed_cells), seq)
    hats = hats_of(*lax.optimization_barrier((query_rows, key_rows, outgoing))[:2])
    arrived, *hats = lax.optimization_barrier((arrived, *hats))
    mixed_cells = time_forward(counts, normed_cells, arrived)
    mixed = exchange(mixed_cells, seq).reshape(CELLS, inner)
    late_cells, dspatial_cells, late_gains = time_back(counts, normed_cells, arrived)
    first = (cotangents, dspatial_cells)
    gathered = lax.all_gather(after(mixed, first), group, axis=0, tiled=True)
    dspatial = exchange(after(dspatial_cells, mixed), seq).reshape(CELLS, inner)
    late = exchange(after(late_cells, dspatial), seq)
    block_out = project(mixed, out_weight)
    dq, dk, grad_values, gain_sums = space_back(
        late_gains, *gains, hats[:2], normed, value_rows, dspatial, chances
    )
    for flip in range(1, cores):
        pairs = [(i, (i + flip) % cores) for i in range(cores)]
        gain_sums = gain_sums + lax.ppermute(gain_sums, "core", pairs)
    gain_sums = [gain_sums] + [
        lax.ppermute(gain_sums, "x", [(i, (i + step) % planes) for i in range(planes)])
        for step in range(1, planes)
    ]
    grad_queries, grad_keys = norm_back(hats, *gains, dq, dk, late)
    order = feature_order(inner, planes, cores, shares)
    parts = weight_parts(counts, order, gathered, cotangents, gain_sums, shares)
    parts = exchange(after(parts, late), sums)
    own = order.shape[1] // shares
    grad_weight, grad_gain_query, grad_gain_key = sum_parts(parts, own)
    return (
        block_out.reshape(cotangent.shape),
        grad_queries.reshape(queries.shape),
        grad_keys.reshape(queries.shape),
        grad_values.reshape(queries.shape),
        grad_weight,
        grad_gain_query.reshape(HD),
        grad_gain_key.reshape(HD),
    )


def solution(mesh):
    planes = 4 if mesh.shape["dp"] == 16 else mesh.shape["dp"]
    fine = Mesh(
        mesh.devices.reshape(planes, mesh.shape["dp"] // planes, -1, 2), ("x", "z", "y", "core")
    )
    tokens = P(("x", "z"), ("y", "core"), None, None)
    clips = P(("x", "z"))
    return jax.shard_map(
        local,
        mesh=fine,
        in_specs=(tokens, tokens, tokens, P(), P(), clips, clips, clips, P(), tokens),
        out_specs=(
            tokens,
            tokens,
            tokens,
            tokens,
            P(("x", "z", "y", "core"), None),
            P(),
            P(),
        ),
        check_vma=False,
    )
```

```python
import jax
import jax.numpy as jnp
import numpy as np
from jax import lax
from jax.experimental import pallas as pl
from jax.experimental.pallas import tpu as pltpu
from jax.sharding import Mesh
from jax.sharding import PartitionSpec as P

BF = jnp.bfloat16
F32 = jnp.float32
HD = 64
PW = 16
CELLS = 256
FRAMES = 8
LANES = 128
WIDE = 384
PAIRS = WIDE // LANES
CELLS_HERE = CELLS // FRAMES
BLOCK = 16
NEG = -1e30
SCALE = HD**-0.5
PARAMS = pltpu.CompilerParams(vmem_limit_bytes=56 * 1024 * 1024)
SMALL = pltpu.CompilerParams(vmem_limit_bytes=16 * 1024 * 1024)


def cost(microseconds):
    return pl.CostEstimate(flops=0, bytes_accessed=int(microseconds * 3.69e6), transcendentals=0)


SMEM = pl.BlockSpec(memory_space=pltpu.SMEM)
VMEM = pl.BlockSpec(memory_space=pltpu.VMEM)


def nn(left, right):
    return jnp.dot(left, right, preferred_element_type=F32)


def nt(left, right):
    return lax.dot_general(left, right, (((1,), (1,)), ((), ())), preferred_element_type=F32)


def tn(left, right):
    return lax.dot_general(left, right, (((0,), (0,)), ((), ())), preferred_element_type=F32)


def low_lanes(shape):
    return lax.broadcasted_iota(jnp.int32, shape, len(shape) - 1) < HD


def stack_heads(pair):
    low = low_lanes((1, LANES)).astype(F32)
    return jnp.concatenate([pair * low.astype(BF), pair * (1.0 - low).astype(BF)], 0)


def pick_heads(stacked):
    half = stacked.shape[0] // 2
    return jnp.where(low_lanes((half, LANES)), stacked[:half], stacked[half:])


def softmax_rows(scores):
    grouped = scores.reshape(2, scores.shape[0] // 2, scores.shape[1])
    expo = jnp.exp(grouped - jnp.max(grouped, 1, keepdims=True))
    return expo * (1.0 / jnp.sum(expo, 1, keepdims=True))


def score_back(chances, dchances):
    grouped = dchances.reshape(chances.shape)
    total = jnp.sum(chances * grouped, 1, keepdims=True)
    return (chances * (grouped - total)).astype(BF).reshape(dchances.shape)


def cell_ok(cells, height, width):
    row = lax.shift_right_logical(cells, 4)
    return (row < height) & ((cells & (PW - 1)) < width)


def head_ones(rows, columns):
    row = lax.broadcasted_iota(jnp.int32, (rows, columns), 0) & (columns - 1)
    column = lax.broadcasted_iota(jnp.int32, (rows, columns), 1)
    same = lax.shift_right_logical(row, 6) == lax.shift_right_logical(column, 6)
    return jnp.where(same, 1.0, 0.0).astype(BF)


def head_mean(tensor, twice):
    high = tensor.astype(BF)
    rest = (tensor - high.astype(F32)).astype(BF)
    return nn(jnp.concatenate([high, rest], 1), twice) * (1.0 / HD)


def hat_of(raw, ones, twice):
    centre = raw.astype(F32) - nn(raw, ones) * (1.0 / HD)
    hats, inverses = [], []
    for left in range(0, raw.shape[1], LANES):
        part = centre[:, left : left + LANES]
        inverse = lax.rsqrt(head_mean(part * part, twice) + 1e-06)
        hats.append(part * inverse)
        inverses.append(inverse)
    return hats, inverses


def both_heads(gain_ref):
    return jnp.concatenate([gain_ref[...], gain_ref[...]], 1)


def pair_slice(number):
    return slice(number * LANES, (number + 1) * LANES)


NORM_WIDE = 512
DUO = 2 * LANES


def norm_kernel(q_ref, k_ref, gain_q_ref, gain_k_ref, out_ref):
    ones, twice = head_ones(DUO, DUO), head_ones(DUO, LANES)
    gains = both_heads(gain_q_ref), both_heads(gain_k_ref)
    for left in range(0, NORM_WIDE, DUO):
        for number, source in enumerate((q_ref, k_ref)):
            hats, _ = hat_of(source[:, left : left + DUO], ones, twice)
            for pair, hat in enumerate(hats):
                normed = (hat * gains[number]).astype(BF)
                if number == 0:
                    normed = normed * jnp.asarray(SCALE, BF)
                at = slice(left + pair * LANES, left + (pair + 1) * LANES)
                out_ref[:, number, :, at] = normed.reshape(FRAMES, CELLS_HERE, LANES)


def norm(queries, keys, gain_query, gain_key):
    inner = queries.shape[1]
    tokens = pl.BlockSpec((CELLS, NORM_WIDE), lambda n: (0, n))
    gain = pl.BlockSpec((1, HD), lambda n: (0, 0))
    return pl.pallas_call(
        norm_kernel,
        grid=(inner // NORM_WIDE,),
        in_specs=[tokens, tokens, gain, gain],
        out_specs=pl.BlockSpec((FRAMES, 2, CELLS_HERE, NORM_WIDE), lambda n: (0, 0, 0, n)),
        out_shape=jax.ShapeDtypeStruct((FRAMES, 2, CELLS_HERE, inner), BF),
        compiler_params=PARAMS,
        cost_estimate=cost(5),
        name="norm",
    )(queries, keys, gain_query, gain_key)


def hats_kernel(q_ref, k_ref, *out_refs):
    ones, twice = head_ones(DUO, DUO), head_ones(DUO, LANES)
    for left in range(0, NORM_WIDE, DUO):
        for number, source in enumerate((q_ref, k_ref)):
            hats, inverses = hat_of(source[:, left : left + DUO], ones, twice)
            at = slice(left, left + DUO)
            out_refs[number][:, at] = jnp.concatenate(hats, 1)
            out_refs[2 + number][:, at] = jnp.concatenate(inverses, 1)


def hats_of(queries, keys):
    inner = queries.shape[1]
    tokens = pl.BlockSpec((CELLS, NORM_WIDE), lambda n: (0, n))
    return pl.pallas_call(
        hats_kernel,
        grid=(inner // NORM_WIDE,),
        in_specs=[tokens, tokens],
        out_specs=[tokens] * 4,
        out_shape=[jax.ShapeDtypeStruct((CELLS, inner), F32)] * 4,
        compiler_params=PARAMS,
        cost_estimate=cost(5.6),
        name="hats",
    )(queries, keys)


def space_kernel(counts_ref, qk_ref, v_ref, gm_ref, out_ref, chances_ref):
    height, width = counts_ref[1], counts_ref[2]
    frame_on = jnp.where(counts_ref[3] < counts_ref[0], 1.0, 0.0)
    key_cell = lax.broadcasted_iota(jnp.int32, (2 * CELLS, CELLS), 0) & (CELLS - 1)
    bias = jnp.where(cell_ok(key_cell, height, width), 0.0, NEG)
    cell = lax.broadcasted_iota(jnp.int32, (CELLS, LANES), 0)
    usable = cell_ok(cell, height, width).astype(F32) * frame_on
    scores = []
    for pair in range(PAIRS):
        query = qk_ref[:, 0, :, pair_slice(pair)].reshape(CELLS, LANES)
        key = qk_ref[:, 1, :, pair_slice(pair)].reshape(CELLS, LANES)
        scores.append(nt(stack_heads(key), query) + bias)
    weights = []
    for pair in range(PAIRS):
        probs = softmax_rows(scores[pair]).reshape(scores[pair].shape)
        chances_ref[pair] = probs
        weights.append(probs.astype(BF))
    for pair in range(PAIRS):
        mixed = tn(weights[pair], stack_heads(v_ref[:, pair_slice(pair)]))
        mixed = (mixed * usable).astype(BF)
        out_ref[:, 0, :, pair_slice(pair)] = mixed.reshape(FRAMES, CELLS_HERE, LANES)
    out_ref[:, 1] = gm_ref[...].reshape(FRAMES, CELLS_HERE, WIDE)


def space_forward(counts, normed, values, grad_mixed):
    inner = values.shape[1]
    tokens = pl.BlockSpec((CELLS, WIDE), lambda n: (0, n))
    return pl.pallas_call(
        space_kernel,
        grid=(inner // WIDE,),
        in_specs=[
            SMEM,
            pl.BlockSpec((FRAMES, 2, CELLS_HERE, WIDE), lambda n: (0, 0, 0, n)),
            tokens,
            tokens,
        ],
        out_specs=[
            pl.BlockSpec((FRAMES, 2, CELLS_HERE, WIDE), lambda n: (0, 0, 0, n)),
            pl.BlockSpec((PAIRS, 2 * CELLS, CELLS), lambda n: (n, 0, 0)),
        ],
        out_shape=[
            jax.ShapeDtypeStruct((FRAMES, 2, CELLS_HERE, inner), BF),
            jax.ShapeDtypeStruct((inner // LANES, 2 * CELLS, CELLS), F32),
        ],
        compiler_params=PARAMS,
        cost_estimate=cost(7),
        name="space_forward",
    )(counts, normed, values, grad_mixed)


def gain_part(grad, normed):
    return jnp.sum(grad * normed.astype(F32), 0, keepdims=True)


def add_gains(sums_ref, of_query, of_key, begin=None):
    @pl.when(pl.program_id(0) == 0)
    def _():
        sums_ref[...] = jnp.zeros_like(sums_ref) if begin is None else begin()

    sums_ref[0:1] += of_query
    sums_ref[1:2] += of_key


def space_back_kernel(
    late_ref,
    gain_q_ref,
    gain_k_ref,
    hat_q_ref,
    hat_k_ref,
    qk_ref,
    v_ref,
    up_ref,
    chances_ref,
    dq_ref,
    dk_ref,
    dv_ref,
    sums_ref,
):
    def late_gains():
        scale = [both_heads(gain_q_ref) * SCALE, both_heads(gain_k_ref)]
        return late_ref[...] / jnp.concatenate(scale + [jnp.ones((6, LANES), F32)], 0)

    of_query = jnp.zeros((1, LANES), F32)
    of_key = jnp.zeros((1, LANES), F32)
    slices = [pair_slice(pair) for pair in range(PAIRS)]
    queries = [qk_ref[:, 0, :, at].reshape(CELLS, LANES) for at in slices]
    keys = [stack_heads(qk_ref[:, 1, :, at].reshape(CELLS, LANES)) for at in slices]
    dchances = [nt(stack_heads(v_ref[:, at]), up_ref[:, at]) for at in slices]
    dscores = []
    for pair, at in enumerate(slices):
        probs = chances_ref[pair]
        dv_ref[:, at] = pick_heads(nn(probs.astype(BF), up_ref[:, at])).astype(BF)
        dscores.append(score_back(probs.reshape(2, CELLS, CELLS), dchances[pair]))
    for pair, at in enumerate(slices):
        dk = pick_heads(nn(dscores[pair], queries[pair]))
        dq = tn(dscores[pair], keys[pair]) * SCALE
        dk_ref[:, at] = dk
        dq_ref[:, at] = dq
        of_query += gain_part(dq, hat_q_ref[:, at])
        of_key += gain_part(dk, hat_k_ref[:, at])
    add_gains(sums_ref, of_query, of_key, late_gains)


def space_back(late_sums, gain_query, gain_key, hats, normed, values, upstream, chances):
    inner = values.shape[1]
    tokens = pl.BlockSpec((CELLS, WIDE), lambda n: (0, n))
    wide = jax.ShapeDtypeStruct((CELLS, inner), F32)
    return pl.pallas_call(
        space_back_kernel,
        grid=(inner // WIDE,),
        in_specs=[
            pl.BlockSpec((8, LANES), lambda n: (0, 0)),
            pl.BlockSpec((1, HD), lambda n: (0, 0)),
            pl.BlockSpec((1, HD), lambda n: (0, 0)),
            tokens,
            tokens,
            pl.BlockSpec((FRAMES, 2, CELLS_HERE, WIDE), lambda n: (0, 0, 0, n)),
            tokens,
            tokens,
            pl.BlockSpec((PAIRS, 2 * CELLS, CELLS), lambda n: (n, 0, 0)),
        ],
        out_specs=[tokens, tokens, tokens, pl.BlockSpec((8, LANES), lambda n: (0, 0))],
        out_shape=[
            wide,
            wide,
            jax.ShapeDtypeStruct((CELLS, inner), BF),
            jax.ShapeDtypeStruct((8, LANES), F32),
        ],
        compiler_params=PARAMS,
        cost_estimate=cost(9),
        name="space_back",
    )(late_sums, gain_query, gain_key, *hats, normed, values, upstream, chances)


def time_bias(frame_total):
    key = lax.broadcasted_iota(jnp.int32, (2 * LANES, LANES), 0) & (LANES - 1)
    query = lax.broadcasted_iota(jnp.int32, (2 * LANES, LANES), 1)
    same = (key & (BLOCK - 1)) == (query & (BLOCK - 1))
    return jnp.where(same & (lax.shift_right_logical(key, 4) < frame_total), 0.0, NEG)


def time_usable(counts_ref, block):
    row = lax.broadcasted_iota(jnp.int32, (LANES, LANES), 0)
    cell = counts_ref[3] * CELLS_HERE + block * BLOCK + (row & (BLOCK - 1))
    on = cell_ok(cell, counts_ref[1], counts_ref[2])
    return (on & (lax.shift_right_logical(row, 4) < counts_ref[0])).astype(F32)


def time_blocks():
    for block in range(CELLS_HERE // BLOCK):
        for pair in range(PAIRS):
            yield block, slice(block * BLOCK, (block + 1) * BLOCK), pair_slice(pair)


def time_kernel(counts_ref, qk_ref, sg_ref, out_ref):
    bias = time_bias(counts_ref[0])
    usable = [time_usable(counts_ref, block) for block in range(CELLS_HERE // BLOCK)]
    scores = []
    for block, rows, at in time_blocks():
        query = qk_ref[:, 0, rows, at].reshape(LANES, LANES)
        keys = stack_heads(qk_ref[:, 1, rows, at].reshape(LANES, LANES))
        scores.append(nt(keys, query) + bias)
    weights = [softmax_rows(part).astype(BF).reshape(part.shape) for part in scores]
    for number, (block, rows, at) in enumerate(time_blocks()):
        values = stack_heads(sg_ref[:, 0, rows, at].reshape(LANES, LANES))
        mixed = tn(weights[number], values) * usable[block]
        out_ref[:, rows, at] = mixed.astype(BF).reshape(FRAMES, BLOCK, LANES)


def time_back_kernel(counts_ref, qk_ref, sg_ref, dqk_ref, ds_ref, sums_ref):
    bias = time_bias(counts_ref[0])
    of_query = jnp.zeros((1, LANES), F32)
    of_key = jnp.zeros((1, LANES), F32)
    usable = [time_usable(counts_ref, block) for block in range(CELLS_HERE // BLOCK)]
    blocks = list(time_blocks())

    def load(ref, number, rows, at):
        return ref[:, number, rows, at].reshape(LANES, LANES)

    def shaped(tensor):
        return tensor.astype(BF).reshape(FRAMES, BLOCK, LANES)

    queries = [load(qk_ref, 0, rows, at) for _, rows, at in blocks]
    singles = [load(qk_ref, 1, rows, at) for _, rows, at in blocks]
    keys = [stack_heads(key) for key in singles]
    upstreams = [
        (load(sg_ref, 1, rows, at).astype(F32) * usable[block]).astype(BF)
        for block, rows, at in blocks
    ]
    scores = [nt(key, query) + bias for key, query in zip(keys, queries)]
    dchances = [
        nt(stack_heads(load(sg_ref, 0, rows, at)), upstream)
        for (_, rows, at), upstream in zip(blocks, upstreams)
    ]
    chances = [softmax_rows(part) for part in scores]
    dscores = [score_back(probs, part) for probs, part in zip(chances, dchances)]
    for number, (_, rows, at) in enumerate(blocks):
        weights = chances[number].astype(BF).reshape(2 * LANES, LANES)
        ds_ref[:, rows, at] = shaped(pick_heads(nn(weights, upstreams[number])))
        dq = tn(dscores[number], keys[number]) * SCALE
        dk = pick_heads(nn(dscores[number], queries[number]))
        dqk_ref[:, 0, rows, at] = shaped(dq)
        dqk_ref[:, 1, rows, at] = shaped(dk)
        of_query += gain_part(dq, queries[number])
        of_key += gain_part(dk, singles[number])
    add_gains(sums_ref, of_query, of_key)


def time_specs(inner):
    double = pl.BlockSpec((FRAMES, 2, CELLS_HERE, WIDE), lambda n: (0, 0, 0, n))
    single = pl.BlockSpec((FRAMES, CELLS_HERE, WIDE), lambda n: (0, 0, n))
    return (
        double,
        single,
        jax.ShapeDtypeStruct((FRAMES, 2, CELLS_HERE, inner), BF),
        jax.ShapeDtypeStruct((FRAMES, CELLS_HERE, inner), BF),
    )


def time_forward(counts, normed, arrived):
    inner = arrived.shape[3]
    double, single, _, single_shape = time_specs(inner)
    return pl.pallas_call(
        time_kernel,
        grid=(inner // WIDE,),
        in_specs=[SMEM, double, double],
        out_specs=single,
        out_shape=single_shape,
        compiler_params=SMALL,
        cost_estimate=cost(5),
        name="time_forward",
    )(counts, normed, arrived)


def time_back(counts, normed, arrived):
    inner = arrived.shape[3]
    double, single, double_shape, single_shape = time_specs(inner)
    return pl.pallas_call(
        time_back_kernel,
        grid=(inner // WIDE,),
        in_specs=[SMEM, double, double],
        out_specs=[double, single, pl.BlockSpec((8, LANES), lambda n: (0, 0))],
        out_shape=[double_shape, single_shape, jax.ShapeDtypeStruct((8, LANES), F32)],
        compiler_params=SMALL,
        cost_estimate=cost(6.5),
        name="time_back",
    )(counts, normed, arrived)


def norm_back_kernel(
    hat_q_ref,
    hat_k_ref,
    inverse_q_ref,
    inverse_k_ref,
    gain_q_ref,
    gain_k_ref,
    dq_ref,
    dk_ref,
    late_ref,
    gq_ref,
    gk_ref,
):
    twice = head_ones(DUO, LANES)
    for left in range(0, NORM_WIDE, LANES):
        at = slice(left, left + LANES)
        for number, (hat_ref, inverse_ref, gain_ref, early, target) in enumerate(
            (
                (hat_q_ref, inverse_q_ref, gain_q_ref, dq_ref, gq_ref),
                (hat_k_ref, inverse_k_ref, gain_k_ref, dk_ref, gk_ref),
            )
        ):
            hat = hat_ref[:, at]
            late = late_ref[:, number, :, at].reshape(CELLS, LANES)
            scaled = (early[:, at] + late.astype(F32)) * both_heads(gain_ref)
            mean = head_mean(scaled, twice)
            dinput = scaled - mean - hat * head_mean(scaled * hat, twice)
            target[:, at] = (inverse_ref[:, at] * dinput).astype(BF)


def norm_back(hats, gain_query, gain_key, dq, dk, late):
    inner = dq.shape[1]
    tokens = pl.BlockSpec((CELLS, NORM_WIDE), lambda n: (0, n))
    gain = pl.BlockSpec((1, HD), lambda n: (0, 0))
    grads = jax.ShapeDtypeStruct((CELLS, inner), BF)
    return pl.pallas_call(
        norm_back_kernel,
        grid=(inner // NORM_WIDE,),
        in_specs=[
            tokens,
            tokens,
            tokens,
            tokens,
            gain,
            gain,
            tokens,
            tokens,
            pl.BlockSpec((FRAMES, 2, CELLS_HERE, NORM_WIDE), lambda n: (0, 0, 0, n)),
        ],
        out_specs=[tokens, tokens],
        out_shape=[grads, grads],
        compiler_params=PARAMS,
        cost_estimate=cost(7),
        name="norm_back",
    )(*hats, gain_query, gain_key, dq, dk, late)


def grad_mixed_kernel(cot_ref, weight_ref, out_ref):
    out_ref[...] = nt(cot_ref[...], weight_ref[...]).astype(BF)


def grad_mixed_of(cotangent, weight):
    inner, width = weight.shape
    return pl.pallas_call(
        grad_mixed_kernel,
        grid=(inner // WIDE,),
        in_specs=[
            pl.BlockSpec((CELLS, width), lambda n: (0, 0)),
            pl.BlockSpec((WIDE, width), lambda n: (n, 0)),
        ],
        out_specs=pl.BlockSpec((CELLS, WIDE), lambda n: (0, n)),
        out_shape=jax.ShapeDtypeStruct((CELLS, inner), BF),
        compiler_params=PARAMS,
        cost_estimate=cost(8.7),
        name="grad_mixed",
    )(cotangent, weight)


def project_kernel(mixed_ref, weight_ref, out_ref):
    out_ref[...] = nn(mixed_ref[...], weight_ref[...]).astype(BF)


def project(mixed, weight):
    inner, width = weight.shape
    block = width // 4
    return pl.pallas_call(
        project_kernel,
        grid=(4,),
        in_specs=[
            pl.BlockSpec((CELLS, inner), lambda n: (0, 0)),
            pl.BlockSpec((inner, block), lambda n: (0, n)),
        ],
        out_specs=pl.BlockSpec((CELLS, block), lambda n: (0, n)),
        out_shape=jax.ShapeDtypeStruct((CELLS, width), BF),
        compiler_params=PARAMS,
        cost_estimate=cost(7),
        name="project",
    )(mixed, weight)


PIECES = 6
STEPS = 3
TAIL = 8


def gain_rows(gain_refs, block):
    total = gain_refs[0][...]
    for gain_ref in gain_refs[1:]:
        total = total + gain_ref[...]
    terms = []
    for row in range(2):
        rest = total[row : row + 1]
        for _ in range(3):
            terms.append(rest.astype(BF).astype(F32))
            rest = rest - terms[-1]
    rows = jnp.concatenate(terms + [jnp.zeros((TAIL - 6, LANES), F32)], 0)
    return jnp.concatenate([rows, jnp.zeros((TAIL, block - LANES), F32)], 1).astype(BF)


def weight_kernel(place_ref, order_ref, mixed_ref, cot_ref, *refs):
    *gain_refs, out_ref, turned, product = refs
    shares, rows, block = out_ref.shape
    own = product.shape[0] // shares

    @pl.when(pl.program_id(0) == 0)
    def _():
        turned[...] = nt(order_ref[0], mixed_ref[...]).astype(BF)
        tail = gain_rows(gain_refs, block)
        for share in range(shares):
            out_ref[share, rows - TAIL :] = tail

    product[...] = nn(turned[...], cot_ref[...])
    for step in range(STEPS):

        @pl.when(pl.program_id(0) == step)
        def _():
            for share in range(shares):
                for half in range(PIECES // STEPS):
                    top = (step * (PIECES // STEPS) + half) * own
                    out_ref[share, top : top + own] = product[
                        share * own : (share + 1) * own, half * block : (half + 1) * block
                    ].astype(BF)


def weight_parts(counts, order, mixed, cotangents, gain_sums, shares):
    tokens, width = cotangents.shape
    _, features, wide = order.shape
    block = width // PIECES
    columns = width // STEPS
    rows = -(-(PIECES * (features // shares) + TAIL) // 16) * 16
    gain = pl.BlockSpec((8, LANES), lambda n, place: (0, 0))
    return pl.pallas_call(
        weight_kernel,
        grid_spec=pltpu.PrefetchScalarGridSpec(
            num_scalar_prefetch=1,
            grid=(STEPS,),
            in_specs=[
                pl.BlockSpec((1, features, wide), lambda n, place: (place[5], 0, 0)),
                pl.BlockSpec((tokens, wide), lambda n, place: (0, place[4])),
                pl.BlockSpec((tokens, columns), lambda n, place: (0, n)),
            ]
            + [gain] * len(gain_sums),
            out_specs=pl.BlockSpec((shares, rows, block), lambda n, place: (0, 0, 0)),
            scratch_shapes=[
                pltpu.VMEM((features, tokens), BF),
                pltpu.VMEM((features, columns), F32),
            ],
        ),
        out_shape=jax.ShapeDtypeStruct((shares, rows, block), BF),
        compiler_params=PARAMS,
        cost_estimate=cost(9.5),
        name="weight_parts",
    )(counts, order, mixed, cotangents, *gain_sums)


def sum_kernel(parts_ref, out_ref, gain_q_ref, gain_k_ref):
    shares, rows, block = parts_ref.shape
    own = out_ref.shape[0]
    total = parts_ref[0].astype(F32)
    for share in range(1, shares):
        total = total + parts_ref[share].astype(F32)
    for piece in range(PIECES):
        out_ref[:, piece * block : (piece + 1) * block] = total[piece * own : (piece + 1) * own]
    tail = total[rows - TAIL :, :LANES]
    for number, gain_ref in enumerate((gain_q_ref, gain_k_ref)):
        gain = jnp.sum(tail[3 * number : 3 * number + 3], 0, keepdims=True)
        gain_ref[...] = gain[:, :HD] + gain[:, HD:]


def sum_parts(parts, own):
    block = parts.shape[2]
    gain = jax.ShapeDtypeStruct((1, HD), F32)
    return pl.pallas_call(
        sum_kernel,
        in_specs=[VMEM],
        out_specs=[VMEM] * 3,
        out_shape=[jax.ShapeDtypeStruct((own, PIECES * block), F32), gain, gain],
        compiler_params=SMALL,
        cost_estimate=cost(2.2),
        name="sum_parts",
    )(parts)


def feature_order(inner, planes, cores, shares, heights):
    depths = shares // heights
    wide = inner // planes
    features = wide // cores
    own = features // shares
    order = np.zeros((cores, features, wide), np.float32)
    for core in range(cores):
        for feature in range(features):
            share, row = divmod(feature, own)
            y, z = divmod(share, depths)
            share = z * heights + y
            order[core, feature, own * (cores * share + core) + row] = 1.0
    return jnp.asarray(order, BF)


def local(
    queries,
    keys_proj,
    values_proj,
    gain_query,
    gain_key,
    frame_counts,
    heights,
    widths,
    out_weight,
    cotangent,
):
    seq = ("y", "core")
    group = ("x", "core")
    sums = ("y", "z")
    planes, cores = lax.axis_size("x"), lax.axis_size("core")
    shares = lax.axis_size("z") * lax.axis_size("y")
    inner = out_weight.shape[0]
    rank = lax.axis_index(seq).astype(jnp.int32)
    place = [lax.axis_index("x").astype(jnp.int32), lax.axis_index("core").astype(jnp.int32)]
    counts = jnp.stack([frame_counts[0], heights[0], widths[0], rank, *place])
    gains = gain_query.reshape(1, HD), gain_key.reshape(1, HD)
    query_rows, key_rows, value_rows = queries[0, 0], keys_proj[0, 0], values_proj[0, 0]
    cot_rows = cotangent[0, 0]
    by_cells = (FRAMES, CELLS_HERE, inner)

    def exchange(tensor, axes):
        return lax.all_to_all(tensor, axes, split_axis=0, concat_axis=0, tiled=True)

    def after(tensor, earlier):
        return lax.optimization_barrier((tensor, earlier))[0]

    cotangents = lax.all_gather(cot_rows, group, axis=0, tiled=True)
    normed = norm(query_rows, key_rows, *gains)
    normed_cells = exchange(normed, seq)
    grad_mixed = grad_mixed_of(cot_rows, out_weight)
    outgoing, chances = space_forward(counts, normed, value_rows, grad_mixed)
    arrived = exchange(after(outgoing, normed_cells), seq)
    hats = hats_of(*lax.optimization_barrier((query_rows, key_rows, outgoing))[:2])
    arrived, *hats = lax.optimization_barrier((arrived, *hats))
    mixed_cells = time_forward(counts, normed_cells, arrived)
    mixed = exchange(mixed_cells, seq).reshape(CELLS, inner)
    late_cells, dspatial_cells, late_gains = time_back(counts, normed_cells, arrived)
    first = (cotangents, dspatial_cells)
    gathered = lax.all_gather(after(mixed, first), group, axis=0, tiled=True)
    dspatial = exchange(after(dspatial_cells, mixed), seq).reshape(CELLS, inner)
    late = exchange(after(late_cells, dspatial), seq)
    block_out = project(mixed, out_weight)
    dq, dk, grad_values, gain_sums = space_back(
        late_gains, *gains, hats[:2], normed, value_rows, dspatial, chances
    )
    for flip in range(1, cores):
        pairs = [(i, (i + flip) % cores) for i in range(cores)]
        gain_sums = gain_sums + lax.ppermute(gain_sums, "core", pairs)
    gain_sums = [gain_sums] + [
        lax.ppermute(gain_sums, "x", [(i, (i + step) % planes) for i in range(planes)])
        for step in range(1, planes)
    ]
    grad_queries, grad_keys = norm_back(hats, *gains, dq, dk, late)
    order = feature_order(inner, planes, cores, shares, lax.axis_size("y"))
    parts = weight_parts(counts, order, gathered, cotangents, gain_sums, shares)
    parts = exchange(after(parts, late), sums)
    own = order.shape[1] // shares
    grad_weight, grad_gain_query, grad_gain_key = sum_parts(parts, own)
    return (
        block_out.reshape(cotangent.shape),
        grad_queries.reshape(queries.shape),
        grad_keys.reshape(queries.shape),
        grad_values.reshape(queries.shape),
        grad_weight,
        grad_gain_query.reshape(HD),
        grad_gain_key.reshape(HD),
    )


def solution(mesh):
    planes = 4 if mesh.shape["dp"] == 16 else mesh.shape["dp"]
    fine = Mesh(
        mesh.devices.reshape(planes, mesh.shape["dp"] // planes, -1, 2), ("x", "z", "y", "core")
    )
    tokens = P(("x", "z"), ("y", "core"), None, None)
    clips = P(("x", "z"))
    return jax.shard_map(
        local,
        mesh=fine,
        in_specs=(tokens, tokens, tokens, P(), P(), clips, clips, clips, P(), tokens),
        out_specs=(
            tokens,
            tokens,
            tokens,
            tokens,
            P(("x", "z", "y", "core"), None),
            P(),
            P(),
        ),
        check_vma=False,
    )
```

```python
import jax
import jax.numpy as jnp
import numpy as np
from jax import lax
from jax.experimental import pallas as pl
from jax.experimental.pallas import tpu as pltpu
from jax.sharding import Mesh
from jax.sharding import PartitionSpec as P

BF = jnp.bfloat16
F32 = jnp.float32
HD = 64
PW = 16
CELLS = 256
FRAMES = 8
LANES = 128
WIDE = 384
PAIRS = WIDE // LANES
CELLS_HERE = CELLS // FRAMES
BLOCK = 16
NEG = -1e30
SCALE = HD**-0.5
PARAMS = pltpu.CompilerParams(vmem_limit_bytes=56 * 1024 * 1024)
SMALL = pltpu.CompilerParams(vmem_limit_bytes=16 * 1024 * 1024)


def cost(microseconds):
    return pl.CostEstimate(flops=0, bytes_accessed=int(microseconds * 3.69e6), transcendentals=0)


SMEM = pl.BlockSpec(memory_space=pltpu.SMEM)
VMEM = pl.BlockSpec(memory_space=pltpu.VMEM)


def nn(left, right):
    return jnp.dot(left, right, preferred_element_type=F32)


def nt(left, right):
    return lax.dot_general(left, right, (((1,), (1,)), ((), ())), preferred_element_type=F32)


def tn(left, right):
    return lax.dot_general(left, right, (((0,), (0,)), ((), ())), preferred_element_type=F32)


def low_lanes(shape):
    return lax.broadcasted_iota(jnp.int32, shape, len(shape) - 1) < HD


def stack_heads(pair):
    low = low_lanes((1, LANES)).astype(F32)
    return jnp.concatenate([pair * low.astype(BF), pair * (1.0 - low).astype(BF)], 0)


def pick_heads(stacked):
    half = stacked.shape[0] // 2
    return jnp.where(low_lanes((half, LANES)), stacked[:half], stacked[half:])


def softmax_rows(scores):
    grouped = scores.reshape(2, scores.shape[0] // 2, scores.shape[1])
    expo = jnp.exp(grouped - jnp.max(grouped, 1, keepdims=True))
    return expo * (1.0 / jnp.sum(expo, 1, keepdims=True))


def score_back(chances, dchances):
    grouped = dchances.reshape(chances.shape)
    total = jnp.sum(chances * grouped, 1, keepdims=True)
    return (chances * (grouped - total)).astype(BF).reshape(dchances.shape)


def cell_ok(cells, height, width):
    row = lax.shift_right_logical(cells, 4)
    return (row < height) & ((cells & (PW - 1)) < width)


def head_ones(rows, columns):
    row = lax.broadcasted_iota(jnp.int32, (rows, columns), 0) & (columns - 1)
    column = lax.broadcasted_iota(jnp.int32, (rows, columns), 1)
    same = lax.shift_right_logical(row, 6) == lax.shift_right_logical(column, 6)
    return jnp.where(same, 1.0, 0.0).astype(BF)


def head_mean(tensor, twice):
    high = tensor.astype(BF)
    rest = (tensor - high.astype(F32)).astype(BF)
    return nn(jnp.concatenate([high, rest], 1), twice) * (1.0 / HD)


def hat_of(raw, ones, twice):
    centre = raw.astype(F32) - nn(raw, ones) * (1.0 / HD)
    hats, inverses = [], []
    for left in range(0, raw.shape[1], LANES):
        part = centre[:, left : left + LANES]
        inverse = lax.rsqrt(head_mean(part * part, twice) + 1e-06)
        hats.append(part * inverse)
        inverses.append(inverse)
    return hats, inverses


def both_heads(gain_ref):
    return jnp.concatenate([gain_ref[...], gain_ref[...]], 1)


def pair_slice(number):
    return slice(number * LANES, (number + 1) * LANES)


NORM_WIDE = 512
DUO = 2 * LANES


def norm_kernel(q_ref, k_ref, gain_q_ref, gain_k_ref, out_ref):
    ones, twice = head_ones(DUO, DUO), head_ones(DUO, LANES)
    gains = both_heads(gain_q_ref), both_heads(gain_k_ref)
    for left in range(0, NORM_WIDE, DUO):
        for number, source in enumerate((q_ref, k_ref)):
            hats, _ = hat_of(source[:, left : left + DUO], ones, twice)
            for pair, hat in enumerate(hats):
                normed = (hat * gains[number]).astype(BF)
                if number == 0:
                    normed = normed * jnp.asarray(SCALE, BF)
                at = slice(left + pair * LANES, left + (pair + 1) * LANES)
                out_ref[:, number, :, at] = normed.reshape(FRAMES, CELLS_HERE, LANES)


def norm(queries, keys, gain_query, gain_key):
    inner = queries.shape[1]
    tokens = pl.BlockSpec((CELLS, NORM_WIDE), lambda n: (0, n))
    gain = pl.BlockSpec((1, HD), lambda n: (0, 0))
    return pl.pallas_call(
        norm_kernel,
        grid=(inner // NORM_WIDE,),
        in_specs=[tokens, tokens, gain, gain],
        out_specs=pl.BlockSpec((FRAMES, 2, CELLS_HERE, NORM_WIDE), lambda n: (0, 0, 0, n)),
        out_shape=jax.ShapeDtypeStruct((FRAMES, 2, CELLS_HERE, inner), BF),
        compiler_params=PARAMS,
        cost_estimate=cost(5),
        name="norm",
    )(queries, keys, gain_query, gain_key)


def hats_kernel(q_ref, k_ref, *out_refs):
    ones, twice = head_ones(DUO, DUO), head_ones(DUO, LANES)
    for left in range(0, NORM_WIDE, DUO):
        for number, source in enumerate((q_ref, k_ref)):
            hats, inverses = hat_of(source[:, left : left + DUO], ones, twice)
            at = slice(left, left + DUO)
            out_refs[number][:, at] = jnp.concatenate(hats, 1)
            out_refs[2 + number][:, at] = jnp.concatenate(inverses, 1)


def hats_of(queries, keys):
    inner = queries.shape[1]
    tokens = pl.BlockSpec((CELLS, NORM_WIDE), lambda n: (0, n))
    return pl.pallas_call(
        hats_kernel,
        grid=(inner // NORM_WIDE,),
        in_specs=[tokens, tokens],
        out_specs=[tokens] * 4,
        out_shape=[jax.ShapeDtypeStruct((CELLS, inner), F32)] * 4,
        compiler_params=PARAMS,
        cost_estimate=cost(5.6),
        name="hats",
    )(queries, keys)


def space_kernel(counts_ref, qk_ref, v_ref, gm_ref, out_ref, chances_ref):
    height, width = counts_ref[1], counts_ref[2]
    frame_on = jnp.where(counts_ref[3] < counts_ref[0], 1.0, 0.0)
    key_cell = lax.broadcasted_iota(jnp.int32, (2 * CELLS, CELLS), 0) & (CELLS - 1)
    bias = jnp.where(cell_ok(key_cell, height, width), 0.0, NEG)
    cell = lax.broadcasted_iota(jnp.int32, (CELLS, LANES), 0)
    usable = cell_ok(cell, height, width).astype(F32) * frame_on
    scores = []
    for pair in range(PAIRS):
        query = qk_ref[:, 0, :, pair_slice(pair)].reshape(CELLS, LANES)
        key = qk_ref[:, 1, :, pair_slice(pair)].reshape(CELLS, LANES)
        scores.append(nt(stack_heads(key), query) + bias)
    weights = []
    for pair in range(PAIRS):
        probs = softmax_rows(scores[pair]).reshape(scores[pair].shape)
        chances_ref[pair] = probs
        weights.append(probs.astype(BF))
    for pair in range(PAIRS):
        mixed = tn(weights[pair], stack_heads(v_ref[:, pair_slice(pair)]))
        mixed = (mixed * usable).astype(BF)
        out_ref[:, 0, :, pair_slice(pair)] = mixed.reshape(FRAMES, CELLS_HERE, LANES)
    out_ref[:, 1] = gm_ref[...].reshape(FRAMES, CELLS_HERE, WIDE)


def space_forward(counts, normed, values, grad_mixed):
    inner = values.shape[1]
    tokens = pl.BlockSpec((CELLS, WIDE), lambda n: (0, n))
    return pl.pallas_call(
        space_kernel,
        grid=(inner // WIDE,),
        in_specs=[
            SMEM,
            pl.BlockSpec((FRAMES, 2, CELLS_HERE, WIDE), lambda n: (0, 0, 0, n)),
            tokens,
            tokens,
        ],
        out_specs=[
            pl.BlockSpec((FRAMES, 2, CELLS_HERE, WIDE), lambda n: (0, 0, 0, n)),
            pl.BlockSpec((PAIRS, 2 * CELLS, CELLS), lambda n: (n, 0, 0)),
        ],
        out_shape=[
            jax.ShapeDtypeStruct((FRAMES, 2, CELLS_HERE, inner), BF),
            jax.ShapeDtypeStruct((inner // LANES, 2 * CELLS, CELLS), F32),
        ],
        compiler_params=PARAMS,
        cost_estimate=cost(7),
        name="space_forward",
    )(counts, normed, values, grad_mixed)


def gain_part(grad, normed):
    return jnp.sum(grad * normed.astype(F32), 0, keepdims=True)


def add_gains(sums_ref, of_query, of_key, begin=None):
    @pl.when(pl.program_id(0) == 0)
    def _():
        sums_ref[...] = jnp.zeros_like(sums_ref) if begin is None else begin()

    sums_ref[0:1] += of_query
    sums_ref[1:2] += of_key


def space_back_kernel(
    late_ref,
    gain_q_ref,
    gain_k_ref,
    hat_q_ref,
    hat_k_ref,
    qk_ref,
    v_ref,
    up_ref,
    chances_ref,
    dq_ref,
    dk_ref,
    dv_ref,
    sums_ref,
):
    def late_gains():
        scale = [both_heads(gain_q_ref) * SCALE, both_heads(gain_k_ref)]
        return late_ref[...] / jnp.concatenate(scale + [jnp.ones((6, LANES), F32)], 0)

    of_query = jnp.zeros((1, LANES), F32)
    of_key = jnp.zeros((1, LANES), F32)
    slices = [pair_slice(pair) for pair in range(PAIRS)]
    queries = [qk_ref[:, 0, :, at].reshape(CELLS, LANES) for at in slices]
    keys = [stack_heads(qk_ref[:, 1, :, at].reshape(CELLS, LANES)) for at in slices]
    dchances = [nt(stack_heads(v_ref[:, at]), up_ref[:, at]) for at in slices]
    dscores = []
    for pair, at in enumerate(slices):
        probs = chances_ref[pair]
        dv_ref[:, at] = pick_heads(nn(probs.astype(BF), up_ref[:, at])).astype(BF)
        dscores.append(score_back(probs.reshape(2, CELLS, CELLS), dchances[pair]))
    for pair, at in enumerate(slices):
        dk = pick_heads(nn(dscores[pair], queries[pair]))
        dq = tn(dscores[pair], keys[pair]) * SCALE
        dk_ref[:, at] = dk
        dq_ref[:, at] = dq
        of_query += gain_part(dq, hat_q_ref[:, at])
        of_key += gain_part(dk, hat_k_ref[:, at])
    add_gains(sums_ref, of_query, of_key, late_gains)


def space_back(late_sums, gain_query, gain_key, hats, normed, values, upstream, chances):
    inner = values.shape[1]
    tokens = pl.BlockSpec((CELLS, WIDE), lambda n: (0, n))
    wide = jax.ShapeDtypeStruct((CELLS, inner), F32)
    return pl.pallas_call(
        space_back_kernel,
        grid=(inner // WIDE,),
        in_specs=[
            pl.BlockSpec((8, LANES), lambda n: (0, 0)),
            pl.BlockSpec((1, HD), lambda n: (0, 0)),
            pl.BlockSpec((1, HD), lambda n: (0, 0)),
            tokens,
            tokens,
            pl.BlockSpec((FRAMES, 2, CELLS_HERE, WIDE), lambda n: (0, 0, 0, n)),
            tokens,
            tokens,
            pl.BlockSpec((PAIRS, 2 * CELLS, CELLS), lambda n: (n, 0, 0)),
        ],
        out_specs=[tokens, tokens, tokens, pl.BlockSpec((8, LANES), lambda n: (0, 0))],
        out_shape=[
            wide,
            wide,
            jax.ShapeDtypeStruct((CELLS, inner), BF),
            jax.ShapeDtypeStruct((8, LANES), F32),
        ],
        compiler_params=PARAMS,
        cost_estimate=cost(9),
        name="space_back",
    )(late_sums, gain_query, gain_key, *hats, normed, values, upstream, chances)


def time_bias(frame_total):
    key = lax.broadcasted_iota(jnp.int32, (2 * LANES, LANES), 0) & (LANES - 1)
    query = lax.broadcasted_iota(jnp.int32, (2 * LANES, LANES), 1)
    same = (key & (BLOCK - 1)) == (query & (BLOCK - 1))
    return jnp.where(same & (lax.shift_right_logical(key, 4) < frame_total), 0.0, NEG)


def time_usable(counts_ref, block):
    row = lax.broadcasted_iota(jnp.int32, (LANES, LANES), 0)
    cell = counts_ref[3] * CELLS_HERE + block * BLOCK + (row & (BLOCK - 1))
    on = cell_ok(cell, counts_ref[1], counts_ref[2])
    return (on & (lax.shift_right_logical(row, 4) < counts_ref[0])).astype(F32)


def time_blocks():
    for block in range(CELLS_HERE // BLOCK):
        for pair in range(PAIRS):
            yield block, slice(block * BLOCK, (block + 1) * BLOCK), pair_slice(pair)


def time_kernel(counts_ref, qk_ref, sg_ref, out_ref):
    bias = time_bias(counts_ref[0])
    usable = [time_usable(counts_ref, block) for block in range(CELLS_HERE // BLOCK)]
    scores = []
    for block, rows, at in time_blocks():
        query = qk_ref[:, 0, rows, at].reshape(LANES, LANES)
        keys = stack_heads(qk_ref[:, 1, rows, at].reshape(LANES, LANES))
        scores.append(nt(keys, query) + bias)
    weights = [softmax_rows(part).astype(BF).reshape(part.shape) for part in scores]
    for number, (block, rows, at) in enumerate(time_blocks()):
        values = stack_heads(sg_ref[:, 0, rows, at].reshape(LANES, LANES))
        mixed = tn(weights[number], values) * usable[block]
        out_ref[:, rows, at] = mixed.astype(BF).reshape(FRAMES, BLOCK, LANES)


def time_back_kernel(counts_ref, qk_ref, sg_ref, dqk_ref, ds_ref, sums_ref):
    bias = time_bias(counts_ref[0])
    of_query = jnp.zeros((1, LANES), F32)
    of_key = jnp.zeros((1, LANES), F32)
    usable = [time_usable(counts_ref, block) for block in range(CELLS_HERE // BLOCK)]
    blocks = list(time_blocks())

    def load(ref, number, rows, at):
        return ref[:, number, rows, at].reshape(LANES, LANES)

    def shaped(tensor):
        return tensor.astype(BF).reshape(FRAMES, BLOCK, LANES)

    queries = [load(qk_ref, 0, rows, at) for _, rows, at in blocks]
    singles = [load(qk_ref, 1, rows, at) for _, rows, at in blocks]
    keys = [stack_heads(key) for key in singles]
    upstreams = [
        (load(sg_ref, 1, rows, at).astype(F32) * usable[block]).astype(BF)
        for block, rows, at in blocks
    ]
    scores = [nt(key, query) + bias for key, query in zip(keys, queries)]
    dchances = [
        nt(stack_heads(load(sg_ref, 0, rows, at)), upstream)
        for (_, rows, at), upstream in zip(blocks, upstreams)
    ]
    chances = [softmax_rows(part) for part in scores]
    dscores = [score_back(probs, part) for probs, part in zip(chances, dchances)]
    for number, (_, rows, at) in enumerate(blocks):
        weights = chances[number].astype(BF).reshape(2 * LANES, LANES)
        ds_ref[:, rows, at] = shaped(pick_heads(nn(weights, upstreams[number])))
        dq = tn(dscores[number], keys[number]) * SCALE
        dk = pick_heads(nn(dscores[number], queries[number]))
        dqk_ref[:, 0, rows, at] = shaped(dq)
        dqk_ref[:, 1, rows, at] = shaped(dk)
        of_query += gain_part(dq, queries[number])
        of_key += gain_part(dk, singles[number])
    add_gains(sums_ref, of_query, of_key)


def time_specs(inner):
    double = pl.BlockSpec((FRAMES, 2, CELLS_HERE, WIDE), lambda n: (0, 0, 0, n))
    single = pl.BlockSpec((FRAMES, CELLS_HERE, WIDE), lambda n: (0, 0, n))
    return (
        double,
        single,
        jax.ShapeDtypeStruct((FRAMES, 2, CELLS_HERE, inner), BF),
        jax.ShapeDtypeStruct((FRAMES, CELLS_HERE, inner), BF),
    )


def time_forward(counts, normed, arrived):
    inner = arrived.shape[3]
    double, single, _, single_shape = time_specs(inner)
    return pl.pallas_call(
        time_kernel,
        grid=(inner // WIDE,),
        in_specs=[SMEM, double, double],
        out_specs=single,
        out_shape=single_shape,
        compiler_params=SMALL,
        cost_estimate=cost(5),
        name="time_forward",
    )(counts, normed, arrived)


def time_back(counts, normed, arrived):
    inner = arrived.shape[3]
    double, single, double_shape, single_shape = time_specs(inner)
    return pl.pallas_call(
        time_back_kernel,
        grid=(inner // WIDE,),
        in_specs=[SMEM, double, double],
        out_specs=[double, single, pl.BlockSpec((8, LANES), lambda n: (0, 0))],
        out_shape=[double_shape, single_shape, jax.ShapeDtypeStruct((8, LANES), F32)],
        compiler_params=SMALL,
        cost_estimate=cost(6.5),
        name="time_back",
    )(counts, normed, arrived)


def norm_back_kernel(
    hat_q_ref,
    hat_k_ref,
    inverse_q_ref,
    inverse_k_ref,
    gain_q_ref,
    gain_k_ref,
    dq_ref,
    dk_ref,
    late_ref,
    gq_ref,
    gk_ref,
):
    twice = head_ones(DUO, LANES)
    for left in range(0, NORM_WIDE, LANES):
        at = slice(left, left + LANES)
        for number, (hat_ref, inverse_ref, gain_ref, early, target) in enumerate(
            (
                (hat_q_ref, inverse_q_ref, gain_q_ref, dq_ref, gq_ref),
                (hat_k_ref, inverse_k_ref, gain_k_ref, dk_ref, gk_ref),
            )
        ):
            hat = hat_ref[:, at]
            late = late_ref[:, number, :, at].reshape(CELLS, LANES)
            scaled = (early[:, at] + late.astype(F32)) * both_heads(gain_ref)
            mean = head_mean(scaled, twice)
            dinput = scaled - mean - hat * head_mean(scaled * hat, twice)
            target[:, at] = (inverse_ref[:, at] * dinput).astype(BF)


def norm_back(hats, gain_query, gain_key, dq, dk, late):
    inner = dq.shape[1]
    tokens = pl.BlockSpec((CELLS, NORM_WIDE), lambda n: (0, n))
    gain = pl.BlockSpec((1, HD), lambda n: (0, 0))
    grads = jax.ShapeDtypeStruct((CELLS, inner), BF)
    return pl.pallas_call(
        norm_back_kernel,
        grid=(inner // NORM_WIDE,),
        in_specs=[
            tokens,
            tokens,
            tokens,
            tokens,
            gain,
            gain,
            tokens,
            tokens,
            pl.BlockSpec((FRAMES, 2, CELLS_HERE, NORM_WIDE), lambda n: (0, 0, 0, n)),
        ],
        out_specs=[tokens, tokens],
        out_shape=[grads, grads],
        compiler_params=PARAMS,
        cost_estimate=cost(7),
        name="norm_back",
    )(*hats, gain_query, gain_key, dq, dk, late)


def grad_mixed_kernel(cot_ref, weight_ref, out_ref):
    out_ref[...] = nt(cot_ref[...], weight_ref[...]).astype(BF)


def grad_mixed_of(cotangent, weight):
    inner, width = weight.shape
    return pl.pallas_call(
        grad_mixed_kernel,
        grid=(inner // WIDE,),
        in_specs=[
            pl.BlockSpec((CELLS, width), lambda n: (0, 0)),
            pl.BlockSpec((WIDE, width), lambda n: (n, 0)),
        ],
        out_specs=pl.BlockSpec((CELLS, WIDE), lambda n: (0, n)),
        out_shape=jax.ShapeDtypeStruct((CELLS, inner), BF),
        compiler_params=PARAMS,
        cost_estimate=cost(8.7),
        name="grad_mixed",
    )(cotangent, weight)


def project_kernel(mixed_ref, weight_ref, out_ref):
    out_ref[...] = nn(mixed_ref[...], weight_ref[...]).astype(BF)


def project(mixed, weight):
    inner, width = weight.shape
    block = width // 4
    return pl.pallas_call(
        project_kernel,
        grid=(4,),
        in_specs=[
            pl.BlockSpec((CELLS, inner), lambda n: (0, 0)),
            pl.BlockSpec((inner, block), lambda n: (0, n)),
        ],
        out_specs=pl.BlockSpec((CELLS, block), lambda n: (0, n)),
        out_shape=jax.ShapeDtypeStruct((CELLS, width), BF),
        compiler_params=PARAMS,
        cost_estimate=cost(7),
        name="project",
    )(mixed, weight)


PIECES = 24
STEPS = 3
TAIL = 8


def gain_rows(gain_refs, block):
    total = gain_refs[0][...]
    for gain_ref in gain_refs[1:]:
        total = total + gain_ref[...]
    terms = []
    for row in range(2):
        rest = total[row : row + 1]
        for _ in range(3):
            terms.append(rest.astype(BF).astype(F32))
            rest = rest - terms[-1]
    rows = jnp.concatenate(terms + [jnp.zeros((TAIL - 6, LANES), F32)], 0)
    if block > LANES:
        rows = jnp.concatenate([rows, jnp.zeros((TAIL, block - LANES), F32)], 1)
    return rows.astype(BF)


def weight_kernel(place_ref, order_ref, mixed_ref, cot_ref, *refs):
    *gain_refs, out_ref, turned, product = refs
    shares, rows, block = out_ref.shape
    own = product.shape[0] // shares

    @pl.when(pl.program_id(0) == 0)
    def _():
        turned[...] = nt(order_ref[0], mixed_ref[...]).astype(BF)
        tail = gain_rows(gain_refs, block)
        for share in range(shares):
            out_ref[share, rows - TAIL :] = tail

    product[...] = nn(turned[...], cot_ref[...])
    for step in range(STEPS):

        @pl.when(pl.program_id(0) == step)
        def _():
            for share in range(shares):
                for half in range(PIECES // STEPS):
                    top = (step * (PIECES // STEPS) + half) * own
                    out_ref[share, top : top + own] = product[
                        share * own : (share + 1) * own, half * block : (half + 1) * block
                    ].astype(BF)


def weight_parts(counts, order, mixed, cotangents, gain_sums, shares):
    tokens, width = cotangents.shape
    _, features, wide = order.shape
    block = width // PIECES
    columns = width // STEPS
    rows = -(-(PIECES * (features // shares) + TAIL) // 16) * 16
    gain = pl.BlockSpec((8, LANES), lambda n, place: (0, 0))
    return pl.pallas_call(
        weight_kernel,
        grid_spec=pltpu.PrefetchScalarGridSpec(
            num_scalar_prefetch=1,
            grid=(STEPS,),
            in_specs=[
                pl.BlockSpec((1, features, wide), lambda n, place: (place[5], 0, 0)),
                pl.BlockSpec((tokens, wide), lambda n, place: (0, place[4])),
                pl.BlockSpec((tokens, columns), lambda n, place: (0, n)),
            ]
            + [gain] * len(gain_sums),
            out_specs=pl.BlockSpec((shares, rows, block), lambda n, place: (0, 0, 0)),
            scratch_shapes=[
                pltpu.VMEM((features, tokens), BF),
                pltpu.VMEM((features, columns), F32),
            ],
        ),
        out_shape=jax.ShapeDtypeStruct((shares, rows, block), BF),
        compiler_params=PARAMS,
        cost_estimate=cost(9.5),
        name="weight_parts",
    )(counts, order, mixed, cotangents, *gain_sums)


def sum_kernel(parts_ref, out_ref, gain_q_ref, gain_k_ref):
    shares, rows, block = parts_ref.shape
    own = out_ref.shape[0]
    total = parts_ref[0].astype(F32)
    for share in range(1, shares):
        total = total + parts_ref[share].astype(F32)
    for piece in range(PIECES):
        out_ref[:, piece * block : (piece + 1) * block] = total[piece * own : (piece + 1) * own]
    tail = total[rows - TAIL :, :LANES]
    for number, gain_ref in enumerate((gain_q_ref, gain_k_ref)):
        gain = jnp.sum(tail[3 * number : 3 * number + 3], 0, keepdims=True)
        gain_ref[...] = gain[:, :HD] + gain[:, HD:]


def sum_parts(parts, own):
    block = parts.shape[2]
    gain = jax.ShapeDtypeStruct((1, HD), F32)
    return pl.pallas_call(
        sum_kernel,
        in_specs=[VMEM],
        out_specs=[VMEM] * 3,
        out_shape=[jax.ShapeDtypeStruct((own, PIECES * block), F32), gain, gain],
        compiler_params=SMALL,
        cost_estimate=cost(2.2),
        name="sum_parts",
    )(parts)


def feature_order(inner, planes, cores, shares, heights):
    depths = shares // heights
    wide = inner // planes
    features = wide // cores
    own = features // shares
    order = np.zeros((cores, features, wide), np.float32)
    for core in range(cores):
        for feature in range(features):
            share, row = divmod(feature, own)
            y, z = divmod(share, depths)
            share = z * heights + y
            order[core, feature, own * (cores * share + core) + row] = 1.0
    return jnp.asarray(order, BF)


def local(
    queries,
    keys_proj,
    values_proj,
    gain_query,
    gain_key,
    frame_counts,
    heights,
    widths,
    out_weight,
    cotangent,
):
    seq = ("y", "core")
    group = ("x", "core")
    sums = ("y", "z")
    planes, cores = lax.axis_size("x"), lax.axis_size("core")
    shares = lax.axis_size("z") * lax.axis_size("y")
    inner = out_weight.shape[0]
    rank = lax.axis_index(seq).astype(jnp.int32)
    place = [lax.axis_index("x").astype(jnp.int32), lax.axis_index("core").astype(jnp.int32)]
    counts = jnp.stack([frame_counts[0], heights[0], widths[0], rank, *place])
    gains = gain_query.reshape(1, HD), gain_key.reshape(1, HD)
    query_rows, key_rows, value_rows = queries[0, 0], keys_proj[0, 0], values_proj[0, 0]
    cot_rows = cotangent[0, 0]
    by_cells = (FRAMES, CELLS_HERE, inner)

    def exchange(tensor, axes):
        return lax.all_to_all(tensor, axes, split_axis=0, concat_axis=0, tiled=True)

    def after(tensor, earlier):
        return lax.optimization_barrier((tensor, earlier))[0]

    cotangents = lax.all_gather(cot_rows, group, axis=0, tiled=True)
    normed = norm(query_rows, key_rows, *gains)
    normed_cells = exchange(normed, seq)
    grad_mixed = grad_mixed_of(cot_rows, out_weight)
    outgoing, chances = space_forward(counts, normed, value_rows, grad_mixed)
    arrived = exchange(after(outgoing, normed_cells), seq)
    hats = hats_of(*lax.optimization_barrier((query_rows, key_rows, outgoing))[:2])
    arrived, *hats = lax.optimization_barrier((arrived, *hats))
    mixed_cells = time_forward(counts, normed_cells, arrived)
    mixed = exchange(mixed_cells, seq).reshape(CELLS, inner)
    late_cells, dspatial_cells, late_gains = time_back(counts, normed_cells, arrived)
    first = (cotangents, dspatial_cells)
    gathered = lax.all_gather(after(mixed, first), group, axis=0, tiled=True)
    dspatial = exchange(after(dspatial_cells, mixed), seq).reshape(CELLS, inner)
    late = exchange(after(late_cells, dspatial), seq)
    block_out = project(mixed, out_weight)
    dq, dk, grad_values, gain_sums = space_back(
        late_gains, *gains, hats[:2], normed, value_rows, dspatial, chances
    )
    for flip in range(1, cores):
        pairs = [(i, (i + flip) % cores) for i in range(cores)]
        gain_sums = gain_sums + lax.ppermute(gain_sums, "core", pairs)
    gain_sums = [gain_sums] + [
        lax.ppermute(gain_sums, "x", [(i, (i + step) % planes) for i in range(planes)])
        for step in range(1, planes)
    ]
    grad_queries, grad_keys = norm_back(hats, *gains, dq, dk, late)
    order = feature_order(inner, planes, cores, shares, lax.axis_size("y"))
    parts = weight_parts(counts, order, gathered, cotangents, gain_sums, shares)
    parts = exchange(after(parts, late), sums)
    own = order.shape[1] // shares
    grad_weight, grad_gain_query, grad_gain_key = sum_parts(parts, own)
    return (
        block_out.reshape(cotangent.shape),
        grad_queries.reshape(queries.shape),
        grad_keys.reshape(queries.shape),
        grad_values.reshape(queries.shape),
        grad_weight,
        grad_gain_query.reshape(HD),
        grad_gain_key.reshape(HD),
    )


def solution(mesh):
    planes = 4 if mesh.shape["dp"] == 16 else mesh.shape["dp"]
    fine = Mesh(
        mesh.devices.reshape(planes, mesh.shape["dp"] // planes, -1, 2), ("x", "z", "y", "core")
    )
    tokens = P(("x", "z"), ("y", "core"), None, None)
    clips = P(("x", "z"))
    return jax.shard_map(
        local,
        mesh=fine,
        in_specs=(tokens, tokens, tokens, P(), P(), clips, clips, clips, P(), tokens),
        out_specs=(
            tokens,
            tokens,
            tokens,
            tokens,
            P(("x", "z", "y", "core"), None),
            P(),
            P(),
        ),
        check_vma=False,
    )
```
